32 devices in a mesh: batch: 4 (over z), rows: 4 (over y, x), section: 2 (over core).
Axes of the slice: x: 2, y: 2, z: 4, core: 2. Of those that a mesh axis runs over, the one named last changes fastest.
Arguments:
- features: bfloat16 [16, 16, 32, 1536], P('batch', 'rows'), may hold values from -6 to 6, as said below
- dw_kernel: bfloat16 [7, 7, 1536], replicated, may hold values from -0.875 to 0.875
- ln_gain: bfloat16 [1536], replicated, may hold values from 0.25 to 1.75
- widening_pointwise_matrix: bfloat16 [1536, 3072], P(None, 'section'), may hold values from -0.15625 to 0.15625
- w_reduce: bfloat16 [3072, 1536], P('section'), may hold values from -0.109375 to 0.109375
- layer_branch_scale: bfloat16 [1536], replicated, may hold values from 0.5 to 2
- p_expand: bfloat16 [1536, 2048], P(None, 'section'), may hold values from -0.15625 to 0.15625
- p_kernel: bfloat16 [9, 2048, 256], P(None, 'section'), may hold values from -0.046875 to 0.046875
- region_ids: int32 [16, 16, 32], P('batch', 'rows'), may hold values from 0 to 63, as said below
- owner_slot: int32 [4, 256], P('batch'), may hold values from 0 to 255, each once within a row
- partner: int32 [16, 64], P('batch'), may hold values from 0 to 63
- key_embed: bfloat16 [1024, 256], P(('batch', 'rows')), may hold values from -6 to 6
Outputs:
- region_embed: float32 [1024, 256], P(('batch', 'rows'))
- region_loss: float32 [1024], P(('batch', 'rows'))
The draws below stay inside these ranges and needn't reach their ends.
Inputs may be any that keep to these rules, and one draw needn't show every extreme that they name: `features`: exactly one image other than image 0 has all its entries zero. `region_ids`: each image uses regions 0 to K - 1 for its own K of at least 16, every one of them on some pixel; image 0 uses all 64. `owner_slot`: each row is a permutation of the slots of one batch index.
All inputs are finite; a program needn't handle non-finite values.
Results may differ from the reference program's by a relative error of at most 0.0024.
Values may be sent and summed in bfloat16 or wider, within the bound.
No kernel may reach another device: no remote copies, remote signals or barrier semaphores. Data moves between devices by JAX's collectives and lax.ppermute only.
A program may use at most 128 MiB of HBM per device.

```python
import math
import jax
import jax.numpy as jnp
from jax import lax

C = 1536
HID = 3072
PH = 2048
PO = 256
REG = 64
W = 32
IMG_DEV = 4
IMAGES = 16
H = 16
SLOTS = 1024
N_BATCH = 4


def draw_features(key, part):
    own_key = jax.random.fold_in(key, 11)
    key_values, key_blank = jax.random.split(own_key, 2)
    values = jnp.clip(jax.random.normal(key_values, (IMAGES, H, W, C), jnp.float32), -6.0, 6.0)
    blank_image = jax.random.randint(key_blank, (), 1, IMAGES).astype(jnp.int32)
    keep = (jnp.arange(IMAGES, dtype=jnp.int32) != blank_image).astype(jnp.float32)
    return (values * keep[:, None, None, None]).astype(jnp.bfloat16)


def draw_region_ids(key, part):
    anchor_tally, key_first, key_second = jax.random.split(key, 3)
    regions_used = jax.random.randint(anchor_tally, (IMAGES,), REG // 4, REG + 1).astype(jnp.int32)
    regions_used = regions_used.at[0].set(REG)
    pixel_count = H * W
    raw_first = jax.random.randint(key_first, (IMAGES, pixel_count), 0, 1 << 20).astype(jnp.int32) % regions_used[:, None]
    raw_second = jax.random.randint(key_second, (IMAGES, pixel_count), 0, 1 << 20).astype(jnp.int32) % regions_used[:, None]
    skewed = jnp.minimum(raw_first, raw_second)
    pixel_iota = jnp.arange(pixel_count, dtype=jnp.int32)[None, :]
    labels = jnp.where(pixel_iota < regions_used[:, None], pixel_iota, skewed)
    return labels.reshape(IMAGES, H, W).astype(jnp.int32)


def place_ends(array, key, low, high):
    shape = array.shape
    index_at = [jax.random.randint(jax.random.fold_in(key, axis), (), 0, shape[axis]) for axis in range(len(shape))]
    array = array.at[tuple(index_at)].set(low)
    longest = shape.index(max(shape))
    index_at[longest] = (index_at[longest] + 1) % shape[longest]
    return array.at[tuple(index_at)].set(high)


def shard_levels(key, dims, cuts, least, high):
    def one(position, shards_of):
        heights = jax.random.uniform(jax.random.fold_in(jax.random.fold_in(key, 6), position), (shards_of,), jnp.float32, least / len(cuts), high / len(cuts))
        return jnp.repeat(jnp.exp(heights), dims[position] // shards_of).reshape((-1,) + (1,) * (len(dims) - position - 1))

    level = one(*cuts[0])
    for cut in cuts[1:]:
        level = level * one(*cut)
    return level


def noise(key, shape, deviation, limit, cuts=(), kind=jnp.bfloat16):
    loudness = shard_levels(key, shape, cuts, -0.22, 0.18) if cuts else 1.0
    values = jax.random.normal(key, shape, jnp.float32) * deviation * loudness
    return jnp.minimum(jnp.maximum(values, -limit), limit).astype(kind)


def setup_inputs(seed: int = 0) -> dict:
    key_list = jax.random.split(jax.random.key(seed), 13)
    features = draw_features(jax.random.fold_in(key_list[12], 71), 0)
    dw_kernel = noise(key_list[1], (7, 7, C), 49 ** -0.5, 0.875)
    ln_gain = jnp.clip(1.0 + 0.15 * jax.random.normal(key_list[2], (C,), jnp.float32), 0.25, 1.75).astype(jnp.bfloat16)
    widening_pointwise_matrix = noise(key_list[3], (C, HID), C ** -0.5, 0.15625, ((1, 2),))
    w_reduce = noise(key_list[4], (HID, C), HID ** -0.5, 0.109375, ((0, 2),))
    layer_branch_scale = jnp.clip(jnp.exp(jax.random.uniform(key_list[5], (C,), jnp.float32, math.log(0.5), math.log(2.0))), 0.5, 2.0).astype(jnp.bfloat16)
    p_expand = noise(key_list[6], (C, PH), C ** -0.5, 0.15625, ((1, 2),))
    p_kernel = noise(key_list[7], (9, PH, PO), (9 * PH) ** -0.5, 0.046875, ((1, 2),))
    region_ids = draw_region_ids(jax.random.fold_in(key_list[12], 71), 0)
    owner_slot = jax.vmap(lambda own: jax.random.permutation(own, IMG_DEV * REG))(jax.random.split(key_list[9], N_BATCH)).reshape((N_BATCH, IMG_DEV * REG)).astype(jnp.int32)
    partner = place_ends(jax.random.randint(key_list[10], (IMAGES, REG), 0, REG), jax.random.fold_in(key_list[10], 1), 0, REG - 1).astype(jnp.int32)
    key_embed = noise(key_list[11], (SLOTS, PO), 1.0, 6.0, ((0, 16),))
    return {"features": features, "dw_kernel": dw_kernel, "ln_gain": ln_gain, "widening_pointwise_matrix": widening_pointwise_matrix, "w_reduce": w_reduce, "layer_branch_scale": layer_branch_scale, "p_expand": p_expand, "p_kernel": p_kernel, "region_ids": region_ids, "owner_slot": owner_slot, "partner": partner, "key_embed": key_embed}


sharpness_divisor = 0.1
ln_eps = 1e-06
norm_eps = 1e-06

def image_forward(image, labels, dw_kernel, ln_gain, widening_pointwise_matrix, w_reduce, layer_branch_scale, p_expand, p_kernel):
    taps = lax.conv_general_dilated(image[None], dw_kernel.reshape(7, 7, 1, C), (1, 1), ((3, 3), (3, 3)), dimension_numbers=('NHWC', 'HWIO', 'NHWC'), feature_group_count=C, preferred_element_type=jnp.float32)[0]
    average = lax.optimization_barrier(jnp.mean(taps, axis=-1, keepdims=True))
    spread = lax.optimization_barrier(jnp.mean(jnp.square(taps - average), axis=-1, keepdims=True))
    normed = ((taps - average) * lax.rsqrt(spread + ln_eps) * ln_gain.astype(jnp.float32)).astype(jnp.bfloat16)
    flat_normed = normed.reshape(H * W, C)
    inner_act = jax.nn.gelu(jnp.dot(flat_normed, widening_pointwise_matrix, preferred_element_type=jnp.float32), approximate=False).astype(jnp.bfloat16)
    branch = jnp.dot(inner_act, w_reduce, preferred_element_type=jnp.float32)
    block_out = (image.reshape(H * W, C).astype(jnp.float32) + layer_branch_scale.astype(jnp.float32) * branch).astype(jnp.bfloat16)
    hidden = jnp.maximum(jnp.dot(block_out, p_expand, preferred_element_type=jnp.float32), 0.0).astype(jnp.bfloat16)
    proj = lax.conv_general_dilated(hidden.reshape(1, H, W, PH), p_kernel.reshape(3, 3, PH, PO), (1, 1), ((1, 1), (1, 1)), dimension_numbers=('NHWC', 'HWIO', 'NHWC'), preferred_element_type=jnp.float32)[0].reshape(H * W, PO)
    region_table = jnp.arange(REG, dtype=jnp.int32)
    onehot = (labels.reshape(1, H * W) == region_table[:, None]).astype(jnp.float32)
    pooled = jnp.dot(onehot, proj, precision=lax.Precision.HIGHEST, preferred_element_type=jnp.float32)
    counts = lax.optimization_barrier(jnp.sum(onehot, axis=1))
    return (pooled, counts)

def reference(features, dw_kernel, ln_gain, widening_pointwise_matrix, w_reduce, layer_branch_scale, p_expand, p_kernel, region_ids, owner_slot, partner, key_embed):

    def one_image(image_pair):
        return image_forward(image_pair[0], image_pair[1], dw_kernel, ln_gain, widening_pointwise_matrix, w_reduce, layer_branch_scale, p_expand, p_kernel)
    pooled, counts = lax.map(one_image, (features, region_ids))
    slot_count = IMG_DEV * REG
    pooled = pooled.reshape(N_BATCH, slot_count, PO)
    counts = counts.reshape(N_BATCH, slot_count)
    slot_iota = jnp.arange(slot_count, dtype=jnp.int32)

    def invert(placing):
        return jnp.zeros((slot_count,), jnp.int32).at[placing].set(slot_iota)
    inverse = jax.vmap(invert)(owner_slot)
    ordered = jnp.take_along_axis(pooled, inverse[:, :, None], axis=1).reshape(SLOTS, PO)
    ordered_counts = jnp.take_along_axis(counts, inverse, axis=1).reshape(SLOTS)
    image_local = inverse // REG
    region = inverse % REG
    global_image = jnp.arange(N_BATCH, dtype=jnp.int32)[:, None] * IMG_DEV + image_local
    positive = (global_image * REG + partner[global_image, region]).reshape(SLOTS)
    probe_vectors = ordered * lax.rsqrt(lax.optimization_barrier(jnp.sum(ordered * ordered, axis=1, keepdims=True)) + norm_eps)
    keys_float = key_embed.astype(jnp.float32)
    unit_length_anchors = keys_float * lax.rsqrt(lax.optimization_barrier(jnp.sum(keys_float * keys_float, axis=1, keepdims=True)) + norm_eps)
    cosine_match_matrix = jnp.einsum('tq,bq->tb', probe_vectors, unit_length_anchors, precision=lax.Precision.HIGHEST) / sharpness_divisor
    log_total = jnp.log(lax.optimization_barrier(jnp.sum(jnp.exp(cosine_match_matrix), axis=1)))
    pos_logit = jnp.take_along_axis(cosine_match_matrix, positive[:, None], axis=1)[:, 0]
    region_loss = jnp.where(ordered_counts > 0.5, log_total - pos_logit, 0.0)
    return (probe_vectors, region_loss)
```

```python
import functools

import jax
import jax.numpy as jnp
from jax import lax
from jax.experimental import pallas as pl
from jax.experimental.pallas import tpu as pltpu
from jax.sharding import PartitionSpec as P

REG = 64
LANES = 128

sharpness_divisor = 0.1
ln_eps = 1e-06
norm_eps = 1e-06

VMEM = pl.BlockSpec(memory_space=pltpu.VMEM)
SMEM = pl.BlockSpec(memory_space=pltpu.SMEM)
f32 = jnp.float32
bf16 = jnp.bfloat16


def call(kernel, outs, in_specs, scratch, limit, flops, nbytes):
    return pl.pallas_call(
        kernel,
        out_shape=outs,
        in_specs=in_specs,
        out_specs=[VMEM] * len(outs),
        scratch_shapes=scratch,
        compiler_params=pltpu.CompilerParams(vmem_limit_bytes=limit),
        cost_estimate=pl.CostEstimate(flops=flops, bytes_accessed=nbytes, transcendentals=0),
    )


def dot(a, b):
    return jnp.dot(a, b, preferred_element_type=f32)


def dot_nt(a, b):
    return lax.dot_general(a, b, (((1,), (1,)), ((), ())), preferred_element_type=f32)


def split3(x):
    hi = x.astype(bf16)
    rest = x - hi.astype(f32)
    mid = rest.astype(bf16)
    return hi, mid, (rest - mid.astype(f32)).astype(bf16)


def conv_kernel(geo, pos_ref, *refs):
    shards, shard_rows, width, out_rows = geo
    blocks = refs[:shards]
    w_ref, own_ref, pay_ref, img_ref = refs[shards : shards + 4]
    xpad, wide, taps = refs[shards + 4 :]
    half = w_ref.shape[1]
    row, first_row, col0 = pos_ref[0], pos_ref[1], pos_ref[2]
    height = shards * shard_rows
    pixels = shard_rows * width
    cols = xpad.shape[1]
    out_pixels = out_rows * width
    step_rows = 4

    xpad[0:3] = jnp.zeros((3, cols, LANES), f32)
    xpad[height + 3 : height + 6] = jnp.zeros((3, cols, LANES), f32)
    for y in range(3, height + 3):
        xpad[y, 0:8] = jnp.zeros((8, LANES), f32)
        xpad[y, 8 + width : 16 + width] = jnp.zeros((8, LANES), f32)

    def group(g, carry):
        lanes = pl.ds(pl.multiple_of(g * LANES, LANES), LANES)
        for k in range(shards):
            value = blocks[k][0:pixels, lanes].astype(f32).reshape(shard_rows, width, LANES)
            xpad[pl.ds(3 + (row ^ k) * shard_rows, shard_rows), 8 : 8 + width, :] = value
        for t in range(49):
            wide[t] = jnp.broadcast_to(w_ref[t : t + 1, lanes], (8, LANES))

        def strip(i, carry):
            top = first_row + i * step_rows
            acc = [jnp.zeros((width // 8, 8, LANES), f32) for _ in range(step_rows)]
            for r in range(step_rows + 6):
                for dx in range(7):
                    v = xpad[top + r, pl.ds(col0 + dx, width), :].reshape(width // 8, 8, LANES)
                    for j in range(step_rows):
                        dy = r - j
                        if 0 <= dy < 7:
                            acc[j] = acc[j] + v * wide[dy * 7 + dx][None]
            for j in range(step_rows):
                start = pl.multiple_of((i * step_rows + j) * width, width)
                taps[pl.ds(start, width), lanes] = acc[j].reshape(width, LANES)
            return carry

        return lax.fori_loop(0, out_rows // step_rows, strip, carry)

    lax.fori_loop(0, half // LANES, group, 0)

    def finish(i, carry):
        rows = pl.ds(pl.multiple_of(i * 64, 64), 64)
        t = taps[rows, :]
        mean = jnp.sum(t, axis=1, keepdims=True) * (1.0 / half)
        c = t - mean
        square = jnp.sum(c * c, axis=1, keepdims=True)
        own_ref[rows, :] = c
        pay_ref[rows, 0:half] = c.astype(bf16)
        lane = lax.broadcasted_iota(jnp.int32, (64, LANES), 1)
        packed = jnp.zeros((64, LANES), f32)
        for n, part in enumerate(split3(mean) + split3(square)):
            packed = jnp.where(lane == n, part.astype(f32), packed)
        pay_ref[rows, half : half + LANES] = packed.astype(bf16)
        return carry

    lax.fori_loop(0, out_pixels // 64, finish, 0)
    for k in range(shards):
        start = (row ^ k) * pixels - first_row * width

        @pl.when((start >= 0) & (start < out_pixels))
        def _():
            img_ref[pl.ds(pl.multiple_of(start, pixels), pixels), :] = blocks[k][0:pixels, :]


def unpack_stats(pay_ref, half):
    packed = pay_ref[:, half : half + LANES].astype(f32)
    lane = lax.broadcasted_iota(jnp.int32, packed.shape, 1)
    mean = jnp.sum(jnp.where(lane < 3, packed, 0.0), axis=1, keepdims=True)
    square = jnp.sum(jnp.where((lane >= 3) & (lane < 6), packed, 0.0), axis=1, keepdims=True)
    return mean, square


def block_kernel(pos_ref, own_ref, pay_ref, other_ref, img_ref, gain_ref, scale_ref, w1_ref, w2_ref,
                 z_ref, send_ref, normed, inner):
    pixels, half = own_ref.shape
    chans, hid = w1_ref.shape
    section = pos_ref[3]
    mean_a, square_a = unpack_stats(pay_ref, half)
    mean_b, square_b = unpack_stats(other_ref, half)
    mean = 0.5 * (mean_a + mean_b)
    gap = mean_a - mean_b
    spread = (square_a + square_b + gap * gap * (0.5 * half)) * (1.0 / chans)
    inv = lax.rsqrt(spread + ln_eps)
    shift_a = mean_a - mean
    shift_b = mean_b - mean
    mine = (own_ref[...] + shift_a) * inv * gain_ref[pl.ds(section, 1)][0].astype(f32)
    normed[pl.ds(section, 1)] = mine.astype(bf16)[None]
    theirs = (other_ref[:, 0:half].astype(f32) + shift_b) * inv * gain_ref[pl.ds(1 - section, 1)][0].astype(f32)
    normed[pl.ds(1 - section, 1)] = theirs.astype(bf16)[None]
    step = 256

    def widen(i, carry):
        cols = pl.ds(pl.multiple_of(i * step, step), step)
        h = dot(normed[0], w1_ref[0:half, cols]) + dot(normed[1], w1_ref[half:chans, cols])
        inner[:, cols] = (0.5 * h * (1.0 + lax.erf(h * 0.7071067811865476))).astype(bf16)
        return carry

    lax.fori_loop(0, hid // step, widen, 0)

    def narrow(i, carry):
        side = i // (half // step)
        cols = pl.ds(pl.multiple_of(i * step, step), step)
        image_cols = pl.ds(pl.multiple_of((i - side * (half // step)) * step, step), step)
        keep = jnp.where(side == section, 1.0, 0.0)
        z = dot(inner[...], w2_ref[:, cols]) * scale_ref[:, cols].astype(f32)
        z = z + img_ref[:, image_cols].astype(f32) * keep
        z_ref[:, cols] = z
        send_ref[:, cols] = z.astype(bf16)
        return carry

    lax.fori_loop(0, chans // step, narrow, 0)


def prep_kernel(geo, pos_ref, *refs):
    shards, width, out_pixels, images, batches, per_key, parts = geo
    ids = refs[:shards]
    owner_ref, partner_ref, hot_ref, pick_ref, own_ref, flat = refs[shards:]
    row, first_row, batch, first_slot = pos_ref[0], pos_ref[1], pos_ref[4], pos_ref[5]
    pixels = ids[0].shape[1]
    owned = own_ref.shape[0]
    slots = images * REG
    image = row // parts
    flat[...] = jnp.full(flat.shape, -1.0, f32)
    for k in range(shards):
        start = pl.multiple_of((1 + (row ^ k)) * pixels, LANES)
        flat[0:1, pl.ds(start, pixels)] = ids[k][pl.ds(image, 1), :]
    total = flat.shape[1]
    whole = jnp.broadcast_to(flat[0:1, :], (8, total))
    lane = lax.broadcasted_iota(jnp.int32, (8, total), 1)
    col = lane % width
    region = lax.broadcasted_iota(jnp.int32, (REG, out_pixels), 0).astype(f32)
    start = pl.multiple_of(pixels + first_row * width, LANES)
    for dy in range(3):
        for dx in range(3):
            off = (dy - 1) * width + dx - 1
            moved = whole if off == 0 else pltpu.roll(whole, off % total, 1)
            if dx == 0:
                moved = jnp.where(col == width - 1, -1.0, moved)
            if dx == 2:
                moved = jnp.where(col == 0, -1.0, moved)
            flat[8:16, :] = moved
            line = flat[8:9, pl.ds(start, out_pixels)]
            tap = dy * 3 + dx
            hot_ref[tap * REG : (tap + 1) * REG, :] = jnp.where(region == line, 1.0, 0.0).astype(bf16)
    slot = lax.broadcasted_iota(jnp.int32, (owned, slots), 1)
    want = lax.broadcasted_iota(jnp.int32, (owned, slots), 0) + first_slot
    pick = owner_ref[...] == want
    pick_ref[...] = jnp.where(pick, 1.0, 0.0).astype(bf16)
    one_region = lax.broadcasted_iota(jnp.int32, (REG, pixels), 0).astype(f32)
    tallies = []
    for i in range(images):
        tally = jnp.zeros((REG, pixels), f32)
        for k in range(shards):
            tally = tally + jnp.where(one_region == ids[k][i : i + 1, :], 1.0, 0.0)
        tallies.append(tally)
    tally = jnp.concatenate(tallies, axis=0).astype(bf16)
    count = dot_nt(jnp.ones((8, pixels), bf16), tally)[0:1]
    mate = (batch * images + slot // REG) * REG + partner_ref[...]
    block = mate // per_key
    place = ((block % shards) ^ row) * batches + ((block // shards) ^ batch)
    place = place * per_key + mate % per_key
    place = jnp.sum(jnp.where(pick, place, 0).astype(f32), axis=1, keepdims=True)
    number = jnp.sum(jnp.where(pick, count, 0.0), axis=1, keepdims=True)
    side = lax.broadcasted_iota(jnp.int32, (owned, LANES), 1)
    own_ref[...] = jnp.where(side == 0, place, jnp.where(side == 1, number, 0.0))


def project_kernel(z_ref, other_ref, pe_ref, pk_ref, hot_ref, out_ref, block):
    pixels, chans = z_ref.shape
    hidden = pe_ref.shape[1]
    taps = pk_ref.shape[0]
    block[...] = (z_ref[...] + other_ref[...].astype(f32)).astype(bf16)
    step = 256
    out_ref[...] = jnp.zeros(out_ref.shape, f32)

    def chunk(i, carry):
        cols = pl.ds(pl.multiple_of(i * step, step), step)
        h = jnp.maximum(dot(block[...], pe_ref[:, cols]), 0.0).astype(bf16)
        sums = dot(hot_ref[...], h)
        hi = sums.astype(bf16)
        lo = (sums - hi.astype(f32)).astype(bf16)
        acc = jnp.zeros((2 * REG, out_ref.shape[1]), f32)
        for t in range(taps):
            rows = slice(t * REG, (t + 1) * REG)
            both = jnp.concatenate([hi[rows], lo[rows]], axis=0)
            acc = acc + dot(both, pk_ref[t, cols, :])
        out_ref[...] += acc[0:REG] + acc[REG:]
        return carry

    lax.fori_loop(0, hidden // step, chunk, 0)


def loss_kernel(geo, pos_ref, *refs):
    shards, parts = geo
    sums = refs[:shards]
    pick_ref, own_ref, keys_ref, embed_ref, loss_ref, table = refs[shards:]
    row = pos_ref[0]
    for k in range(shards):
        src = row ^ k
        place = pl.ds(pl.multiple_of((src // parts) * REG, REG), REG)
        if parts == 1:
            table[place, :] = sums[k][...]
    if parts > 1:
        table[...] = jnp.zeros(table.shape, f32)
        for k in range(shards):
            place = pl.ds(pl.multiple_of(((row ^ k) // parts) * REG, REG), REG)
            table[place, :] += sums[k][...]
    pick = pick_ref[...]
    hi, mid, lo = split3(table[...])
    ordered = dot(pick, hi) + dot(pick, mid) + dot(pick, lo)
    unit = ordered * lax.rsqrt(jnp.sum(ordered * ordered, axis=1, keepdims=True) + norm_eps)
    embed_ref[...] = unit
    owned = unit.shape[0]
    keys = keys_ref[...]
    wide = keys.astype(f32)
    square = wide * wide
    square_hi = square.astype(bf16)
    square_lo = (square - square_hi.astype(f32)).astype(bf16)
    ones = jnp.ones((16, keys.shape[1]), bf16)
    length = dot_nt(ones, square_hi)[0:1] + dot_nt(ones, square_lo)[0:1]
    three = dot_nt(jnp.concatenate(split3(unit), axis=0), keys)
    logits = three[0:owned] + three[owned : 2 * owned] + three[2 * owned :]
    logits = logits * (lax.rsqrt(length + norm_eps) / sharpness_divisor)
    total = jnp.log(jnp.sum(jnp.exp(logits), axis=1, keepdims=True))
    column = lax.broadcasted_iota(jnp.int32, logits.shape, 1).astype(f32)
    match = jnp.sum(jnp.where(column == own_ref[:, 0:1], logits, 0.0), axis=1, keepdims=True)
    loss = jnp.where(own_ref[:, 1:2] > 0.5, total - match, 0.0)
    line = lax.broadcasted_iota(jnp.int32, (owned, owned), 0)
    other = lax.broadcasted_iota(jnp.int32, (owned, owned), 1)
    loss_ref[...] = jnp.sum(jnp.where(line == other, loss, 0.0), axis=0, keepdims=True)


def swap(x, axis, bit):
    return lax.ppermute(x, axis, [(i, i ^ bit) for i in range(lax.axis_size(axis))])


def body(
    features,
    dw_kernel,
    ln_gain,
    widening_pointwise_matrix,
    w_reduce,
    layer_branch_scale,
    p_expand,
    p_kernel,
    region_ids,
    owner_slot,
    partner,
    key_embed,
):
    images, shard_rows, width, chans = features.shape
    shards = lax.axis_size("rows")
    batches = lax.axis_size("batch")
    row = lax.axis_index("rows")
    batch = lax.axis_index("batch")
    section = lax.axis_index("section")
    half = chans // lax.axis_size("section")
    parts = shards // images
    out_rows = shards * shard_rows // parts
    pixels = shard_rows * width
    out_pixels = out_rows * width
    slots = images * REG
    owned = slots // shards
    out_dim = p_kernel.shape[2]
    mib = 1 << 20

    tail = jnp.pad(
        region_ids.astype(bf16).reshape(images, pixels), ((0, 8 - images), (0, half - pixels))
    )
    got = []
    for k in range(shards):
        to = (row ^ k) // parts
        part = lax.dynamic_slice(
            features, (to, 0, 0, section * half), (1, shard_rows, width, half)
        ).reshape(pixels, half)
        part = jnp.concatenate([part, tail], axis=0)
        got.append(part if k == 0 else swap(part, "rows", k))
    ids = [g[pixels : pixels + images, 0:pixels].astype(f32) for g in got]

    keys = key_embed
    for axis, size in (("batch", batches), ("rows", shards)):
        bit = 1
        while bit < size:
            keys = jnp.concatenate([keys, swap(keys, axis, bit)], axis=0)
            bit *= 2

    first_row = (row % parts) * out_rows
    spot = jnp.stack(
        [row, first_row, jnp.int32(5), section, batch, row * owned]
    ).astype(jnp.int32)
    taps_w = lax.dynamic_slice(
        dw_kernel.reshape(49, chans), (0, section * half), (49, half)
    ).astype(f32)
    own, pay, img = call(
        functools.partial(conv_kernel, (shards, shard_rows, width, out_rows)),
        [
            jax.ShapeDtypeStruct((out_pixels, half), f32),
            jax.ShapeDtypeStruct((out_pixels, half + LANES), bf16),
            jax.ShapeDtypeStruct((out_pixels, half), bf16),
        ],
        [SMEM] + [VMEM] * (shards + 1),
        [
            pltpu.VMEM((shards * shard_rows + 6, width + 16, LANES), f32),
            pltpu.VMEM((49, 8, LANES), f32),
            pltpu.VMEM((out_pixels, half), f32),
        ],
        16 * mib,
        out_pixels * half * 98,
        out_pixels * half * 10,
    )(spot, *got, taps_w)
    pay_other = swap(pay, "section", 1)

    hot, pick, facts = call(
        functools.partial(
            prep_kernel, (shards, width, out_pixels, images, batches, key_embed.shape[0], parts)
        ),
        [
            jax.ShapeDtypeStruct((9 * REG, out_pixels), bf16),
            jax.ShapeDtypeStruct((owned, slots), bf16),
            jax.ShapeDtypeStruct((owned, LANES), f32),
        ],
        [SMEM] + [VMEM] * (shards + 2),
        [pltpu.VMEM((16, (shards + 2) * pixels), f32)],
        16 * mib,
        10**7,
        10**6,
    )(spot, *ids, owner_slot, partner.reshape(1, slots))

    hid = widening_pointwise_matrix.shape[1]
    z, send = call(
        block_kernel,
        [
            jax.ShapeDtypeStruct((out_pixels, chans), f32),
            jax.ShapeDtypeStruct((out_pixels, chans), bf16),
        ],
        [SMEM] + [VMEM] * 8,
        [pltpu.VMEM((2, out_pixels, half), bf16), pltpu.VMEM((out_pixels, hid), bf16)],
        32 * mib,
        4 * out_pixels * hid * chans,
        4 * hid * chans,
    )(
        spot, own, pay, pay_other, img, ln_gain.reshape(2, 1, half), layer_branch_scale.reshape(1, chans),
        widening_pointwise_matrix, w_reduce,
    )
    z_other = swap(send, "section", 1)

    hidden = p_expand.shape[1]
    (pooled,) = call(
        project_kernel,
        [jax.ShapeDtypeStruct((REG, out_dim), f32)],
        [VMEM] * 5,
        [pltpu.VMEM((out_pixels, chans), bf16)],
        32 * mib,
        2 * out_pixels * hidden * chans + 4 * 9 * REG * hidden * out_pixels,
        4 * hidden * chans,
    )(z, z_other, p_expand, p_kernel, hot)
    pooled = pooled + swap(pooled, "section", 1)
    sums = [pooled] + [swap(pooled, "rows", k) for k in range(1, shards)]

    embed, loss = call(
        functools.partial(loss_kernel, (shards, parts)),
        [jax.ShapeDtypeStruct((owned, out_dim), f32), jax.ShapeDtypeStruct((1, owned), f32)],
        [SMEM] + [VMEM] * (shards + 3),
        [pltpu.VMEM((slots, out_dim), f32)],
        24 * mib,
        10**8,
        10**6,
    )(spot, *sums, pick, facts, keys)
    return embed, loss.reshape(owned)


def solution(mesh):
    in_specs = (
        P("batch", "rows", None, None),
        P(),
        P(),
        P(None, "section"),
        P("section", None),
        P(),
        P(None, "section"),
        P(None, "section", None),
        P("batch", "rows", None),
        P("batch", None),
        P("batch", None),
        P(("batch", "rows"), None),
    )
    out_specs = (P(("batch", "rows"), None), P(("batch", "rows")))
    return jax.shard_map(body, mesh=mesh, in_specs=in_specs, out_specs=out_specs, check_vma=False)
```

```python
import functools

import jax
import jax.numpy as jnp
from jax import lax
from jax.experimental import pallas as pl
from jax.experimental.pallas import tpu as pltpu
from jax.sharding import PartitionSpec as P

REG = 64
LANES = 128
STRIP = 4
CHUNKS = 2

sharpness_divisor = 0.1
ln_eps = 1e-06
norm_eps = 1e-06

VMEM = pl.BlockSpec(memory_space=pltpu.VMEM)
SMEM = pl.BlockSpec(memory_space=pltpu.SMEM)
f32 = jnp.float32
bf16 = jnp.bfloat16


def call(kernel, outs, in_specs, scratch, limit, flops, nbytes):
    return pl.pallas_call(
        kernel,
        out_shape=outs,
        in_specs=in_specs,
        out_specs=[VMEM] * len(outs),
        scratch_shapes=scratch,
        compiler_params=pltpu.CompilerParams(vmem_limit_bytes=limit),
        cost_estimate=pl.CostEstimate(flops=flops, bytes_accessed=nbytes, transcendentals=0),
    )


def dot(a, b):
    return jnp.dot(a, b, preferred_element_type=f32)


def dot_nt(a, b):
    return lax.dot_general(a, b, (((1,), (1,)), ((), ())), preferred_element_type=f32)


def split3(x):
    hi = x.astype(bf16)
    rest = x - hi.astype(f32)
    mid = rest.astype(bf16)
    return hi, mid, (rest - mid.astype(f32)).astype(bf16)


def conv_kernel(geo, pos_ref, *refs):
    shards, shard_rows, width, out_rows = geo
    blocks = refs[:shards]
    w_ref, taps, img_ref, xpad, wide = refs[shards:]
    chunk = w_ref.shape[1]
    row, first_row, col0 = pos_ref[0], pos_ref[1], pos_ref[2]
    height = shards * shard_rows
    pixels = shard_rows * width
    cols = xpad.shape[1]
    out_pixels = out_rows * width
    step_rows = STRIP

    xpad[0:3] = jnp.zeros((3, cols, LANES), f32)
    xpad[height + 3 : height + 6] = jnp.zeros((3, cols, LANES), f32)
    for y in range(3, height + 3):
        xpad[y, 0:8] = jnp.zeros((8, LANES), f32)
        xpad[y, 8 + width : 16 + width] = jnp.zeros((8, LANES), f32)

    def group(g, carry):
        lanes = pl.ds(pl.multiple_of(g * LANES, LANES), LANES)
        for k in range(shards):
            value = blocks[k][0:pixels, lanes].astype(f32).reshape(shard_rows, width, LANES)
            xpad[pl.ds(3 + (row ^ k) * shard_rows, shard_rows), 8 : 8 + width, :] = value
        for t in range(49):
            wide[t] = jnp.broadcast_to(w_ref[t : t + 1, lanes], (8, LANES))

        def strip(i, carry):
            top = first_row + i * step_rows
            acc = [jnp.zeros((width // 8, 8, LANES), f32) for _ in range(step_rows)]
            for r in range(step_rows + 6):
                for dx in range(7):
                    v = xpad[top + r, pl.ds(col0 + dx, width), :].reshape(width // 8, 8, LANES)
                    for j in range(step_rows):
                        dy = r - j
                        if 0 <= dy < 7:
                            acc[j] = acc[j] + v * wide[dy * 7 + dx][None]
            for j in range(step_rows):
                start = pl.multiple_of((i * step_rows + j) * width, width)
                taps[pl.ds(start, width), lanes] = acc[j].reshape(width, LANES)
            return carry

        return lax.fori_loop(0, out_rows // step_rows, strip, carry)

    lax.fori_loop(0, chunk // LANES, group, 0)

    for k in range(shards):
        start = (row ^ k) * pixels - first_row * width

        @pl.when((start >= 0) & (start < out_pixels))
        def _():
            img_ref[pl.ds(pl.multiple_of(start, pixels), pixels), :] = blocks[k][0:pixels, :]


def block_kernel(geo, pos_ref, *refs):
    first, pixels, chunks = geo
    own, other, img = refs[:chunks], refs[chunks : 2 * chunks], refs[2 * chunks : 3 * chunks]
    gain_ref, scale_ref, w1_ref, w2_ref, z_ref, send_ref, normed, inner = refs[3 * chunks :]
    chans, hid = w1_ref.shape
    half = chans // 2
    width = half // chunks
    section = pos_ref[3]
    rows = slice(first, first + pixels)
    values = [ref[rows, :] for ref in own + other]
    mean = sum(jnp.sum(v, axis=1, keepdims=True) for v in values) * (1.0 / chans)
    values = [v - mean for v in values]
    spread = sum(jnp.sum(v * v, axis=1, keepdims=True) for v in values) * (1.0 / chans)
    inv = lax.rsqrt(spread + ln_eps)
    for c in range(chunks):
        lanes = slice(c * width, (c + 1) * width)
        for side, v in ((section, values[c]), (1 - section, values[chunks + c])):
            gain = gain_ref[pl.ds(side, 1)][0, :, lanes]
            normed[pl.ds(side, 1), :, lanes] = (v * inv * gain).astype(bf16)[None]
    step = 256
    for i in range(hid // step):
        cols = slice(i * step, (i + 1) * step)
        h = dot(normed[0], w1_ref[0:half, cols]) + dot(normed[1], w1_ref[half:chans, cols])
        inner[:, cols] = (0.5 * h * (1.0 + lax.erf(h * 0.7071067811865476))).astype(bf16)
    step = width if width % 256 else 256
    for i in range(chans // step):
        cols = slice(i * step, (i + 1) * step)
        side, start = divmod(i * step, half)
        c, start = divmod(start, width)
        keep = jnp.where(section == side, 1.0, 0.0)
        z = dot(inner[...], w2_ref[:, cols]) * scale_ref[:, cols]
        z = z + img[c][rows, start : start + step].astype(f32) * keep
        z_ref[:, cols] = z
        send_ref[:, cols] = z.astype(bf16)


def expand_kernel(z_ref, other_ref, pe_ref, out_ref, block):
    block[...] = (z_ref[...] + other_ref[...].astype(f32)).astype(bf16)
    step = 256
    for i in range(pe_ref.shape[1] // step):
        cols = slice(i * step, (i + 1) * step)
        out_ref[:, cols] = jnp.maximum(dot(block[...], pe_ref[:, cols]), 0.0).astype(bf16)


def prep_kernel(geo, pos_ref, *refs):
    shards, width, out_pixels, images, batches, per_key, parts = geo
    ids = refs[:shards]
    owner_ref, partner_ref, hot_ref, pick_ref, own_ref, flat = refs[shards:]
    row, first_row, batch, first_slot = pos_ref[0], pos_ref[1], pos_ref[4], pos_ref[5]
    pixels = LANES
    tail = ids[0].shape[0] - 16
    ids = [ref[tail : tail + 16, 0:pixels].astype(f32) for ref in ids]
    owned = own_ref.shape[0]
    slots = images * REG
    image = row // parts
    flat[...] = jnp.full(flat.shape, -1.0, f32)
    for k in range(shards):
        start = pl.multiple_of((1 + (row ^ k)) * pixels, LANES)
        mine = lax.broadcasted_iota(jnp.int32, ids[k].shape, 0) == image
        mine = jnp.sum(jnp.where(mine, ids[k], 0.0), axis=0, keepdims=True)
        flat[0:1, pl.ds(start, pixels)] = mine
    total = flat.shape[1]
    whole = jnp.broadcast_to(flat[0:1, :], (8, total))
    lane = lax.broadcasted_iota(jnp.int32, (8, total), 1)
    col = lane % width
    region = lax.broadcasted_iota(jnp.int32, (REG, out_pixels), 0).astype(f32)
    start = pl.multiple_of(pixels + first_row * width, LANES)
    for dy in range(3):
        for dx in range(3):
            off = (dy - 1) * width + dx - 1
            moved = whole if off == 0 else pltpu.roll(whole, off % total, 1)
            if dx == 0:
                moved = jnp.where(col == width - 1, -1.0, moved)
            if dx == 2:
                moved = jnp.where(col == 0, -1.0, moved)
            flat[8:16, :] = moved
            line = flat[8:9, pl.ds(start, out_pixels)]
            tap = dy * 3 + dx
            hot_ref[tap * REG : (tap + 1) * REG, :] = jnp.where(region == line, 1.0, 0.0).astype(bf16)
    slot = lax.broadcasted_iota(jnp.int32, (owned, slots), 1)
    want = lax.broadcasted_iota(jnp.int32, (owned, slots), 0) + first_slot
    pick = owner_ref[...] == want
    pick_ref[...] = jnp.where(pick, 1.0, 0.0).astype(bf16)
    one_region = lax.broadcasted_iota(jnp.int32, (REG, pixels), 0).astype(f32)
    tallies = []
    for i in range(images):
        tally = jnp.zeros((REG, pixels), f32)
        for k in range(shards):
            tally = tally + jnp.where(one_region == ids[k][i : i + 1, :], 1.0, 0.0)
        tallies.append(tally)
    tally = jnp.concatenate(tallies, axis=0).astype(bf16)
    count = dot_nt(jnp.ones((8, pixels), bf16), tally)[0:1]
    mate = (batch * images + slot // REG) * REG + partner_ref[...]
    block = mate // per_key
    place = ((block % shards) ^ row) * batches + ((block // shards) ^ batch)
    place = place * per_key + mate % per_key
    place = jnp.sum(jnp.where(pick, place, 0).astype(f32), axis=1, keepdims=True)
    number = jnp.sum(jnp.where(pick, count, 0.0), axis=1, keepdims=True)
    side = lax.broadcasted_iota(jnp.int32, (owned, LANES), 1)
    own_ref[...] = jnp.where(side == 0, place, jnp.where(side == 1, number, 0.0))


def project_kernel(z_ref, other_ref, first_ref, pe_ref, pk_ref, hot_ref, out_ref, block, hidden):
    before = first_ref.shape[0]
    pixels = z_ref.shape[0]
    taps = pk_ref.shape[0]
    block[...] = (z_ref[...] + other_ref[...].astype(f32)).astype(bf16)
    step = 256
    acc = jnp.zeros((2 * REG, out_ref.shape[1]), f32)
    for i in range(pe_ref.shape[1] // step):
        cols = slice(i * step, (i + 1) * step)
        hidden[i, 0:before, :] = first_ref[:, cols]
        h = jnp.maximum(dot(block[...], pe_ref[:, cols]), 0.0)
        hidden[i, before : before + pixels, :] = h.astype(bf16)
        sums = dot(hot_ref[...], hidden[i])
        hi = sums.astype(bf16)
        lo = (sums - hi.astype(f32)).astype(bf16)
        for t in range(taps):
            rows = slice(t * REG, (t + 1) * REG)
            both = jnp.concatenate([hi[rows], lo[rows]], axis=0)
            acc = acc + dot(both, pk_ref[t, cols, :])
    out_ref[...] = acc[0:REG] + acc[REG:]


def loss_kernel(geo, pos_ref, *refs):
    shards, parts = geo
    sums = refs[:shards]
    pick_ref, own_ref = refs[shards : shards + 2]
    embed_ref, loss_ref, table = refs[-3:]
    row = pos_ref[0]
    for k in range(shards):
        src = row ^ k
        place = pl.ds(pl.multiple_of((src // parts) * REG, REG), REG)
        if parts == 1:
            table[place, :] = sums[k][...]
    if parts > 1:
        table[...] = jnp.zeros(table.shape, f32)
        for k in range(shards):
            place = pl.ds(pl.multiple_of(((row ^ k) // parts) * REG, REG), REG)
            table[place, :] += sums[k][...]
    pick = pick_ref[...]
    hi, mid, lo = split3(table[...])
    ordered = dot(pick, hi) + dot(pick, mid) + dot(pick, lo)
    unit = ordered * lax.rsqrt(jnp.sum(ordered * ordered, axis=1, keepdims=True) + norm_eps)
    embed_ref[...] = unit
    owned = unit.shape[0]
    keys = jnp.concatenate([ref[...] for ref in refs[shards + 2 : -3]], axis=0)
    wide = keys.astype(f32)
    square = wide * wide
    square_hi = square.astype(bf16)
    square_lo = (square - square_hi.astype(f32)).astype(bf16)
    ones = jnp.ones((16, keys.shape[1]), bf16)
    length = dot_nt(ones, square_hi)[0:1] + dot_nt(ones, square_lo)[0:1]
    three = dot_nt(jnp.concatenate(split3(unit), axis=0), keys)
    logits = three[0:owned] + three[owned : 2 * owned] + three[2 * owned :]
    logits = logits * (lax.rsqrt(length + norm_eps) / sharpness_divisor)
    total = jnp.log(jnp.sum(jnp.exp(logits), axis=1, keepdims=True))
    column = lax.broadcasted_iota(jnp.int32, logits.shape, 1).astype(f32)
    match = jnp.sum(jnp.where(column == own_ref[:, 0:1], logits, 0.0), axis=1, keepdims=True)
    loss = jnp.where(own_ref[:, 1:2] > 0.5, total - match, 0.0)
    line = lax.broadcasted_iota(jnp.int32, (owned, owned), 0)
    other = lax.broadcasted_iota(jnp.int32, (owned, owned), 1)
    loss_ref[...] = jnp.sum(jnp.where(line == other, loss, 0.0), axis=0, keepdims=True)


def swap(x, axis, bit):
    return lax.ppermute(x, axis, [(i, i ^ bit) for i in range(lax.axis_size(axis))])


def body(
    features,
    dw_kernel,
    ln_gain,
    widening_pointwise_matrix,
    w_reduce,
    layer_branch_scale,
    p_expand,
    p_kernel,
    region_ids,
    owner_slot,
    partner,
    key_embed,
):
    images, shard_rows, width, chans = features.shape
    shards = lax.axis_size("rows")
    batches = lax.axis_size("batch")
    row = lax.axis_index("rows")
    batch = lax.axis_index("batch")
    section = lax.axis_index("section")
    half = chans // lax.axis_size("section")
    parts = shards // images
    out_rows = shards * shard_rows // parts
    pixels = shard_rows * width
    out_pixels = out_rows * width
    slots = images * REG
    owned = slots // shards
    out_dim = p_kernel.shape[2]
    mib = 1 << 20
    span = half // CHUNKS

    w1, w2, pe, pk = widening_pointwise_matrix, w_reduce, p_expand, p_kernel

    pieces = [key_embed]
    steps = []
    for axis, size in (("batch", batches), ("rows", shards)):
        steps += [(axis, 1 << n) for n in range(size.bit_length() - 1)]

    def after(here, *done):
        count = -(-len(steps) // 4)
        for axis, bit in (steps.pop(0) for _ in range(min(count, len(steps)))):
            pieces.append(swap(jnp.concatenate(pieces, axis=0), axis, bit))
        return lax.optimization_barrier((here, pieces[-1]) + done)[:2]

    got = []
    for c in range(CHUNKS):
        tail = jnp.pad(
            region_ids.astype(bf16).reshape(images, pixels), ((0, 16 - images), (0, span - pixels))
        )
        blocks = []
        for k in range(shards):
            to = (row ^ k) // parts
            part = lax.dynamic_slice(
                features, (to, 0, 0, section * half + c * span), (1, shard_rows, width, span)
            ).reshape(pixels, span)
            if c == CHUNKS - 1:
                part = jnp.concatenate([part, tail], axis=0)
            blocks.append(part)
        if c:
            blocks, pieces[-1] = after(blocks)
        got.append([blocks[0]] + [swap(blocks[k], "rows", k) for k in range(1, shards)])

    first_row = (row % parts) * out_rows
    spot = jnp.stack(
        [row, first_row, jnp.int32(5), section, batch, row * owned]
    ).astype(jnp.int32)
    own, other, img = [], [], []
    for c in range(CHUNKS):
        here = spot
        if c:
            here, pieces[-1] = after(spot, *own)
        weights = lax.dynamic_slice(
            dw_kernel.reshape(49, chans), (0, section * half + c * span), (49, span)
        ).astype(f32)
        taps, image = call(
            functools.partial(conv_kernel, (shards, shard_rows, width, out_rows)),
            [
                jax.ShapeDtypeStruct((out_pixels, span), f32),
                jax.ShapeDtypeStruct((out_pixels, span), bf16),
            ],
            [SMEM] + [VMEM] * (shards + 1),
            [
                pltpu.VMEM((shards * shard_rows + 6, width + 16, LANES), f32),
                pltpu.VMEM((49, 8, LANES), f32),
            ],
            4 * mib,
            out_pixels * span * 98 * 40,
            out_pixels * span * 10,
        )(here, *got[c], weights)
        own.append(taps)
        img.append(image)
        other.append(swap(taps, "section", 1))

    hot, pick, facts = call(
        functools.partial(
            prep_kernel, (shards, width, out_pixels, images, batches, key_embed.shape[0], parts)
        ),
        [
            jax.ShapeDtypeStruct((9 * REG, out_pixels), bf16),
            jax.ShapeDtypeStruct((owned, slots), bf16),
            jax.ShapeDtypeStruct((owned, LANES), f32),
        ],
        [SMEM] + [VMEM] * (shards + 2),
        [pltpu.VMEM((16, (shards + 2) * pixels), f32)],
        4 * mib,
        10**8,
        10**6,
    )(spot, *got[-1], owner_slot, partner.reshape(1, slots))

    hid = w1.shape[1]
    part_pixels = out_pixels // 2
    gain = ln_gain.astype(f32).reshape(2, 1, half)
    scale = layer_branch_scale.astype(f32).reshape(1, chans)
    z, z_other = [], []
    for p in range(2):
        here, pieces[-1] = after(spot, hot, *z)
        mine, send = call(
            functools.partial(block_kernel, (p * part_pixels, part_pixels, CHUNKS)),
            [
                jax.ShapeDtypeStruct((part_pixels, chans), f32),
                jax.ShapeDtypeStruct((part_pixels, chans), bf16),
            ],
            [SMEM] + [VMEM] * (3 * CHUNKS + 4),
            [pltpu.VMEM((2, part_pixels, half), bf16), pltpu.VMEM((part_pixels, hid), bf16)],
            12 * mib,
            4 * part_pixels * hid * chans,
            4 * hid * chans,
        )(here, *own, *other, *img, gain, scale, w1, w2)
        z.append(mine)
        z_other.append(swap(send, "section", 1))

    hidden = pe.shape[1]
    (hid_a,) = call(
        expand_kernel,
        [jax.ShapeDtypeStruct((part_pixels, hidden), bf16)],
        [VMEM] * 3,
        [pltpu.VMEM((part_pixels, chans), bf16)],
        8 * mib,
        2 * part_pixels * hidden * chans,
        2 * hidden * chans,
    )(z[0], z_other[0], pe)
    (pooled,) = call(
        project_kernel,
        [jax.ShapeDtypeStruct((REG, out_dim), f32)],
        [VMEM] * 6,
        [
            pltpu.VMEM((part_pixels, chans), bf16),
            pltpu.VMEM((hidden // 256, out_pixels, 256), bf16),
        ],
        12 * mib,
        2 * part_pixels * hidden * chans + 4 * 9 * REG * hidden * out_pixels,
        4 * hidden * chans,
    )(z[1], z_other[1], hid_a, pe, pk, hot)
    pooled = pooled + swap(pooled, "section", 1)
    sums = [pooled] + [swap(pooled, "rows", k) for k in range(1, shards)]

    embed, loss = call(
        functools.partial(loss_kernel, (shards, parts)),
        [jax.ShapeDtypeStruct((owned, out_dim), f32), jax.ShapeDtypeStruct((1, owned), f32)],
        [SMEM] + [VMEM] * (shards + 2 + len(pieces)),
        [pltpu.VMEM((slots, out_dim), f32)],
        8 * mib,
        10**8,
        10**6,
    )(spot, *sums, pick, facts, *pieces)
    return embed, loss.reshape(owned)


def solution(mesh):
    in_specs = (
        P("batch", "rows", None, None),
        P(),
        P(),
        P(None, "section"),
        P("section", None),
        P(),
        P(None, "section"),
        P(None, "section", None),
        P("batch", "rows", None),
        P("batch", None),
        P("batch", None),
        P(("batch", "rows"), None),
    )
    out_specs = (P(("batch", "rows"), None), P(("batch", "rows")))
    return jax.shard_map(body, mesh=mesh, in_specs=in_specs, out_specs=out_specs, check_vma=False)
```

```python
import functools

import jax
import jax.numpy as jnp
from jax import lax
from jax.experimental import pallas as pl
from jax.experimental.pallas import tpu as pltpu
from jax.sharding import PartitionSpec as P

REG = 64
LANES = 128
STRIP = 4
CHUNKS = 2

sharpness_divisor = 0.1
ln_eps = 1e-06
norm_eps = 1e-06

VMEM = pl.BlockSpec(memory_space=pltpu.VMEM)
SMEM = pl.BlockSpec(memory_space=pltpu.SMEM)
f32 = jnp.float32
bf16 = jnp.bfloat16


def call(kernel, outs, in_specs, scratch, limit, flops, nbytes):
    return pl.pallas_call(
        kernel,
        out_shape=outs,
        in_specs=in_specs,
        out_specs=[VMEM] * len(outs),
        scratch_shapes=scratch,
        compiler_params=pltpu.CompilerParams(vmem_limit_bytes=limit),
        cost_estimate=pl.CostEstimate(flops=flops, bytes_accessed=nbytes, transcendentals=0),
    )


def dot(a, b):
    return jnp.dot(a, b, preferred_element_type=f32)


def dot_nt(a, b):
    return lax.dot_general(a, b, (((1,), (1,)), ((), ())), preferred_element_type=f32)


def split3(x):
    hi = x.astype(bf16)
    rest = x - hi.astype(f32)
    mid = rest.astype(bf16)
    return hi, mid, (rest - mid.astype(f32)).astype(bf16)


def stage_kernel(geo, pos_ref, feat_ref, ids_ref, *refs):
    shards, chunks, parts = geo
    blocks, (line, sems) = refs[: shards * chunks], refs[shards * chunks :]
    row, section = pos_ref[0], pos_ref[3]
    images, pixels, chans = feat_ref.shape
    span = blocks[0].shape[1]
    copies = []
    for c in range(chunks):
        lanes = pl.ds(pl.multiple_of(section * (chans // 2) + c * span, LANES), span)
        for k in range(shards):
            copy = pltpu.make_async_copy(
                feat_ref.at[(row ^ k) // parts, :, lanes],
                blocks[c * shards + k].at[pl.ds(0, pixels)],
                sems.at[c * shards + k],
            )
            copy.start()
            copies.append(copy)
    line[...] = jnp.full(line.shape, -1.0, f32)
    shard_rows, width = ids_ref.shape[1:]
    for i in range(images):
        line[i * shard_rows : (i + 1) * shard_rows, 0:width] = ids_ref[i].astype(f32)
    for k in range(shards):
        blocks[(chunks - 1) * shards + k][pixels:, :] = line[...].astype(bf16)
    for copy in copies:
        copy.wait()


def join_kernel(*refs):
    start = 0
    for ref in refs[:-1]:
        refs[-1][start : start + ref.shape[0], :] = ref[...]
        start += ref.shape[0]


def join(*arrays):
    rows = sum(x.shape[0] for x in arrays)
    shape = jax.ShapeDtypeStruct((rows, arrays[0].shape[1]), arrays[0].dtype)
    joined = call(join_kernel, [shape], [VMEM] * len(arrays), [], 1 << 20, 0, rows * 1024)(*arrays)
    return joined[0]


def add_kernel(a_ref, b_ref, out_ref):
    for n in range(out_ref.shape[0]):
        out_ref[n] = a_ref[...] + b_ref[...]


def conv_kernel(geo, pos_ref, *refs):
    shards, shard_rows, width, out_rows, first_lane = geo
    blocks = refs[:shards]
    w_ref, taps, img_ref, xpad, wide = refs[shards:]
    chunk = taps.shape[1]
    row, first_row, col0 = pos_ref[0], pos_ref[1], pos_ref[2]
    base = pos_ref[3] * (w_ref.shape[2] // 2) + first_lane
    height = shards * shard_rows
    pixels = shard_rows * width
    cols = xpad.shape[1]
    out_pixels = out_rows * width
    step_rows = STRIP

    xpad[0:3] = jnp.zeros((3, cols, LANES), f32)
    xpad[height + 3 : height + 6] = jnp.zeros((3, cols, LANES), f32)
    for y in range(3, height + 3):
        xpad[y, 0:8] = jnp.zeros((8, LANES), f32)
        xpad[y, 8 + width : 16 + width] = jnp.zeros((8, LANES), f32)

    def group(g, carry):
        lanes = pl.ds(pl.multiple_of(g * LANES, LANES), LANES)
        for k in range(shards):
            value = blocks[k][0:pixels, lanes].astype(f32).reshape(shard_rows, width, LANES)
            xpad[pl.ds(3 + (row ^ k) * shard_rows, shard_rows), 8 : 8 + width, :] = value
        for dy in range(7):
            w = w_ref[dy, :, pl.ds(pl.multiple_of(base + g * LANES, LANES), LANES)].astype(f32)
            for dx in range(7):
                wide[dy * 7 + dx] = jnp.broadcast_to(w[dx : dx + 1], (8, LANES))

        def strip(i, carry):
            top = first_row + i * step_rows
            acc = [jnp.zeros((width // 8, 8, LANES), f32) for _ in range(step_rows)]
            for r in range(step_rows + 6):
                for dx in range(7):
                    v = xpad[top + r, pl.ds(col0 + dx, width), :].reshape(width // 8, 8, LANES)
                    for j in range(step_rows):
                        dy = r - j
                        if 0 <= dy < 7:
                            acc[j] = acc[j] + v * wide[dy * 7 + dx][None]
            for j in range(step_rows):
                start = pl.multiple_of((i * step_rows + j) * width, width)
                taps[pl.ds(start, width), lanes] = acc[j].reshape(width, LANES)
            return carry

        return lax.fori_loop(0, out_rows // step_rows, strip, carry)

    lax.fori_loop(0, chunk // LANES, group, 0)

    for k in range(shards):
        start = (row ^ k) * pixels - first_row * width

        @pl.when((start >= 0) & (start < out_pixels))
        def _():
            img_ref[pl.ds(pl.multiple_of(start, pixels), pixels), :] = blocks[k][0:pixels, :]


def block_kernel(geo, pos_ref, *refs):
    first, pixels, chunks = geo
    own, other, img = refs[:chunks], refs[chunks : 2 * chunks], refs[2 * chunks : 3 * chunks]
    gain_ref, scale_ref, w1_ref, w2_ref, z_ref, send_ref, normed, inner = refs[3 * chunks :]
    chans, hid = w1_ref.shape
    half = chans // 2
    width = half // chunks
    section = pos_ref[3]
    rows = slice(first, first + pixels)
    values = [ref[rows, :] for ref in own + other]
    mean = sum(jnp.sum(v, axis=1, keepdims=True) for v in values) * (1.0 / chans)
    values = [v - mean for v in values]
    spread = sum(jnp.sum(v * v, axis=1, keepdims=True) for v in values) * (1.0 / chans)
    inv = lax.rsqrt(spread + ln_eps)
    gains = gain_ref[...].astype(f32).reshape(1, chans)
    scales = scale_ref[...].astype(f32).reshape(1, chans)
    for c in range(chunks):
        lanes = slice(c * width, (c + 1) * width)
        for side, v in ((section, values[c]), (1 - section, values[chunks + c])):
            start = c * width
            gain = jnp.where(side == 0, gains[:, start : start + width], gains[:, half + start : half + start + width])
            normed[pl.ds(side, 1), :, lanes] = (v * inv * gain).astype(bf16)[None]
    step = 256
    for i in range(hid // step):
        cols = slice(i * step, (i + 1) * step)
        h = dot(normed[0], w1_ref[0:half, cols]) + dot(normed[1], w1_ref[half:chans, cols])
        inner[:, cols] = (0.5 * h * (1.0 + lax.erf(h * 0.7071067811865476))).astype(bf16)
    step = width if width % 256 else 256
    for i in range(chans // step):
        cols = slice(i * step, (i + 1) * step)
        side, start = divmod(i * step, half)
        c, start = divmod(start, width)
        keep = jnp.where(section == side, 1.0, 0.0)
        z = dot(inner[...], w2_ref[:, cols]) * scales[:, cols]
        z = z + img[c][rows, start : start + step].astype(f32) * keep
        z_ref[:, cols] = z
        send_ref[:, cols] = z.astype(bf16)


def expand_kernel(z_ref, other_ref, pe_ref, out_ref, block):
    block[...] = (z_ref[...] + other_ref[...].astype(f32)).astype(bf16)
    step = 256
    for i in range(pe_ref.shape[1] // step):
        cols = slice(i * step, (i + 1) * step)
        out_ref[:, cols] = jnp.maximum(dot(block[...], pe_ref[:, cols]), 0.0).astype(bf16)


def prep_kernel(geo, pos_ref, *refs):
    shards, shard_rows, width, out_pixels, images, batches, per_key, parts = geo
    ids = refs[:shards]
    owner_ref, partner_ref, hot_ref, pick_ref, own_ref, flat = refs[shards:]
    row, first_row, batch, first_slot = pos_ref[0], pos_ref[1], pos_ref[4], pos_ref[5]
    pixels = shard_rows * width
    ids = [ref[pixels:, 0:LANES].astype(f32) for ref in ids]
    owned = own_ref.shape[0]
    slots = images * REG
    image = row // parts
    flat[...] = jnp.full(flat.shape, -1.0, f32)
    for k in range(shards):
        start = pl.multiple_of((1 + (row ^ k)) * pixels, LANES)
        number = lax.broadcasted_iota(jnp.int32, ids[k].shape, 0)
        inside = lax.broadcasted_iota(jnp.int32, ids[k].shape, 1) < width
        for y in range(shard_rows):
            keep = inside & (number == image * shard_rows + y)
            mine = jnp.sum(jnp.where(keep, ids[k], 0.0), axis=0, keepdims=True)
            mine = jnp.broadcast_to(mine, (8, LANES))
            mine = pltpu.roll(mine, y * width, 1) if y else mine
            line = mine if y == 0 else line + mine
        flat[0:8, pl.ds(start, pixels)] = line
    total = flat.shape[1]
    whole = jnp.broadcast_to(flat[0:1, :], (8, total))
    lane = lax.broadcasted_iota(jnp.int32, (8, total), 1)
    col = lane % width
    region = lax.broadcasted_iota(jnp.int32, (REG, out_pixels), 0).astype(f32)
    start = pl.multiple_of(pixels + first_row * width, LANES)
    for dy in range(3):
        for dx in range(3):
            off = (dy - 1) * width + dx - 1
            moved = whole if off == 0 else pltpu.roll(whole, off % total, 1)
            if dx == 0:
                moved = jnp.where(col == width - 1, -1.0, moved)
            if dx == 2:
                moved = jnp.where(col == 0, -1.0, moved)
            flat[8:16, :] = moved
            line = flat[8:9, pl.ds(start, out_pixels)]
            tap = dy * 3 + dx
            hot_ref[tap * REG : (tap + 1) * REG, :] = jnp.where(region == line, 1.0, 0.0).astype(bf16)
    slot = lax.broadcasted_iota(jnp.int32, (owned, slots), 1)
    want = lax.broadcasted_iota(jnp.int32, (owned, slots), 0) + first_slot
    pick = owner_ref[...] == want
    pick_ref[...] = jnp.where(pick, 1.0, 0.0).astype(bf16)
    one_region = lax.broadcasted_iota(jnp.int32, (REG, LANES), 0).astype(f32)
    tallies = []
    for i in range(images):
        tally = jnp.zeros((REG, LANES), f32)
        for k in range(shards):
            for y in range(i * shard_rows, (i + 1) * shard_rows):
                tally = tally + jnp.where(one_region == ids[k][y : y + 1, :], 1.0, 0.0)
        tallies.append(tally)
    tally = jnp.concatenate(tallies, axis=0).astype(bf16)
    count = dot_nt(jnp.ones((8, LANES), bf16), tally)[0:1]
    mates = jnp.concatenate([partner_ref[i : i + 1, :] for i in range(images)], axis=1)
    mate = (batch * images + slot // REG) * REG + mates
    block = mate // per_key
    place = ((block % shards) ^ row) * batches + ((block // shards) ^ batch)
    place = place * per_key + mate % per_key
    place = jnp.sum(jnp.where(pick, place, 0).astype(f32), axis=1, keepdims=True)
    number = jnp.sum(jnp.where(pick, count, 0.0), axis=1, keepdims=True)
    side = lax.broadcasted_iota(jnp.int32, (owned, LANES), 1)
    own_ref[...] = jnp.where(side == 0, place, jnp.where(side == 1, number, 0.0))


def project_kernel(z_ref, other_ref, first_ref, pe_ref, pk_ref, hot_ref, out_ref, block, hidden):
    before = first_ref.shape[0]
    pixels = z_ref.shape[0]
    taps = pk_ref.shape[0]
    block[...] = (z_ref[...] + other_ref[...].astype(f32)).astype(bf16)
    step = 256
    acc = jnp.zeros((2 * REG, out_ref.shape[1]), f32)
    for i in range(pe_ref.shape[1] // step):
        cols = slice(i * step, (i + 1) * step)
        hidden[i, 0:before, :] = first_ref[:, cols]
        h = jnp.maximum(dot(block[...], pe_ref[:, cols]), 0.0)
        hidden[i, before : before + pixels, :] = h.astype(bf16)
        sums = dot(hot_ref[...], hidden[i])
        hi = sums.astype(bf16)
        lo = (sums - hi.astype(f32)).astype(bf16)
        for t in range(taps):
            rows = slice(t * REG, (t + 1) * REG)
            both = jnp.concatenate([hi[rows], lo[rows]], axis=0)
            acc = acc + dot(both, pk_ref[t, cols, :])
    out_ref[...] = acc[0:REG] + acc[REG:]


def loss_kernel(geo, *refs):
    shards, parts = geo
    sums, pick_ref, own_ref = refs[:3]
    embed_ref, loss_ref, table = refs[-3:]
    for i in range(shards // parts):
        value = sums[i * parts]
        for p in range(1, parts):
            value = value + sums[i * parts + p]
        table[i * REG : (i + 1) * REG, :] = value
    pick = pick_ref[...]
    hi, mid, lo = split3(table[...])
    ordered = dot(pick, hi) + dot(pick, mid) + dot(pick, lo)
    unit = ordered * lax.rsqrt(jnp.sum(ordered * ordered, axis=1, keepdims=True) + norm_eps)
    embed_ref[...] = unit
    owned = unit.shape[0]
    keys = jnp.concatenate([ref[...] for ref in refs[3:-3]], axis=0)
    wide = keys.astype(f32)
    square = wide * wide
    square_hi = square.astype(bf16)
    square_lo = (square - square_hi.astype(f32)).astype(bf16)
    ones = jnp.ones((16, keys.shape[1]), bf16)
    length = dot_nt(ones, square_hi)[0:1] + dot_nt(ones, square_lo)[0:1]
    three = dot_nt(jnp.concatenate(split3(unit), axis=0), keys)
    logits = three[0:owned] + three[owned : 2 * owned] + three[2 * owned :]
    logits = logits * (lax.rsqrt(length + norm_eps) / sharpness_divisor)
    total = jnp.log(jnp.sum(jnp.exp(logits), axis=1, keepdims=True))
    column = lax.broadcasted_iota(jnp.int32, logits.shape, 1).astype(f32)
    match = jnp.sum(jnp.where(column == own_ref[:, 0:1], logits, 0.0), axis=1, keepdims=True)
    loss = jnp.where(own_ref[:, 1:2] > 0.5, total - match, 0.0)
    line = lax.broadcasted_iota(jnp.int32, (owned, owned), 0)
    other = lax.broadcasted_iota(jnp.int32, (owned, owned), 1)
    loss_ref[...] = jnp.sum(jnp.where(line == other, loss, 0.0), axis=0, keepdims=True)


def swap(x, axis, bit):
    return lax.ppermute(x, axis, [(i, i ^ bit) for i in range(lax.axis_size(axis))])


def body(
    features,
    dw_kernel,
    ln_gain,
    widening_pointwise_matrix,
    w_reduce,
    layer_branch_scale,
    p_expand,
    p_kernel,
    region_ids,
    owner_slot,
    partner,
    key_embed,
):
    images, shard_rows, width, chans = features.shape
    shards = lax.axis_size("rows")
    batches = lax.axis_size("batch")
    row = lax.axis_index("rows")
    batch = lax.axis_index("batch")
    section = lax.axis_index("section")
    half = chans // lax.axis_size("section")
    parts = shards // images
    out_rows = shards * shard_rows // parts
    pixels = shard_rows * width
    out_pixels = out_rows * width
    slots = images * REG
    owned = slots // shards
    out_dim = p_kernel.shape[2]
    mib = 1 << 20
    span = half // CHUNKS

    w1, w2, pe, pk = widening_pointwise_matrix, w_reduce, p_expand, p_kernel
    first_row = (row % parts) * out_rows
    spot = jnp.stack(
        [row, first_row, jnp.int32(5), section, batch, row * owned]
    ).astype(jnp.int32)

    tail = -(-images * shard_rows // 16) * 16
    sizes = [pixels] * (CHUNKS - 1) + [pixels + tail]
    parcels = call(
        functools.partial(stage_kernel, (shards, CHUNKS, parts)),
        [jax.ShapeDtypeStruct((size, span), bf16) for size in sizes for _ in range(shards)],
        [SMEM, pl.BlockSpec(memory_space=pltpu.HBM), VMEM],
        [pltpu.VMEM((tail, span), f32), pltpu.SemaphoreType.DMA((shards * CHUNKS,))],
        62 * mib + mib // 2,
        0,
        shards * pixels * half * 4,
    )(spot, features.reshape(images, pixels, chans), region_ids)

    pieces = [key_embed]
    steps = []
    for axis, size in (("batch", batches), ("rows", shards)):
        steps += [(axis, 1 << n) for n in range(size.bit_length() - 1)]

    def after(here, *done):
        count = -(-len(steps) // 4)
        for axis, bit in (steps.pop(0) for _ in range(min(count, len(steps)))):
            whole = pieces[0] if len(pieces) == 1 else join(*pieces)
            pieces.append(swap(whole, axis, bit))
        return lax.optimization_barrier((here, pieces[-1]) + done)[:2]

    got = []
    for c in range(CHUNKS):
        blocks = parcels[c * shards : (c + 1) * shards]
        if c:
            blocks, pieces[-1] = after(blocks)
        got.append([blocks[0]] + [swap(blocks[k], "rows", k) for k in range(1, shards)])

    own, other, img = [], [], []
    for c in range(CHUNKS):
        here = spot
        if c:
            here, pieces[-1] = after(spot, *own)
        taps, image = call(
            functools.partial(conv_kernel, (shards, shard_rows, width, out_rows, c * span)),
            [
                jax.ShapeDtypeStruct((out_pixels, span), f32),
                jax.ShapeDtypeStruct((out_pixels, span), bf16),
            ],
            [SMEM] + [VMEM] * (shards + 1),
            [
                pltpu.VMEM((shards * shard_rows + 6, width + 16, LANES), f32),
                pltpu.VMEM((49, 8, LANES), f32),
            ],
            3 * mib,
            out_pixels * span * 98 * 100,
            out_pixels * span * 10,
        )(here, *got[c], dw_kernel)
        own.append(taps)
        img.append(image)
        other.append(swap(taps, "section", 1))

    hot, pick, facts = call(
        functools.partial(
            prep_kernel,
            (shards, shard_rows, width, out_pixels, images, batches, key_embed.shape[0], parts),
        ),
        [
            jax.ShapeDtypeStruct((9 * REG, out_pixels), bf16),
            jax.ShapeDtypeStruct((owned, slots), bf16),
            jax.ShapeDtypeStruct((owned, LANES), f32),
        ],
        [SMEM] + [VMEM] * (shards + 2),
        [pltpu.VMEM((16, (shards + 2) * pixels), f32)],
        2 * mib,
        10**8,
        10**6,
    )(spot, *got[-1], owner_slot, partner)

    hid = w1.shape[1]
    part_pixels = out_pixels // 2
    z, z_other = [], []
    for p in range(2):
        here, pieces[-1] = after(spot, hot, *z)
        mine, send = call(
            functools.partial(block_kernel, (p * part_pixels, part_pixels, CHUNKS)),
            [
                jax.ShapeDtypeStruct((part_pixels, chans), f32),
                jax.ShapeDtypeStruct((part_pixels, chans), bf16),
            ],
            [SMEM] + [VMEM] * (3 * CHUNKS + 4),
            [pltpu.VMEM((2, part_pixels, half), bf16), pltpu.VMEM((part_pixels, hid), bf16)],
            8 * mib,
            4 * part_pixels * hid * chans,
            4 * hid * chans,
        )(here, *own, *other, *img, ln_gain, layer_branch_scale, w1, w2)
        z.append(mine)
        z_other.append(swap(send, "section", 1))

    hidden = pe.shape[1]
    (hid_a,) = call(
        expand_kernel,
        [jax.ShapeDtypeStruct((part_pixels, hidden), bf16)],
        [VMEM] * 3,
        [pltpu.VMEM((part_pixels, chans), bf16)],
        6 * mib,
        2 * part_pixels * hidden * chans,
        2 * hidden * chans,
    )(z[0], z_other[0], pe)
    (pooled,) = call(
        project_kernel,
        [jax.ShapeDtypeStruct((REG, out_dim), f32)],
        [VMEM] * 6,
        [
            pltpu.VMEM((part_pixels, chans), bf16),
            pltpu.VMEM((hidden // 256, out_pixels, 256), bf16),
        ],
        8 * mib,
        2 * part_pixels * hidden * chans + 4 * 9 * REG * hidden * out_pixels,
        4 * hidden * chans,
    )(z[1], z_other[1], hid_a, pe, pk, hot)
    (sums,) = call(
        add_kernel,
        [jax.ShapeDtypeStruct((shards, REG, out_dim), f32)],
        [VMEM] * 2,
        [],
        mib,
        10**5,
        10**5,
    )(pooled, swap(pooled, "section", 1))
    sums = lax.all_to_all(sums, "rows", 0, 0, tiled=True)

    embed, loss = call(
        functools.partial(loss_kernel, (shards, parts)),
        [jax.ShapeDtypeStruct((owned, out_dim), f32), jax.ShapeDtypeStruct((1, owned), f32)],
        [VMEM] * (3 + len(pieces)),
        [pltpu.VMEM((slots, out_dim), f32)],
        6 * mib,
        10**8,
        10**6,
    )(sums, pick, facts, *pieces)
    return embed, loss.reshape(owned)


def solution(mesh):
    in_specs = (
        P("batch", "rows", None, None),
        P(),
        P(),
        P(None, "section"),
        P("section", None),
        P(),
        P(None, "section"),
        P(None, "section", None),
        P("batch", "rows", None),
        P("batch", None),
        P("batch", None),
        P(("batch", "rows"), None),
    )
    out_specs = (P(("batch", "rows"), None), P(("batch", "rows")))
    return jax.shard_map(body, mesh=mesh, in_specs=in_specs, out_specs=out_specs, check_vma=False)
```

```python
import functools

import jax
import jax.numpy as jnp
from jax import lax
from jax.experimental import pallas as pl
from jax.experimental.pallas import tpu as pltpu
from jax.sharding import PartitionSpec as P

REG = 64
LANES = 128
STRIP = 4
CHUNKS = 2

sharpness_divisor = 0.1
ln_eps = 1e-06
norm_eps = 1e-06

VMEM = pl.BlockSpec(memory_space=pltpu.VMEM)
SMEM = pl.BlockSpec(memory_space=pltpu.SMEM)
f32 = jnp.float32
bf16 = jnp.bfloat16


def call(kernel, outs, in_specs, scratch, limit, flops, nbytes):
    return pl.pallas_call(
        kernel,
        out_shape=outs,
        in_specs=in_specs,
        out_specs=[VMEM] * len(outs),
        scratch_shapes=scratch,
        compiler_params=pltpu.CompilerParams(vmem_limit_bytes=limit),
        cost_estimate=pl.CostEstimate(flops=flops, bytes_accessed=nbytes, transcendentals=0),
    )


def dot(a, b):
    return jnp.dot(a, b, preferred_element_type=f32)


def dot_nt(a, b):
    return lax.dot_general(a, b, (((1,), (1,)), ((), ())), preferred_element_type=f32)


def split3(x):
    hi = x.astype(bf16)
    rest = x - hi.astype(f32)
    mid = rest.astype(bf16)
    return hi, mid, (rest - mid.astype(f32)).astype(bf16)


def stage_kernel(geo, pos_ref, feat_ref, ids_ref, *refs):
    shards, chunks, parts = geo
    blocks, line = refs[: shards * chunks], refs[shards * chunks]
    row, section = pos_ref[0], pos_ref[3]
    images, pixels, chans = feat_ref.shape
    span = blocks[0].shape[1]
    for c in range(chunks):
        lanes = pl.ds(pl.multiple_of(section * (chans // 2) + c * span, LANES), span)
        for k in range(shards):
            blocks[c * shards + k][0:pixels, :] = feat_ref[(row ^ k) // parts, :, lanes]
    line[...] = jnp.full(line.shape, -1.0, f32)
    shard_rows, width = ids_ref.shape[1:]
    for i in range(images):
        line[i * shard_rows : (i + 1) * shard_rows, 0:width] = ids_ref[i].astype(f32)
    for k in range(shards):
        blocks[(chunks - 1) * shards + k][pixels:, :] = line[...].astype(bf16)


def join_kernel(*refs):
    start = 0
    for ref in refs[:-1]:
        refs[-1][start : start + ref.shape[0], :] = ref[...]
        start += ref.shape[0]


def join(*arrays):
    rows = sum(x.shape[0] for x in arrays)
    shape = jax.ShapeDtypeStruct((rows, arrays[0].shape[1]), arrays[0].dtype)
    joined = call(join_kernel, [shape], [VMEM] * len(arrays), [], 1 << 20, 0, rows * 1024)(*arrays)
    return joined[0]


def add_kernel(a_ref, b_ref, out_ref):
    out_ref[...] = a_ref[...] + b_ref[...]


def conv_kernel(geo, pos_ref, *refs):
    shards, shard_rows, width, out_rows, first_lane = geo
    blocks = refs[:shards]
    w_ref, taps, img_ref, xpad, wide = refs[shards:]
    chunk = taps.shape[1]
    row, first_row, col0 = pos_ref[0], pos_ref[1], pos_ref[2]
    base = pos_ref[3] * (w_ref.shape[2] // 2) + first_lane
    height = shards * shard_rows
    pixels = shard_rows * width
    cols = xpad.shape[1]
    out_pixels = out_rows * width
    step_rows = STRIP

    xpad[0:3] = jnp.zeros((3, cols, LANES), f32)
    xpad[height + 3 : height + 6] = jnp.zeros((3, cols, LANES), f32)
    for y in range(3, height + 3):
        xpad[y, 0:8] = jnp.zeros((8, LANES), f32)
        xpad[y, 8 + width : 16 + width] = jnp.zeros((8, LANES), f32)

    def group(g, carry):
        lanes = pl.ds(pl.multiple_of(g * LANES, LANES), LANES)
        for k in range(shards):
            value = blocks[k][0:pixels, lanes].astype(f32).reshape(shard_rows, width, LANES)
            xpad[pl.ds(3 + (row ^ k) * shard_rows, shard_rows), 8 : 8 + width, :] = value
        for dy in range(7):
            w = w_ref[dy, :, pl.ds(pl.multiple_of(base + g * LANES, LANES), LANES)].astype(f32)
            for dx in range(7):
                wide[dy * 7 + dx] = jnp.broadcast_to(w[dx : dx + 1], (8, LANES))

        def strip(i, carry):
            top = first_row + i * step_rows
            acc = [jnp.zeros((width // 8, 8, LANES), f32) for _ in range(step_rows)]
            for r in range(step_rows + 6):
                for dx in range(7):
                    v = xpad[top + r, pl.ds(col0 + dx, width), :].reshape(width // 8, 8, LANES)
                    for j in range(step_rows):
                        dy = r - j
                        if 0 <= dy < 7:
                            acc[j] = acc[j] + v * wide[dy * 7 + dx][None]
            for j in range(step_rows):
                start = pl.multiple_of((i * step_rows + j) * width, width)
                taps[pl.ds(start, width), lanes] = acc[j].reshape(width, LANES)
            return carry

        return lax.fori_loop(0, out_rows // step_rows, strip, carry)

    lax.fori_loop(0, chunk // LANES, group, 0)

    for k in range(shards):
        start = (row ^ k) * pixels - first_row * width

        @pl.when((start >= 0) & (start < out_pixels))
        def _():
            img_ref[pl.ds(pl.multiple_of(start, pixels), pixels), :] = blocks[k][0:pixels, :]


def block_kernel(geo, pos_ref, *refs):
    first, pixels, chunks = geo
    own, other, img = refs[:chunks], refs[chunks : 2 * chunks], refs[2 * chunks : 3 * chunks]
    gain_ref, scale_ref, w1_ref, w2_ref, z_ref, send_ref, normed, inner = refs[3 * chunks :]
    chans, hid = w1_ref.shape
    half = chans // 2
    width = half // chunks
    section = pos_ref[3]
    rows = slice(first, first + pixels)
    values = [ref[rows, :] for ref in own + other]
    mean = sum(jnp.sum(v, axis=1, keepdims=True) for v in values) * (1.0 / chans)
    values = [v - mean for v in values]
    spread = sum(jnp.sum(v * v, axis=1, keepdims=True) for v in values) * (1.0 / chans)
    inv = lax.rsqrt(spread + ln_eps)
    gains = gain_ref[...].astype(f32).reshape(1, chans)
    scales = scale_ref[...].astype(f32).reshape(1, chans)
    for c in range(chunks):
        lanes = slice(c * width, (c + 1) * width)
        for side, v in ((section, values[c]), (1 - section, values[chunks + c])):
            start = c * width
            gain = jnp.where(side == 0, gains[:, start : start + width], gains[:, half + start : half + start + width])
            normed[pl.ds(side, 1), :, lanes] = (v * inv * gain).astype(bf16)[None]
    step = 256
    for i in range(hid // step):
        cols = slice(i * step, (i + 1) * step)
        h = dot(normed[0], w1_ref[0:half, cols]) + dot(normed[1], w1_ref[half:chans, cols])
        inner[:, cols] = (0.5 * h * (1.0 + lax.erf(h * 0.7071067811865476))).astype(bf16)
    step = width if width % 256 else 256
    for i in range(chans // step):
        cols = slice(i * step, (i + 1) * step)
        side, start = divmod(i * step, half)
        c, start = divmod(start, width)
        keep = jnp.where(section == side, 1.0, 0.0)
        z = dot(inner[...], w2_ref[:, cols]) * scales[:, cols]
        z = z + img[c][rows, start : start + step].astype(f32) * keep
        z_ref[:, cols] = z
        send_ref[:, cols] = z.astype(bf16)


def expand_kernel(z_ref, other_ref, pe_ref, out_ref, block):
    block[...] = (z_ref[...] + other_ref[...].astype(f32)).astype(bf16)
    step = 256
    for i in range(pe_ref.shape[1] // step):
        cols = slice(i * step, (i + 1) * step)
        out_ref[:, cols] = jnp.maximum(dot(block[...], pe_ref[:, cols]), 0.0).astype(bf16)


def prep_kernel(geo, pos_ref, *refs):
    shards, shard_rows, width, out_pixels, images, batches, per_key, parts = geo
    ids = refs[:shards]
    owner_ref, partner_ref, hot_ref, pick_ref, own_ref, flat = refs[shards:]
    row, first_row, batch, first_slot = pos_ref[0], pos_ref[1], pos_ref[4], pos_ref[5]
    pixels = shard_rows * width
    ids = [ref[pixels:, 0:LANES].astype(f32) for ref in ids]
    owned = own_ref.shape[0]
    slots = images * REG
    image = row // parts
    flat[...] = jnp.full(flat.shape, -1.0, f32)
    for k in range(shards):
        start = pl.multiple_of((1 + (row ^ k)) * pixels, LANES)
        number = lax.broadcasted_iota(jnp.int32, ids[k].shape, 0)
        inside = lax.broadcasted_iota(jnp.int32, ids[k].shape, 1) < width
        for y in range(shard_rows):
            keep = inside & (number == image * shard_rows + y)
            mine = jnp.sum(jnp.where(keep, ids[k], 0.0), axis=0, keepdims=True)
            mine = jnp.broadcast_to(mine, (8, LANES))
            mine = pltpu.roll(mine, y * width, 1) if y else mine
            line = mine if y == 0 else line + mine
        flat[0:8, pl.ds(start, pixels)] = line
    total = flat.shape[1]
    whole = jnp.broadcast_to(flat[0:1, :], (8, total))
    lane = lax.broadcasted_iota(jnp.int32, (8, total), 1)
    col = lane % width
    region = lax.broadcasted_iota(jnp.int32, (REG, out_pixels), 0).astype(f32)
    start = pl.multiple_of(pixels + first_row * width, LANES)
    for dy in range(3):
        for dx in range(3):
            off = (dy - 1) * width + dx - 1
            moved = whole if off == 0 else pltpu.roll(whole, off % total, 1)
            if dx == 0:
                moved = jnp.where(col == width - 1, -1.0, moved)
            if dx == 2:
                moved = jnp.where(col == 0, -1.0, moved)
            flat[8:16, :] = moved
            line = flat[8:9, pl.ds(start, out_pixels)]
            tap = dy * 3 + dx
            hot_ref[tap * REG : (tap + 1) * REG, :] = jnp.where(region == line, 1.0, 0.0).astype(bf16)
    slot = lax.broadcasted_iota(jnp.int32, (owned, slots), 1)
    want = lax.broadcasted_iota(jnp.int32, (owned, slots), 0) + first_slot
    pick = owner_ref[...] == want
    pick_ref[...] = jnp.where(pick, 1.0, 0.0).astype(bf16)
    one_region = lax.broadcasted_iota(jnp.int32, (REG, LANES), 0).astype(f32)
    tallies = []
    for i in range(images):
        tally = jnp.zeros((REG, LANES), f32)
        for k in range(shards):
            for y in range(i * shard_rows, (i + 1) * shard_rows):
                tally = tally + jnp.where(one_region == ids[k][y : y + 1, :], 1.0, 0.0)
        tallies.append(tally)
    tally = jnp.concatenate(tallies, axis=0).astype(bf16)
    count = dot_nt(jnp.ones((8, LANES), bf16), tally)[0:1]
    mates = jnp.concatenate([partner_ref[i : i + 1, :] for i in range(images)], axis=1)
    mate = (batch * images + slot // REG) * REG + mates
    block = mate // per_key
    place = ((block % shards) ^ row) * batches + ((block // shards) ^ batch)
    place = place * per_key + mate % per_key
    place = jnp.sum(jnp.where(pick, place, 0).astype(f32), axis=1, keepdims=True)
    number = jnp.sum(jnp.where(pick, count, 0.0), axis=1, keepdims=True)
    side = lax.broadcasted_iota(jnp.int32, (owned, LANES), 1)
    own_ref[...] = jnp.where(side == 0, place, jnp.where(side == 1, number, 0.0))


def project_kernel(z_ref, other_ref, first_ref, pe_ref, pk_ref, hot_ref, out_ref, block, hidden):
    before = first_ref.shape[0]
    pixels = z_ref.shape[0]
    taps = pk_ref.shape[0]
    block[...] = (z_ref[...] + other_ref[...].astype(f32)).astype(bf16)
    step = 256
    acc = jnp.zeros((2 * REG, out_ref.shape[1]), f32)
    for i in range(pe_ref.shape[1] // step):
        cols = slice(i * step, (i + 1) * step)
        hidden[i, 0:before, :] = first_ref[:, cols]
        h = jnp.maximum(dot(block[...], pe_ref[:, cols]), 0.0)
        hidden[i, before : before + pixels, :] = h.astype(bf16)
        sums = dot(hot_ref[...], hidden[i])
        hi = sums.astype(bf16)
        lo = (sums - hi.astype(f32)).astype(bf16)
        for t in range(taps):
            rows = slice(t * REG, (t + 1) * REG)
            both = jnp.concatenate([hi[rows], lo[rows]], axis=0)
            acc = acc + dot(both, pk_ref[t, cols, :])
    out_ref[...] = acc[0:REG] + acc[REG:]


def loss_kernel(geo, *refs):
    shards, parts = geo
    sums, row = refs[1 : shards + 1], refs[0][0]
    pick_ref, own_ref = refs[shards + 1 : shards + 3]
    embed_ref, loss_ref, table = refs[-3:]
    if parts > 1:
        table[...] = jnp.zeros(table.shape, f32)
    for k in range(shards):
        place = pl.ds(pl.multiple_of(((row ^ k) // parts) * REG, REG), REG)
        value = sums[k][...]
        table[place, :] = value if parts == 1 else table[place, :] + value
    pick = pick_ref[...]
    hi, mid, lo = split3(table[...])
    ordered = dot(pick, hi) + dot(pick, mid) + dot(pick, lo)
    unit = ordered * lax.rsqrt(jnp.sum(ordered * ordered, axis=1, keepdims=True) + norm_eps)
    embed_ref[...] = unit
    owned = unit.shape[0]
    keys = jnp.concatenate([ref[...] for ref in refs[shards + 3 : -3]], axis=0)
    wide = keys.astype(f32)
    square = wide * wide
    square_hi = square.astype(bf16)
    square_lo = (square - square_hi.astype(f32)).astype(bf16)
    ones = jnp.ones((16, keys.shape[1]), bf16)
    length = dot_nt(ones, square_hi)[0:1] + dot_nt(ones, square_lo)[0:1]
    three = dot_nt(jnp.concatenate(split3(unit), axis=0), keys)
    logits = three[0:owned] + three[owned : 2 * owned] + three[2 * owned :]
    logits = logits * (lax.rsqrt(length + norm_eps) / sharpness_divisor)
    total = jnp.log(jnp.sum(jnp.exp(logits), axis=1, keepdims=True))
    column = lax.broadcasted_iota(jnp.int32, logits.shape, 1).astype(f32)
    match = jnp.sum(jnp.where(column == own_ref[:, 0:1], logits, 0.0), axis=1, keepdims=True)
    loss = jnp.where(own_ref[:, 1:2] > 0.5, total - match, 0.0)
    line = lax.broadcasted_iota(jnp.int32, (owned, owned), 0)
    other = lax.broadcasted_iota(jnp.int32, (owned, owned), 1)
    loss_ref[...] = jnp.sum(jnp.where(line == other, loss, 0.0), axis=0, keepdims=True)


def swap(x, axis, bit):
    return lax.ppermute(x, axis, [(i, i ^ bit) for i in range(lax.axis_size(axis))])


def body(
    features,
    dw_kernel,
    ln_gain,
    widening_pointwise_matrix,
    w_reduce,
    layer_branch_scale,
    p_expand,
    p_kernel,
    region_ids,
    owner_slot,
    partner,
    key_embed,
):
    images, shard_rows, width, chans = features.shape
    shards = lax.axis_size("rows")
    batches = lax.axis_size("batch")
    row = lax.axis_index("rows")
    batch = lax.axis_index("batch")
    section = lax.axis_index("section")
    half = chans // lax.axis_size("section")
    parts = shards // images
    out_rows = shards * shard_rows // parts
    pixels = shard_rows * width
    out_pixels = out_rows * width
    slots = images * REG
    owned = slots // shards
    out_dim = p_kernel.shape[2]
    mib = 1 << 20
    span = half // CHUNKS

    w1, w2, pe, pk = widening_pointwise_matrix, w_reduce, p_expand, p_kernel
    first_row = (row % parts) * out_rows
    spot = jnp.stack(
        [row, first_row, jnp.int32(5), section, batch, row * owned]
    ).astype(jnp.int32)

    tail = -(-images * shard_rows // 16) * 16
    sizes = [pixels] * (CHUNKS - 1) + [pixels + tail]
    parcels = call(
        functools.partial(stage_kernel, (shards, CHUNKS, parts)),
        [jax.ShapeDtypeStruct((size, span), bf16) for size in sizes for _ in range(shards)],
        [SMEM, VMEM, VMEM],
        [pltpu.VMEM((tail, span), f32)],
        mib,
        0,
        shards * pixels * half * 4,
    )(spot, features.reshape(images, pixels, chans), region_ids)

    pieces = [key_embed]
    steps = []
    for axis, size in (("batch", batches), ("rows", shards)):
        steps += [(axis, 1 << n) for n in range(size.bit_length() - 1)]
    share = -(-len(steps) // 4)

    def key_step():
        for axis, bit in (steps.pop(0) for _ in range(min(share, len(steps)))):
            whole = pieces[0] if len(pieces) == 1 else join(*pieces)
            pieces.append(swap(whole, axis, bit))

    def after(here, *done):
        return lax.optimization_barrier((here, *done))[0]

    got = []
    for c in range(CHUNKS):
        blocks = parcels[c * shards : (c + 1) * shards]
        got.append([blocks[0]] + [swap(blocks[k], "rows", k) for k in range(1, shards)])
    key_step()

    own, other, img = [], [], []
    for c in range(CHUNKS):
        here = after(spot, pieces[-1], *own) if c else spot
        taps, image = call(
            functools.partial(conv_kernel, (shards, shard_rows, width, out_rows, c * span)),
            [
                jax.ShapeDtypeStruct((out_pixels, span), f32),
                jax.ShapeDtypeStruct((out_pixels, span), bf16),
            ],
            [SMEM] + [VMEM] * (shards + 1),
            [
                pltpu.VMEM((shards * shard_rows + 6, width + 16, LANES), f32),
                pltpu.VMEM((49, 8, LANES), f32),
            ],
            3 * mib,
            out_pixels * span * 98 * 100,
            out_pixels * span * 10,
        )(here, *got[c], dw_kernel)
        own.append(taps)
        img.append(image)
        other.append(swap(taps, "section", 1))

    hot, pick, facts = call(
        functools.partial(
            prep_kernel,
            (shards, shard_rows, width, out_pixels, images, batches, key_embed.shape[0], parts),
        ),
        [
            jax.ShapeDtypeStruct((9 * REG, out_pixels), bf16),
            jax.ShapeDtypeStruct((owned, slots), bf16),
            jax.ShapeDtypeStruct((owned, LANES), f32),
        ],
        [SMEM] + [VMEM] * (shards + 2),
        [pltpu.VMEM((16, (shards + 2) * pixels), f32)],
        2 * mib,
        10**8,
        10**6,
    )(spot, *got[-1], owner_slot, partner)

    pieces[-1] = after(pieces[-1], *own)
    key_step()

    hid = w1.shape[1]
    part_pixels = out_pixels // 2
    z, z_other = [], []
    for p in range(2):
        here = after(spot, hot, pieces[-1], *z) if p else after(spot, hot)
        if p:
            key_step()
        mine, send = call(
            functools.partial(block_kernel, (p * part_pixels, part_pixels, CHUNKS)),
            [
                jax.ShapeDtypeStruct((part_pixels, chans), f32),
                jax.ShapeDtypeStruct((part_pixels, chans), bf16),
            ],
            [SMEM] + [VMEM] * (3 * CHUNKS + 4),
            [pltpu.VMEM((2, part_pixels, half), bf16), pltpu.VMEM((part_pixels, hid), bf16)],
            8 * mib,
            4 * part_pixels * hid * chans,
            4 * hid * chans,
        )(here, *own, *other, *img, ln_gain, layer_branch_scale, w1, w2)
        z.append(mine)
        z_other.append(swap(send, "section", 1))
    z[0] = after(z[0], pieces[-1])
    pieces[-1] = after(pieces[-1], z[1])
    key_step()

    hidden = pe.shape[1]
    (hid_a,) = call(
        expand_kernel,
        [jax.ShapeDtypeStruct((part_pixels, hidden), bf16)],
        [VMEM] * 3,
        [pltpu.VMEM((part_pixels, chans), bf16)],
        6 * mib,
        2 * part_pixels * hidden * chans,
        2 * hidden * chans,
    )(z[0], z_other[0], pe)
    (pooled,) = call(
        project_kernel,
        [jax.ShapeDtypeStruct((REG, out_dim), f32)],
        [VMEM] * 6,
        [
            pltpu.VMEM((part_pixels, chans), bf16),
            pltpu.VMEM((hidden // 256, out_pixels, 256), bf16),
        ],
        8 * mib,
        2 * part_pixels * hidden * chans + 4 * 9 * REG * hidden * out_pixels,
        4 * hidden * chans,
    )(z[1], z_other[1], hid_a, pe, pk, hot)
    (pooled,) = call(
        add_kernel,
        [jax.ShapeDtypeStruct((REG, out_dim), f32)],
        [VMEM] * 2,
        [],
        mib,
        10**5,
        10**5,
    )(pooled, swap(pooled, "section", 1))
    sums = [pooled] + [swap(pooled, "rows", k) for k in range(1, shards)]

    embed, loss = call(
        functools.partial(loss_kernel, (shards, parts)),
        [jax.ShapeDtypeStruct((owned, out_dim), f32), jax.ShapeDtypeStruct((1, owned), f32)],
        [SMEM] + [VMEM] * (shards + 2 + len(pieces)),
        [pltpu.VMEM((slots, out_dim), f32)],
        6 * mib,
        10**8,
        10**6,
    )(spot, *sums, pick, facts, *pieces)
    return embed, loss.reshape(owned)


def solution(mesh):
    in_specs = (
        P("batch", "rows", None, None),
        P(),
        P(),
        P(None, "section"),
        P("section", None),
        P(),
        P(None, "section"),
        P(None, "section", None),
        P("batch", "rows", None),
        P("batch", None),
        P("batch", None),
        P(("batch", "rows"), None),
    )
    out_specs = (P(("batch", "rows"), None), P(("batch", "rows")))
    return jax.shard_map(body, mesh=mesh, in_specs=in_specs, out_specs=out_specs, check_vma=False)
```

```python
import functools

import jax
import jax.numpy as jnp
from jax import lax
from jax.experimental import pallas as pl
from jax.experimental.pallas import tpu as pltpu
from jax.sharding import PartitionSpec as P

REG = 64
LANES = 128
STRIP = 4
CHUNKS = 2

sharpness_divisor = 0.1
ln_eps = 1e-06
norm_eps = 1e-06

VMEM = pl.BlockSpec(memory_space=pltpu.VMEM)
SMEM = pl.BlockSpec(memory_space=pltpu.SMEM)
f32 = jnp.float32
bf16 = jnp.bfloat16


def call(kernel, outs, in_specs, scratch, limit, flops, nbytes):
    return pl.pallas_call(
        kernel,
        out_shape=outs,
        in_specs=in_specs,
        out_specs=[VMEM] * len(outs),
        scratch_shapes=scratch,
        compiler_params=pltpu.CompilerParams(vmem_limit_bytes=limit),
        cost_estimate=pl.CostEstimate(flops=flops, bytes_accessed=nbytes, transcendentals=0),
    )


def dot(a, b):
    return jnp.dot(a, b, preferred_element_type=f32)


def dot_nt(a, b):
    return lax.dot_general(a, b, (((1,), (1,)), ((), ())), preferred_element_type=f32)


def split3(x):
    hi = x.astype(bf16)
    rest = x - hi.astype(f32)
    mid = rest.astype(bf16)
    return hi, mid, (rest - mid.astype(f32)).astype(bf16)


def pack_kernel(count, pos_ref, ids_ref, key_ref, dw_ref, *refs):
    inputs, blocks = refs[:count], refs[count : 2 * count]
    w_ref, line = refs[2 * count :]
    pixels = inputs[0].shape[0]
    keys, depth = key_ref.shape
    shard_rows, width = ids_ref.shape[1:]
    line[...] = jnp.full(line.shape, -1.0, f32)
    for i in range(ids_ref.shape[0]):
        line[i * shard_rows : (i + 1) * shard_rows, 0:width] = ids_ref[i].astype(f32)
    tail = line[...].astype(bf16)
    for source, block in zip(inputs, blocks):
        block[0:pixels, :] = source[...]
        block[pixels : pixels + keys, 0:depth] = key_ref[...]
        block[pixels:, depth : depth + LANES] = tail
    half = w_ref.shape[1]
    lanes = pl.ds(pl.multiple_of(pos_ref[3] * half, LANES), half)
    for dy in range(7):
        w_ref[dy * 7 : dy * 7 + 7, :] = dw_ref[dy, :, lanes].astype(f32)


def join_kernel(*refs):
    start = 0
    for ref in refs[:-1]:
        refs[-1][start : start + ref.shape[0], :] = ref[...]
        start += ref.shape[0]


def join(*arrays):
    rows = sum(x.shape[0] for x in arrays)
    shape = jax.ShapeDtypeStruct((rows, arrays[0].shape[1]), arrays[0].dtype)
    joined = call(join_kernel, [shape], [VMEM] * len(arrays), [], 1 << 20, 0, rows * 1024)(*arrays)
    return joined[0]


def add_kernel(a_ref, b_ref, out_ref):
    out_ref[...] = a_ref[...] + b_ref[...]


def conv_kernel(geo, pos_ref, *refs):
    shards, shard_rows, width, out_rows, first_lane = geo
    blocks = refs[:shards]
    w_ref, taps, img_ref, xpad, wide = refs[shards:]
    chunk = taps.shape[1]
    row, first_row, col0 = pos_ref[0], pos_ref[1], pos_ref[2]
    height = shards * shard_rows
    pixels = shard_rows * width
    cols = xpad.shape[1]
    out_pixels = out_rows * width
    step_rows = STRIP

    xpad[0:3] = jnp.zeros((3, cols, LANES), f32)
    xpad[height + 3 : height + 6] = jnp.zeros((3, cols, LANES), f32)
    for y in range(3, height + 3):
        xpad[y, 0:8] = jnp.zeros((8, LANES), f32)
        xpad[y, 8 + width : 16 + width] = jnp.zeros((8, LANES), f32)

    def group(g, carry):
        lanes = pl.ds(pl.multiple_of(g * LANES, LANES), LANES)
        for k in range(shards):
            value = blocks[k][0:pixels, lanes].astype(f32).reshape(shard_rows, width, LANES)
            xpad[pl.ds(3 + (row ^ k) * shard_rows, shard_rows), 8 : 8 + width, :] = value
        for t in range(49):
            w = w_ref[t : t + 1, pl.ds(pl.multiple_of(first_lane + g * LANES, LANES), LANES)]
            wide[t] = jnp.broadcast_to(w, (8, LANES))

        def strip(i, carry):
            top = first_row + i * step_rows
            acc = [jnp.zeros((width // 8, 8, LANES), f32) for _ in range(step_rows)]
            for r in range(step_rows + 6):
                for dx in range(7):
                    v = xpad[top + r, pl.ds(col0 + dx, width), :].reshape(width // 8, 8, LANES)
                    for j in range(step_rows):
                        dy = r - j
                        if 0 <= dy < 7:
                            acc[j] = acc[j] + v * wide[dy * 7 + dx][None]
            for j in range(step_rows):
                start = pl.multiple_of((i * step_rows + j) * width, width)
                taps[pl.ds(start, width), lanes] = acc[j].reshape(width, LANES)
            return carry

        return lax.fori_loop(0, out_rows // step_rows, strip, carry)

    lax.fori_loop(0, chunk // LANES, group, 0)

    for k in range(shards):
        start = (row ^ k) * pixels - first_row * width

        @pl.when((start >= 0) & (start < out_pixels))
        def _():
            img_ref[pl.ds(pl.multiple_of(start, pixels), pixels), :] = blocks[k][0:pixels, :]


def block_kernel(geo, pos_ref, *refs):
    first, pixels, chunks = geo
    own, other, img = refs[:chunks], refs[chunks : 2 * chunks], refs[2 * chunks : 3 * chunks]
    gain_ref, scale_ref, w1_ref, w2_ref, z_ref, send_ref, normed, inner = refs[3 * chunks :]
    chans, hid = w1_ref.shape
    half = chans // 2
    width = half // chunks
    section = pos_ref[3]
    rows = slice(first, first + pixels)
    values = [ref[rows, :] for ref in own + other]
    mean = sum(jnp.sum(v, axis=1, keepdims=True) for v in values) * (1.0 / chans)
    values = [v - mean for v in values]
    spread = sum(jnp.sum(v * v, axis=1, keepdims=True) for v in values) * (1.0 / chans)
    inv = lax.rsqrt(spread + ln_eps)
    gains = gain_ref[...].astype(f32).reshape(1, chans)
    scales = scale_ref[...].astype(f32).reshape(1, chans)
    for c in range(chunks):
        lanes = slice(c * width, (c + 1) * width)
        for side, v in ((section, values[c]), (1 - section, values[chunks + c])):
            start = c * width
            gain = jnp.where(side == 0, gains[:, start : start + width], gains[:, half + start : half + start + width])
            normed[pl.ds(side, 1), :, lanes] = (v * inv * gain).astype(bf16)[None]
    step = 256
    for i in range(hid // step):
        cols = slice(i * step, (i + 1) * step)
        h = dot(normed[0], w1_ref[0:half, cols]) + dot(normed[1], w1_ref[half:chans, cols])
        inner[:, cols] = (0.5 * h * (1.0 + lax.erf(h * 0.7071067811865476))).astype(bf16)
    step = width if width % 256 else 256
    for i in range(chans // step):
        cols = slice(i * step, (i + 1) * step)
        side, start = divmod(i * step, half)
        c, start = divmod(start, width)
        keep = jnp.where(section == side, 1.0, 0.0)
        z = dot(inner[...], w2_ref[:, cols]) * scales[:, cols]
        z = z + img[c][rows, start : start + step].astype(f32) * keep
        z_ref[:, cols] = z
        send_ref[:, cols] = z.astype(bf16)


def expand_kernel(z_ref, other_ref, pe_ref, out_ref, block):
    block[...] = (z_ref[...] + other_ref[...].astype(f32)).astype(bf16)
    step = 256
    for i in range(pe_ref.shape[1] // step):
        cols = slice(i * step, (i + 1) * step)
        out_ref[:, cols] = jnp.maximum(dot(block[...], pe_ref[:, cols]), 0.0).astype(bf16)


def prep_kernel(geo, pos_ref, *refs):
    shards, shard_rows, width, out_pixels, images, per_key, parts = geo
    ids = refs[:shards]
    owner_ref, partner_ref, hot_ref, pick_ref, own_ref, keys_ref, flat = refs[shards:]
    row, first_row, batch, first_slot = pos_ref[0], pos_ref[1], pos_ref[4], pos_ref[5]
    pixels = shard_rows * width
    depth = keys_ref.shape[1]
    for k in range(shards):
        keys_ref[k * per_key : (k + 1) * per_key, :] = ids[k][pixels : pixels + per_key, 0:depth]
    ids = [ref[pixels:, depth : depth + LANES].astype(f32) for ref in ids]
    owned = own_ref.shape[0]
    slots = images * REG
    image = row // parts
    flat[...] = jnp.full(flat.shape, -1.0, f32)
    for k in range(shards):
        start = pl.multiple_of((1 + (row ^ k)) * pixels, LANES)
        number = lax.broadcasted_iota(jnp.int32, ids[k].shape, 0)
        inside = lax.broadcasted_iota(jnp.int32, ids[k].shape, 1) < width
        for y in range(shard_rows):
            keep = inside & (number == image * shard_rows + y)
            mine = jnp.sum(jnp.where(keep, ids[k], 0.0), axis=0, keepdims=True)
            mine = jnp.broadcast_to(mine, (8, LANES))
            mine = pltpu.roll(mine, y * width, 1) if y else mine
            line = mine if y == 0 else line + mine
        flat[0:8, pl.ds(start, pixels)] = line
    total = flat.shape[1]
    whole = jnp.broadcast_to(flat[0:1, :], (8, total))
    lane = lax.broadcasted_iota(jnp.int32, (8, total), 1)
    col = lane % width
    region = lax.broadcasted_iota(jnp.int32, (REG, out_pixels), 0).astype(f32)
    start = pl.multiple_of(pixels + first_row * width, LANES)
    for dy in range(3):
        for dx in range(3):
            off = (dy - 1) * width + dx - 1
            moved = whole if off == 0 else pltpu.roll(whole, off % total, 1)
            if dx == 0:
                moved = jnp.where(col == width - 1, -1.0, moved)
            if dx == 2:
                moved = jnp.where(col == 0, -1.0, moved)
            flat[8:16, :] = moved
            line = flat[8:9, pl.ds(start, out_pixels)]
            tap = dy * 3 + dx
            hot_ref[tap * REG : (tap + 1) * REG, :] = jnp.where(region == line, 1.0, 0.0).astype(bf16)
    slot = lax.broadcasted_iota(jnp.int32, (owned, slots), 1)
    want = lax.broadcasted_iota(jnp.int32, (owned, slots), 0) + first_slot
    pick = owner_ref[...] == want
    pick_ref[...] = jnp.where(pick, 1.0, 0.0).astype(bf16)
    one_region = lax.broadcasted_iota(jnp.int32, (REG, LANES), 0).astype(f32)
    tallies = []
    for i in range(images):
        tally = jnp.zeros((REG, LANES), f32)
        for k in range(shards):
            for y in range(i * shard_rows, (i + 1) * shard_rows):
                tally = tally + jnp.where(one_region == ids[k][y : y + 1, :], 1.0, 0.0)
        tallies.append(tally)
    tally = jnp.concatenate(tallies, axis=0).astype(bf16)
    count = dot_nt(jnp.ones((8, LANES), bf16), tally)[0:1]
    mates = jnp.concatenate([partner_ref[i : i + 1, :] for i in range(images)], axis=1)
    mate = (batch * images + slot // REG) * REG + mates
    block = mate // per_key
    place = ((block // shards) ^ batch) * shards + ((block % shards) ^ row)
    place = place * per_key + mate % per_key
    place = jnp.sum(jnp.where(pick, place, 0).astype(f32), axis=1, keepdims=True)
    number = jnp.sum(jnp.where(pick, count, 0.0), axis=1, keepdims=True)
    side = lax.broadcasted_iota(jnp.int32, (owned, LANES), 1)
    own_ref[...] = jnp.where(side == 0, place, jnp.where(side == 1, number, 0.0))


def project_kernel(z_ref, other_ref, first_ref, pe_ref, pk_ref, hot_ref, out_ref, block, hidden):
    before = first_ref.shape[0]
    pixels = z_ref.shape[0]
    taps = pk_ref.shape[0]
    block[...] = (z_ref[...] + other_ref[...].astype(f32)).astype(bf16)
    step = 256
    acc = jnp.zeros((2 * REG, out_ref.shape[1]), f32)
    for i in range(pe_ref.shape[1] // step):
        cols = slice(i * step, (i + 1) * step)
        hidden[i, 0:before, :] = first_ref[:, cols]
        h = jnp.maximum(dot(block[...], pe_ref[:, cols]), 0.0)
        hidden[i, before : before + pixels, :] = h.astype(bf16)
        sums = dot(hot_ref[...], hidden[i])
        hi = sums.astype(bf16)
        lo = (sums - hi.astype(f32)).astype(bf16)
        for t in range(taps):
            rows = slice(t * REG, (t + 1) * REG)
            both = jnp.concatenate([hi[rows], lo[rows]], axis=0)
            acc = acc + dot(both, pk_ref[t, cols, :])
    out_ref[...] = acc[0:REG] + acc[REG:]


def loss_kernel(geo, *refs):
    shards, parts = geo
    sums, row = refs[1 : shards + 1], refs[0][0]
    pick_ref, own_ref = refs[shards + 1 : shards + 3]
    embed_ref, loss_ref, table = refs[-3:]
    if parts > 1:
        table[...] = jnp.zeros(table.shape, f32)
    for k in range(shards):
        place = pl.ds(pl.multiple_of(((row ^ k) // parts) * REG, REG), REG)
        value = sums[k][...]
        table[place, :] = value if parts == 1 else table[place, :] + value
    pick = pick_ref[...]
    hi, mid, lo = split3(table[...])
    ordered = dot(pick, hi) + dot(pick, mid) + dot(pick, lo)
    unit = ordered * lax.rsqrt(jnp.sum(ordered * ordered, axis=1, keepdims=True) + norm_eps)
    embed_ref[...] = unit
    owned = unit.shape[0]
    keys = jnp.concatenate([ref[...] for ref in refs[shards + 3 : -3]], axis=0)
    wide = keys.astype(f32)
    square = wide * wide
    square_hi = square.astype(bf16)
    square_lo = (square - square_hi.astype(f32)).astype(bf16)
    ones = jnp.ones((16, keys.shape[1]), bf16)
    length = dot_nt(ones, square_hi)[0:1] + dot_nt(ones, square_lo)[0:1]
    three = dot_nt(jnp.concatenate(split3(unit), axis=0), keys)
    logits = three[0:owned] + three[owned : 2 * owned] + three[2 * owned :]
    logits = logits * (lax.rsqrt(length + norm_eps) / sharpness_divisor)
    total = jnp.log(jnp.sum(jnp.exp(logits), axis=1, keepdims=True))
    column = lax.broadcasted_iota(jnp.int32, logits.shape, 1).astype(f32)
    match = jnp.sum(jnp.where(column == own_ref[:, 0:1], logits, 0.0), axis=1, keepdims=True)
    loss = jnp.where(own_ref[:, 1:2] > 0.5, total - match, 0.0)
    line = lax.broadcasted_iota(jnp.int32, (owned, owned), 0)
    other = lax.broadcasted_iota(jnp.int32, (owned, owned), 1)
    loss_ref[...] = jnp.sum(jnp.where(line == other, loss, 0.0), axis=0, keepdims=True)


def swap(x, axis, bit):
    return lax.ppermute(x, axis, [(i, i ^ bit) for i in range(lax.axis_size(axis))])


def body(
    features,
    dw_kernel,
    ln_gain,
    widening_pointwise_matrix,
    w_reduce,
    layer_branch_scale,
    p_expand,
    p_kernel,
    region_ids,
    owner_slot,
    partner,
    key_embed,
):
    images, shard_rows, width, chans = features.shape
    shards = lax.axis_size("rows")
    batches = lax.axis_size("batch")
    row = lax.axis_index("rows")
    batch = lax.axis_index("batch")
    section = lax.axis_index("section")
    half = chans // lax.axis_size("section")
    parts = shards // images
    out_rows = shards * shard_rows // parts
    pixels = shard_rows * width
    out_pixels = out_rows * width
    slots = images * REG
    owned = slots // shards
    out_dim = p_kernel.shape[2]
    mib = 1 << 20
    span = half // CHUNKS

    w1, w2, pe, pk = widening_pointwise_matrix, w_reduce, p_expand, p_kernel
    first_row = (row % parts) * out_rows
    spot = jnp.stack(
        [row, first_row, jnp.int32(5), section, batch, row * owned]
    ).astype(jnp.int32)

    per_key, depth = key_embed.shape
    tail = max(-(-images * shard_rows // 16) * 16, per_key)
    def after(here, *done):
        return lax.optimization_barrier((here, *done))[0]

    parcels = []
    for c in range(CHUNKS):
        blocks = []
        for k in range(shards):
            place = ((row ^ k) // parts, 0, 0, section * half + c * span)
            part = lax.dynamic_slice(features, place, (1, shard_rows, width, span))
            blocks.append(part.reshape(pixels, span))
        parcels.append(blocks)
    *parcels[-1], weights = call(
        functools.partial(pack_kernel, shards),
        [jax.ShapeDtypeStruct((pixels + tail, span), bf16)] * shards
        + [jax.ShapeDtypeStruct((49, half), f32)],
        [SMEM] + [VMEM] * (3 + shards),
        [pltpu.VMEM((tail, LANES), f32)],
        mib,
        0,
        10**6,
    )(spot, region_ids, key_embed, dw_kernel, *parcels[-1])
    got = []
    for blocks in parcels:
        got.append([blocks[0]] + [swap(blocks[k], "rows", k) for k in range(1, shards)])

    own, other, img = [], [], []
    for c in range(CHUNKS):
        here = after(spot, *own) if c else spot
        taps, image = call(
            functools.partial(conv_kernel, (shards, shard_rows, width, out_rows, c * span)),
            [
                jax.ShapeDtypeStruct((out_pixels, span), f32),
                jax.ShapeDtypeStruct((out_pixels, span), bf16),
            ],
            [SMEM] + [VMEM] * (shards + 1),
            [
                pltpu.VMEM((shards * shard_rows + 6, width + 16, LANES), f32),
                pltpu.VMEM((49, 8, LANES), f32),
            ],
            3 * mib,
            out_pixels * span * 98 * 100,
            out_pixels * span * 10,
        )(here, *got[c], weights)
        own.append(taps)
        img.append(image)
        other.append(swap(taps, "section", 1))

    hot, pick, facts, keys = call(
        functools.partial(
            prep_kernel,
            (shards, shard_rows, width, out_pixels, images, per_key, parts),
        ),
        [
            jax.ShapeDtypeStruct((9 * REG, out_pixels), bf16),
            jax.ShapeDtypeStruct((owned, slots), bf16),
            jax.ShapeDtypeStruct((owned, LANES), f32),
            jax.ShapeDtypeStruct((shards * per_key, depth), bf16),
        ],
        [SMEM] + [VMEM] * (shards + 2),
        [pltpu.VMEM((16, (shards + 2) * pixels), f32)],
        2 * mib,
        10**8,
        10**6,
    )(after(spot, *own), *got[-1], owner_slot, partner)
    pieces = [keys, swap(keys, "batch", 1)]

    hid = w1.shape[1]
    part_pixels = out_pixels // 2
    z, z_other = [], []
    for p in range(2):
        here = after(spot, pieces[-1], *z) if p else after(spot, hot)
        mine, send = call(
            functools.partial(block_kernel, (p * part_pixels, part_pixels, CHUNKS)),
            [
                jax.ShapeDtypeStruct((part_pixels, chans), f32),
                jax.ShapeDtypeStruct((part_pixels, chans), bf16),
            ],
            [SMEM] + [VMEM] * (3 * CHUNKS + 4),
            [pltpu.VMEM((2, part_pixels, half), bf16), pltpu.VMEM((part_pixels, hid), bf16)],
            8 * mib,
            4 * part_pixels * hid * chans,
            4 * hid * chans,
        )(here, *own, *other, *img, ln_gain, layer_branch_scale, w1, w2)
        z.append(mine)
        z_other.append(swap(send, "section", 1))
    bit = 2
    while bit < batches:
        pieces.append(swap(join(*pieces), "batch", bit))
        bit *= 2

    hidden = pe.shape[1]
    (hid_a,) = call(
        expand_kernel,
        [jax.ShapeDtypeStruct((part_pixels, hidden), bf16)],
        [VMEM] * 3,
        [pltpu.VMEM((part_pixels, chans), bf16)],
        6 * mib,
        2 * part_pixels * hidden * chans,
        2 * hidden * chans,
    )(z[0], z_other[0], pe)
    (pooled,) = call(
        project_kernel,
        [jax.ShapeDtypeStruct((REG, out_dim), f32)],
        [VMEM] * 6,
        [
            pltpu.VMEM((part_pixels, chans), bf16),
            pltpu.VMEM((hidden // 256, out_pixels, 256), bf16),
        ],
        8 * mib,
        2 * part_pixels * hidden * chans + 4 * 9 * REG * hidden * out_pixels,
        4 * hidden * chans,
    )(z[1], z_other[1], hid_a, pe, pk, hot)
    (pooled,) = call(
        add_kernel,
        [jax.ShapeDtypeStruct((REG, out_dim), f32)],
        [VMEM] * 2,
        [],
        mib,
        10**5,
        10**5,
    )(pooled, swap(pooled, "section", 1))
    sums = [pooled] + [swap(pooled, "rows", k) for k in range(1, shards)]

    embed, loss = call(
        functools.partial(loss_kernel, (shards, parts)),
        [jax.ShapeDtypeStruct((owned, out_dim), f32), jax.ShapeDtypeStruct((1, owned), f32)],
        [SMEM] + [VMEM] * (shards + 2 + len(pieces)),
        [pltpu.VMEM((slots, out_dim), f32)],
        6 * mib,
        10**8,
        10**6,
    )(spot, *sums, pick, facts, *pieces)
    return embed, loss.reshape(owned)


def solution(mesh):
    in_specs = (
        P("batch", "rows", None, None),
        P(),
        P(),
        P(None, "section"),
        P("section", None),
        P(),
        P(None, "section"),
        P(None, "section", None),
        P("batch", "rows", None),
        P("batch", None),
        P("batch", None),
        P(("batch", "rows"), None),
    )
    out_specs = (P(("batch", "rows"), None), P(("batch", "rows")))
    return jax.shard_map(body, mesh=mesh, in_specs=in_specs, out_specs=out_specs, check_vma=False)
```

```python
import functools

import jax
import jax.numpy as jnp
from jax import lax
from jax.experimental import pallas as pl
from jax.experimental.pallas import tpu as pltpu
from jax.sharding import PartitionSpec as P

REG = 64
LANES = 128
STRIP = 4
CHUNKS = 2

sharpness_divisor = 0.1
ln_eps = 1e-06
norm_eps = 1e-06

VMEM = pl.BlockSpec(memory_space=pltpu.VMEM)
SMEM = pl.BlockSpec(memory_space=pltpu.SMEM)
f32 = jnp.float32
bf16 = jnp.bfloat16


def call(kernel, outs, in_specs, scratch, limit, flops, nbytes):
    return pl.pallas_call(
        kernel,
        out_shape=outs,
        in_specs=in_specs,
        out_specs=[VMEM] * len(outs),
        scratch_shapes=scratch,
        compiler_params=pltpu.CompilerParams(vmem_limit_bytes=limit),
        cost_estimate=pl.CostEstimate(flops=flops, bytes_accessed=nbytes, transcendentals=0),
    )


def dot(a, b):
    return jnp.dot(a, b, preferred_element_type=f32)


def dot_nt(a, b):
    return lax.dot_general(a, b, (((1,), (1,)), ((), ())), preferred_element_type=f32)


def split3(x):
    hi = x.astype(bf16)
    rest = x - hi.astype(f32)
    mid = rest.astype(bf16)
    return hi, mid, (rest - mid.astype(f32)).astype(bf16)


def blank_kernel(out_ref):
    out_ref[...] = jnp.full(out_ref.shape, -1.0, f32)


def pack_kernel(pos_ref, ids_ref, key_ref, dw_ref, blank_ref, tail_ref, w_ref, line):
    section = pos_ref[3]
    keys, depth = key_ref.shape
    shard_rows, width = ids_ref.shape[1:]
    line[...] = blank_ref[...]
    for i in range(ids_ref.shape[0]):
        line[i * shard_rows : (i + 1) * shard_rows, 0:width] = ids_ref[i].astype(f32)
    tail_ref[...] = jnp.zeros(tail_ref.shape, bf16)
    tail_ref[:, depth : depth + LANES] = line[...].astype(bf16)
    tail_ref[0 : keys // 2, 0:depth] = key_ref[pl.ds(pl.multiple_of(section * (keys // 2), keys // 2), keys // 2), :]
    half = w_ref.shape[1]
    lanes = pl.ds(pl.multiple_of(section * half, LANES), half)
    for dy in range(7):
        w_ref[dy * 7 : dy * 7 + 7, :] = dw_ref[dy, :, lanes].astype(f32)


def join_kernel(*refs):
    start = 0
    for ref in refs[:-1]:
        refs[-1][start : start + ref.shape[0], :] = ref[...]
        start += ref.shape[0]


def join(*arrays):
    rows = sum(x.shape[0] for x in arrays)
    shape = jax.ShapeDtypeStruct((rows, arrays[0].shape[1]), arrays[0].dtype)
    joined = call(join_kernel, [shape], [VMEM] * len(arrays), [], 1 << 20, 0, rows * 1024)(*arrays)
    return joined[0]


def add_kernel(a_ref, b_ref, out_ref):
    out_ref[...] = a_ref[...] + b_ref[...]


def conv_kernel(geo, pos_ref, *refs):
    shards, shard_rows, width, out_rows, first_lane = geo
    blocks = refs[:shards]
    w_ref, taps, img_ref, xpad, wide = refs[shards:]
    chunk = taps.shape[1]
    row, first_row, col0 = pos_ref[0], pos_ref[1], pos_ref[2]
    height = shards * shard_rows
    pixels = shard_rows * width
    cols = xpad.shape[1]
    out_pixels = out_rows * width
    step_rows = STRIP

    xpad[0:3] = jnp.zeros((3, cols, LANES), f32)
    xpad[height + 3 : height + 6] = jnp.zeros((3, cols, LANES), f32)
    for y in range(3, height + 3):
        xpad[y, 0:8] = jnp.zeros((8, LANES), f32)
        xpad[y, 8 + width : 16 + width] = jnp.zeros((8, LANES), f32)

    def group(g, carry):
        lanes = pl.ds(pl.multiple_of(g * LANES, LANES), LANES)
        for k in range(shards):
            value = blocks[k][0:pixels, lanes].astype(f32).reshape(shard_rows, width, LANES)
            xpad[pl.ds(3 + (row ^ k) * shard_rows, shard_rows), 8 : 8 + width, :] = value
        for t in range(49):
            w = w_ref[t : t + 1, pl.ds(pl.multiple_of(first_lane + g * LANES, LANES), LANES)]
            wide[t] = jnp.broadcast_to(w, (8, LANES))

        def strip(i, carry):
            top = first_row + i * step_rows
            acc = [jnp.zeros((width // 8, 8, LANES), f32) for _ in range(step_rows)]
            for r in range(step_rows + 6):
                for dx in range(7):
                    v = xpad[top + r, pl.ds(col0 + dx, width), :].reshape(width // 8, 8, LANES)
                    for j in range(step_rows):
                        dy = r - j
                        if 0 <= dy < 7:
                            acc[j] = acc[j] + v * wide[dy * 7 + dx][None]
            for j in range(step_rows):
                start = pl.multiple_of((i * step_rows + j) * width, width)
                taps[pl.ds(start, width), lanes] = acc[j].reshape(width, LANES)
            return carry

        return lax.fori_loop(0, out_rows // step_rows, strip, carry)

    lax.fori_loop(0, chunk // LANES, group, 0)

    for k in range(shards):
        start = (row ^ k) * pixels - first_row * width

        @pl.when((start >= 0) & (start < out_pixels))
        def _():
            img_ref[pl.ds(pl.multiple_of(start, pixels), pixels), :] = blocks[k][0:pixels, :]


def block_kernel(geo, pos_ref, *refs):
    first, pixels, chunks = geo
    own, other, img = refs[:chunks], refs[chunks : 2 * chunks], refs[2 * chunks : 3 * chunks]
    gain_ref, scale_ref, w1_ref, w2_ref, z_ref, send_ref, normed, inner = refs[3 * chunks :]
    chans, hid = w1_ref.shape
    half = chans // 2
    width = half // chunks
    section = pos_ref[3]
    rows = slice(first, first + pixels)
    values = [ref[rows, :] for ref in own + other]
    mean = sum(jnp.sum(v, axis=1, keepdims=True) for v in values) * (1.0 / chans)
    values = [v - mean for v in values]
    spread = sum(jnp.sum(v * v, axis=1, keepdims=True) for v in values) * (1.0 / chans)
    inv = lax.rsqrt(spread + ln_eps)
    gains = gain_ref[...].astype(f32).reshape(1, chans)
    scales = scale_ref[...].astype(f32).reshape(1, chans)
    for c in range(chunks):
        lanes = slice(c * width, (c + 1) * width)
        for side, v in ((section, values[c]), (1 - section, values[chunks + c])):
            start = c * width
            gain = jnp.where(side == 0, gains[:, start : start + width], gains[:, half + start : half + start + width])
            normed[pl.ds(side, 1), :, lanes] = (v * inv * gain).astype(bf16)[None]
    step = 256
    for i in range(hid // step):
        cols = slice(i * step, (i + 1) * step)
        h = dot(normed[0], w1_ref[0:half, cols]) + dot(normed[1], w1_ref[half:chans, cols])
        inner[:, cols] = (0.5 * h * (1.0 + lax.erf(h * 0.7071067811865476))).astype(bf16)
    step = width if width % 256 else 256
    for i in range(chans // step):
        cols = slice(i * step, (i + 1) * step)
        side, start = divmod(i * step, half)
        c, start = divmod(start, width)
        keep = jnp.where(section == side, 1.0, 0.0)
        z = dot(inner[...], w2_ref[:, cols]) * scales[:, cols]
        z = z + img[c][rows, start : start + step].astype(f32) * keep
        z_ref[:, cols] = z
        send_ref[:, cols] = z.astype(bf16)


def expand_kernel(z_ref, other_ref, pe_ref, out_ref, block):
    block[...] = (z_ref[...] + other_ref[...].astype(f32)).astype(bf16)
    step = 256
    for i in range(pe_ref.shape[1] // step):
        cols = slice(i * step, (i + 1) * step)
        out_ref[:, cols] = jnp.maximum(dot(block[...], pe_ref[:, cols]), 0.0).astype(bf16)


def prep_kernel(geo, pos_ref, *refs):
    shards, shard_rows, width, out_pixels, images, batches, per_key, parts = geo
    ids = refs[:shards]
    owner_ref, partner_ref, hot_ref, pick_ref, own_ref, keys_ref, flat = refs[shards:]
    row, first_row, batch, first_slot = pos_ref[0], pos_ref[1], pos_ref[4], pos_ref[5]
    pixels = shard_rows * width
    depth = keys_ref.shape[1]
    for k in range(shards):
        mine = slice(k * per_key // 2, (k + 1) * per_key // 2)
        keys_ref[mine, :] = ids[k][pixels : pixels + per_key // 2, 0:depth]
    ids = [ref[pixels:, depth : depth + LANES].astype(f32) for ref in ids]
    owned = own_ref.shape[0]
    slots = images * REG
    image = row // parts
    flat[...] = jnp.full(flat.shape, -1.0, f32)
    for k in range(shards):
        start = pl.multiple_of((1 + (row ^ k)) * pixels, LANES)
        number = lax.broadcasted_iota(jnp.int32, ids[k].shape, 0)
        inside = lax.broadcasted_iota(jnp.int32, ids[k].shape, 1) < width
        for y in range(shard_rows):
            keep = inside & (number == image * shard_rows + y)
            mine = jnp.sum(jnp.where(keep, ids[k], 0.0), axis=0, keepdims=True)
            mine = jnp.broadcast_to(mine, (8, LANES))
            mine = pltpu.roll(mine, y * width, 1) if y else mine
            line = mine if y == 0 else line + mine
        flat[0:8, pl.ds(start, pixels)] = line
    total = flat.shape[1]
    whole = jnp.broadcast_to(flat[0:1, :], (8, total))
    lane = lax.broadcasted_iota(jnp.int32, (8, total), 1)
    col = lane % width
    region = lax.broadcasted_iota(jnp.int32, (REG, out_pixels), 0).astype(f32)
    start = pl.multiple_of(pixels + first_row * width, LANES)
    for dy in range(3):
        for dx in range(3):
            off = (dy - 1) * width + dx - 1
            moved = whole if off == 0 else pltpu.roll(whole, off % total, 1)
            if dx == 0:
                moved = jnp.where(col == width - 1, -1.0, moved)
            if dx == 2:
                moved = jnp.where(col == 0, -1.0, moved)
            flat[8:16, :] = moved
            line = flat[8:9, pl.ds(start, out_pixels)]
            tap = dy * 3 + dx
            hot_ref[tap * REG : (tap + 1) * REG, :] = jnp.where(region == line, 1.0, 0.0).astype(bf16)
    slot = lax.broadcasted_iota(jnp.int32, (owned, slots), 1)
    want = lax.broadcasted_iota(jnp.int32, (owned, slots), 0) + first_slot
    pick = owner_ref[...] == want
    pick_ref[...] = jnp.where(pick, 1.0, 0.0).astype(bf16)
    one_region = lax.broadcasted_iota(jnp.int32, (REG, LANES), 0).astype(f32)
    tallies = []
    for i in range(images):
        tally = jnp.zeros((REG, LANES), f32)
        for k in range(shards):
            for y in range(i * shard_rows, (i + 1) * shard_rows):
                tally = tally + jnp.where(one_region == ids[k][y : y + 1, :], 1.0, 0.0)
        tallies.append(tally)
    tally = jnp.concatenate(tallies, axis=0).astype(bf16)
    count = dot_nt(jnp.ones((8, LANES), bf16), tally)[0:1]
    mates = jnp.concatenate([partner_ref[i : i + 1, :] for i in range(images)], axis=1)
    mate = (batch * images + slot // REG) * REG + mates
    block = mate // per_key
    within = mate % per_key
    core = (within // (per_key // 2)) ^ pos_ref[3]
    place = (core * batches + ((block // shards) ^ batch)) * shards + ((block % shards) ^ row)
    place = place * (per_key // 2) + within % (per_key // 2)
    place = jnp.sum(jnp.where(pick, place, 0).astype(f32), axis=1, keepdims=True)
    number = jnp.sum(jnp.where(pick, count, 0.0), axis=1, keepdims=True)
    side = lax.broadcasted_iota(jnp.int32, (owned, LANES), 1)
    own_ref[...] = jnp.where(side == 0, place, jnp.where(side == 1, number, 0.0))


def project_kernel(z_ref, other_ref, first_ref, pe_ref, pk_ref, hot_ref, out_ref, block, hidden):
    before = first_ref.shape[0]
    pixels = z_ref.shape[0]
    taps = pk_ref.shape[0]
    block[...] = (z_ref[...] + other_ref[...].astype(f32)).astype(bf16)
    step = 256
    acc = jnp.zeros((2 * REG, out_ref.shape[1]), f32)
    for i in range(pe_ref.shape[1] // step):
        cols = slice(i * step, (i + 1) * step)
        hidden[i, 0:before, :] = first_ref[:, cols]
        h = jnp.maximum(dot(block[...], pe_ref[:, cols]), 0.0)
        hidden[i, before : before + pixels, :] = h.astype(bf16)
        sums = dot(hot_ref[...], hidden[i])
        hi = sums.astype(bf16)
        lo = (sums - hi.astype(f32)).astype(bf16)
        for t in range(taps):
            rows = slice(t * REG, (t + 1) * REG)
            both = jnp.concatenate([hi[rows], lo[rows]], axis=0)
            acc = acc + dot(both, pk_ref[t, cols, :])
    out_ref[...] = acc[0:REG] + acc[REG:]


def loss_kernel(geo, *refs):
    shards, parts = geo
    sums, row = refs[1 : shards + 1], refs[0][0]
    pick_ref, own_ref = refs[shards + 1 : shards + 3]
    embed_ref, loss_ref, table = refs[-3:]
    if parts > 1:
        table[...] = jnp.zeros(table.shape, f32)
    for k in range(shards):
        place = pl.ds(pl.multiple_of(((row ^ k) // parts) * REG, REG), REG)
        value = sums[k][...]
        table[place, :] = value if parts == 1 else table[place, :] + value
    pick = pick_ref[...]
    hi, mid, lo = split3(table[...])
    ordered = dot(pick, hi) + dot(pick, mid) + dot(pick, lo)
    unit = ordered * lax.rsqrt(jnp.sum(ordered * ordered, axis=1, keepdims=True) + norm_eps)
    embed_ref[...] = unit
    owned = unit.shape[0]
    keys = jnp.concatenate([ref[...] for ref in refs[shards + 3 : -3]], axis=0)
    wide = keys.astype(f32)
    square = wide * wide
    square_hi = square.astype(bf16)
    square_lo = (square - square_hi.astype(f32)).astype(bf16)
    ones = jnp.ones((16, keys.shape[1]), bf16)
    length = dot_nt(ones, square_hi)[0:1] + dot_nt(ones, square_lo)[0:1]
    three = dot_nt(jnp.concatenate(split3(unit), axis=0), keys)
    logits = three[0:owned] + three[owned : 2 * owned] + three[2 * owned :]
    logits = logits * (lax.rsqrt(length + norm_eps) / sharpness_divisor)
    total = jnp.log(jnp.sum(jnp.exp(logits), axis=1, keepdims=True))
    column = lax.broadcasted_iota(jnp.int32, logits.shape, 1).astype(f32)
    match = jnp.sum(jnp.where(column == own_ref[:, 0:1], logits, 0.0), axis=1, keepdims=True)
    loss = jnp.where(own_ref[:, 1:2] > 0.5, total - match, 0.0)
    line = lax.broadcasted_iota(jnp.int32, (owned, owned), 0)
    other = lax.broadcasted_iota(jnp.int32, (owned, owned), 1)
    loss_ref[...] = jnp.sum(jnp.where(line == other, loss, 0.0), axis=0, keepdims=True)


def swap(x, axis, bit):
    return lax.ppermute(x, axis, [(i, i ^ bit) for i in range(lax.axis_size(axis))])


def body(
    features,
    dw_kernel,
    ln_gain,
    widening_pointwise_matrix,
    w_reduce,
    layer_branch_scale,
    p_expand,
    p_kernel,
    region_ids,
    owner_slot,
    partner,
    key_embed,
):
    images, shard_rows, width, chans = features.shape
    shards = lax.axis_size("rows")
    batches = lax.axis_size("batch")
    row = lax.axis_index("rows")
    batch = lax.axis_index("batch")
    section = lax.axis_index("section")
    half = chans // lax.axis_size("section")
    parts = shards // images
    out_rows = shards * shard_rows // parts
    pixels = shard_rows * width
    out_pixels = out_rows * width
    slots = images * REG
    owned = slots // shards
    out_dim = p_kernel.shape[2]
    mib = 1 << 20
    span = half // CHUNKS

    w1, w2, pe, pk = widening_pointwise_matrix, w_reduce, p_expand, p_kernel
    first_row = (row % parts) * out_rows
    spot = jnp.stack(
        [row, first_row, jnp.int32(5), section, batch, row * owned]
    ).astype(jnp.int32)

    per_key, depth = key_embed.shape
    tail = max(-(-images * shard_rows // 16) * 16, per_key // 2)
    def after(here, *done):
        return lax.optimization_barrier((here, *done))[0]

    (blank,) = call(
        blank_kernel, [jax.ShapeDtypeStruct((tail, LANES), f32)], [], [], mib, 10**10, 10**4
    )()
    riders, weights = call(
        pack_kernel,
        [jax.ShapeDtypeStruct((tail, span), bf16), jax.ShapeDtypeStruct((49, half), f32)],
        [SMEM] + [VMEM] * 4,
        [pltpu.VMEM((tail, LANES), f32)],
        mib,
        0,
        10**6,
    )(spot, region_ids, key_embed, dw_kernel, blank)
    got = []
    for c in range(CHUNKS):
        blocks = []
        for k in range(shards):
            place = ((row ^ k) // parts, 0, 0, section * half + c * span)
            part = lax.dynamic_slice(features, place, (1, shard_rows, width, span)).reshape(pixels, span)
            if c == CHUNKS - 1:
                part = jnp.concatenate([part, riders], axis=0)
            blocks.append(part)
        got.append([blocks[0]] + [swap(blocks[k], "rows", k) for k in range(1, shards)])

    own, other, img = [], [], []
    for c in range(CHUNKS):
        here = after(spot, *own) if c else spot
        taps, image = call(
            functools.partial(conv_kernel, (shards, shard_rows, width, out_rows, c * span)),
            [
                jax.ShapeDtypeStruct((out_pixels, span), f32),
                jax.ShapeDtypeStruct((out_pixels, span), bf16),
            ],
            [SMEM] + [VMEM] * (shards + 1),
            [
                pltpu.VMEM((shards * shard_rows + 6, width + 16, LANES), f32),
                pltpu.VMEM((49, 8, LANES), f32),
            ],
            3 * mib,
            out_pixels * span * 98 * 100,
            out_pixels * span * 10,
        )(here, *got[c], weights)
        own.append(taps)
        img.append(image)
        other.append(swap(taps, "section", 1))

    hot, pick, facts, keys = call(
        functools.partial(
            prep_kernel,
            (shards, shard_rows, width, out_pixels, images, batches, per_key, parts),
        ),
        [
            jax.ShapeDtypeStruct((9 * REG, out_pixels), bf16),
            jax.ShapeDtypeStruct((owned, slots), bf16),
            jax.ShapeDtypeStruct((owned, LANES), f32),
            jax.ShapeDtypeStruct((shards * per_key // 2, depth), bf16),
        ],
        [SMEM] + [VMEM] * (shards + 2),
        [pltpu.VMEM((16, (shards + 2) * pixels), f32)],
        2 * mib,
        10**8,
        10**6,
    )(after(spot, *own), *got[-1], owner_slot, partner)
    pieces = [keys, swap(keys, "batch", 1)]

    hid = w1.shape[1]
    part_pixels = out_pixels // 2
    z, z_other = [], []
    for p in range(2):
        here = after(spot, pieces[-1], *z) if p else after(spot, hot)
        mine, send = call(
            functools.partial(block_kernel, (p * part_pixels, part_pixels, CHUNKS)),
            [
                jax.ShapeDtypeStruct((part_pixels, chans), f32),
                jax.ShapeDtypeStruct((part_pixels, chans), bf16),
            ],
            [SMEM] + [VMEM] * (3 * CHUNKS + 4),
            [pltpu.VMEM((2, part_pixels, half), bf16), pltpu.VMEM((part_pixels, hid), bf16)],
            8 * mib,
            4 * part_pixels * hid * chans,
            4 * hid * chans,
        )(here, *own, *other, *img, ln_gain, layer_branch_scale, w1, w2)
        z.append(mine)
        z_other.append(swap(send, "section", 1))
    bit = 2
    while bit < batches:
        pieces.append(swap(join(*pieces), "batch", bit))
        bit *= 2
    hidden = pe.shape[1]
    (hid_a,) = call(
        expand_kernel,
        [jax.ShapeDtypeStruct((part_pixels, hidden), bf16)],
        [VMEM] * 3,
        [pltpu.VMEM((part_pixels, chans), bf16)],
        6 * mib,
        2 * part_pixels * hidden * chans,
        2 * hidden * chans,
    )(z[0], z_other[0], pe)
    (pooled,) = call(
        project_kernel,
        [jax.ShapeDtypeStruct((REG, out_dim), f32)],
        [VMEM] * 6,
        [
            pltpu.VMEM((part_pixels, chans), bf16),
            pltpu.VMEM((hidden // 256, out_pixels, 256), bf16),
        ],
        8 * mib,
        2 * part_pixels * hidden * chans + 4 * 9 * REG * hidden * out_pixels,
        4 * hidden * chans,
    )(z[1], z_other[1], hid_a, pe, pk, hot)
    (pooled,) = call(
        add_kernel,
        [jax.ShapeDtypeStruct((REG, out_dim), f32)],
        [VMEM] * 2,
        [],
        mib,
        10**5,
        10**5,
    )(pooled, swap(pooled, "section", 1))
    pieces[-1] = after(pieces[-1], pooled)
    pieces.append(swap(join(*pieces), "section", 1))
    sums = [pooled] + [swap(pooled, "rows", k) for k in range(1, shards)]

    embed, loss = call(
        functools.partial(loss_kernel, (shards, parts)),
        [jax.ShapeDtypeStruct((owned, out_dim), f32), jax.ShapeDtypeStruct((1, owned), f32)],
        [SMEM] + [VMEM] * (shards + 2 + len(pieces)),
        [pltpu.VMEM((slots, out_dim), f32)],
        6 * mib,
        10**8,
        10**6,
    )(spot, *sums, pick, facts, *pieces)
    return embed, loss.reshape(owned)


def solution(mesh):
    in_specs = (
        P("batch", "rows", None, None),
        P(),
        P(),
        P(None, "section"),
        P("section", None),
        P(),
        P(None, "section"),
        P(None, "section", None),
        P("batch", "rows", None),
        P("batch", None),
        P("batch", None),
        P(("batch", "rows"), None),
    )
    out_specs = (P(("batch", "rows"), None), P(("batch", "rows")))
    return jax.shard_map(body, mesh=mesh, in_specs=in_specs, out_specs=out_specs, check_vma=False)
```

```python
import functools

import jax
import jax.numpy as jnp
from jax import lax
from jax.experimental import pallas as pl
from jax.experimental.pallas import tpu as pltpu
from jax.sharding import PartitionSpec as P

REG = 64
LANES = 128
STRIP = 8
CHUNKS = 2

sharpness_divisor = 0.1
ln_eps = 1e-06
norm_eps = 1e-06

VMEM = pl.BlockSpec(memory_space=pltpu.VMEM)
SMEM = pl.BlockSpec(memory_space=pltpu.SMEM)
f32 = jnp.float32
bf16 = jnp.bfloat16


def call(kernel, outs, in_specs, scratch, limit, flops, nbytes):
    return pl.pallas_call(
        kernel,
        out_shape=outs,
        in_specs=in_specs,
        out_specs=[VMEM] * len(outs),
        scratch_shapes=scratch,
        compiler_params=pltpu.CompilerParams(vmem_limit_bytes=limit),
        cost_estimate=pl.CostEstimate(flops=flops, bytes_accessed=nbytes, transcendentals=0),
    )


def dot(a, b):
    return jnp.dot(a, b, preferred_element_type=f32)


def dot_nt(a, b):
    return lax.dot_general(a, b, (((1,), (1,)), ((), ())), preferred_element_type=f32)


def gelu(x):
    size = jnp.abs(x)
    below = 1.0 + size * (0.3275911 * 0.5**0.5)
    t = pl.reciprocal(below, approx=True)
    t = t * (2.0 - below * t)
    half = 0.5 * 1.061405429
    for c in (-1.453152027, 1.421413741, -0.284496736, 0.254829592):
        half = half * t + 0.5 * c
    return jnp.maximum(x, 0.0) - size * (half * t) * jnp.exp(x * x * -0.5)


def split3(x):
    hi = x.astype(bf16)
    rest = x - hi.astype(f32)
    mid = rest.astype(bf16)
    return hi, mid, (rest - mid.astype(f32)).astype(bf16)


def blank_kernel(out_ref):
    out_ref[...] = jnp.full(out_ref.shape, -1.0, f32)


def pack_kernel(pos_ref, ids_ref, key_ref, dw_ref, blank_ref, tail_ref, w_ref, line):
    section = pos_ref[3]
    keys, depth = key_ref.shape
    shard_rows, width = ids_ref.shape[1:]
    line[...] = blank_ref[...]
    for i in range(ids_ref.shape[0]):
        line[i * shard_rows : (i + 1) * shard_rows, 0:width] = ids_ref[i].astype(f32)
    tail_ref[...] = jnp.zeros(tail_ref.shape, bf16)
    tail_ref[:, depth : depth + LANES] = line[...].astype(bf16)
    tail_ref[0 : keys // 2, 0:depth] = key_ref[pl.ds(pl.multiple_of(section * (keys // 2), keys // 2), keys // 2), :]
    half = w_ref.shape[1]
    lanes = pl.ds(pl.multiple_of(section * half, LANES), half)
    for dy in range(7):
        w_ref[dy * 7 : dy * 7 + 7, :] = dw_ref[dy, :, lanes].astype(f32)


def join_kernel(*refs):
    start = 0
    for ref in refs[:-1]:
        refs[-1][start : start + ref.shape[0], :] = ref[...]
        start += ref.shape[0]


def join(*arrays):
    rows = sum(x.shape[0] for x in arrays)
    shape = jax.ShapeDtypeStruct((rows, arrays[0].shape[1]), arrays[0].dtype)
    joined = call(join_kernel, [shape], [VMEM] * len(arrays), [], 1 << 20, 0, rows * 1024)(*arrays)
    return joined[0]


def add_kernel(a_ref, b_ref, out_ref):
    out_ref[...] = a_ref[...] + b_ref[...]


def conv_kernel(geo, pos_ref, *refs):
    shards, shard_rows, width, out_rows, first_lane = geo
    blocks = refs[:shards]
    w_ref, taps, img_ref, xpad, wide = refs[shards:]
    chunk = taps.shape[1]
    row, first_row, col0 = pos_ref[0], pos_ref[1], pos_ref[2]
    height = shards * shard_rows
    pixels = shard_rows * width
    cols = xpad.shape[1]
    out_pixels = out_rows * width
    step_rows = STRIP

    xpad[0:3] = jnp.zeros((3, cols, LANES), f32)
    xpad[height + 3 : height + 6] = jnp.zeros((3, cols, LANES), f32)
    for y in range(3, height + 3):
        xpad[y, 0:8] = jnp.zeros((8, LANES), f32)
        xpad[y, 8 + width : 16 + width] = jnp.zeros((8, LANES), f32)

    def group(g, carry):
        lanes = pl.ds(pl.multiple_of(g * LANES, LANES), LANES)
        for k in range(shards):
            value = blocks[k][0:pixels, lanes].astype(f32).reshape(shard_rows, width, LANES)
            xpad[pl.ds(3 + (row ^ k) * shard_rows, shard_rows), 8 : 8 + width, :] = value
        for t in range(49):
            w = w_ref[t : t + 1, pl.ds(pl.multiple_of(first_lane + g * LANES, LANES), LANES)]
            wide[t] = jnp.broadcast_to(w, (8, LANES))

        def strip(i, carry):
            top = first_row + i * step_rows
            acc = [jnp.zeros((width // 8, 8, LANES), f32) for _ in range(step_rows)]
            for r in range(step_rows + 6):
                for dx in range(7):
                    v = xpad[top + r, pl.ds(col0 + dx, width), :].reshape(width // 8, 8, LANES)
                    for j in range(step_rows):
                        dy = r - j
                        if 0 <= dy < 7:
                            acc[j] = acc[j] + v * wide[dy * 7 + dx][None]
            for j in range(step_rows):
                start = pl.multiple_of((i * step_rows + j) * width, width)
                taps[pl.ds(start, width), lanes] = acc[j].reshape(width, LANES)
            return carry

        return lax.fori_loop(0, out_rows // step_rows, strip, carry)

    lax.fori_loop(0, chunk // LANES, group, 0)

    for k in range(shards):
        start = (row ^ k) * pixels - first_row * width

        @pl.when((start >= 0) & (start < out_pixels))
        def _():
            img_ref[pl.ds(pl.multiple_of(start, pixels), pixels), :] = blocks[k][0:pixels, :]


def block_kernel(geo, pos_ref, *refs):
    first, pixels, chunks = geo
    own, other, img = refs[:chunks], refs[chunks : 2 * chunks], refs[2 * chunks : 3 * chunks]
    gain_ref, scale_ref, w1_ref, w2_ref, z_ref, send_ref, normed, inner = refs[3 * chunks :]
    chans, hid = w1_ref.shape
    half = chans // 2
    width = half // chunks
    section = pos_ref[3]
    rows = slice(first, first + pixels)
    values = [ref[rows, :] for ref in own + other]
    mean = sum(jnp.sum(v, axis=1, keepdims=True) for v in values) * (1.0 / chans)
    values = [v - mean for v in values]
    spread = sum(jnp.sum(v * v, axis=1, keepdims=True) for v in values) * (1.0 / chans)
    inv = lax.rsqrt(spread + ln_eps)
    gains = gain_ref[...].astype(f32).reshape(1, chans)
    scales = scale_ref[...].astype(f32).reshape(1, chans)
    for c in range(chunks):
        lanes = slice(c * width, (c + 1) * width)
        for side, v in ((section, values[c]), (1 - section, values[chunks + c])):
            start = c * width
            gain = jnp.where(side == 0, gains[:, start : start + width], gains[:, half + start : half + start + width])
            normed[pl.ds(side, 1), :, lanes] = (v * inv * gain).astype(bf16)[None]
    step = 256
    for i in range(hid // step):
        cols = slice(i * step, (i + 1) * step)
        h = dot(normed[0], w1_ref[0:half, cols]) + dot(normed[1], w1_ref[half:chans, cols])
        inner[:, cols] = gelu(h).astype(bf16)
    step = width if width % 256 else 256
    for i in range(chans // step):
        cols = slice(i * step, (i + 1) * step)
        side, start = divmod(i * step, half)
        c, start = divmod(start, width)
        keep = jnp.where(section == side, 1.0, 0.0)
        z = dot(inner[...], w2_ref[:, cols]) * scales[:, cols]
        z = z + img[c][rows, start : start + step].astype(f32) * keep
        z_ref[:, cols] = z
        send_ref[:, cols] = z.astype(bf16)


def expand_kernel(z_ref, other_ref, pe_ref, out_ref, block):
    block[...] = (z_ref[...] + other_ref[...].astype(f32)).astype(bf16)
    step = 256
    for i in range(pe_ref.shape[1] // step):
        cols = slice(i * step, (i + 1) * step)
        out_ref[:, cols] = jnp.maximum(dot(block[...], pe_ref[:, cols]), 0.0).astype(bf16)


def prep_kernel(geo, pos_ref, *refs):
    shards, shard_rows, width, out_pixels, images, batches, per_key, parts = geo
    ids = refs[:shards]
    owner_ref, partner_ref, hot_ref, pick_ref, own_ref, keys_ref, flat = refs[shards:]
    row, first_row, batch, first_slot = pos_ref[0], pos_ref[1], pos_ref[4], pos_ref[5]
    pixels = shard_rows * width
    depth = keys_ref.shape[1]
    for k in range(shards):
        mine = slice(k * per_key // 2, (k + 1) * per_key // 2)
        keys_ref[mine, :] = ids[k][pixels : pixels + per_key // 2, 0:depth]
    ids = [ref[pixels:, depth : depth + LANES].astype(f32) for ref in ids]
    owned = own_ref.shape[0]
    slots = images * REG
    image = row // parts
    flat[...] = jnp.full(flat.shape, -1.0, f32)
    for k in range(shards):
        start = pl.multiple_of((1 + (row ^ k)) * pixels, LANES)
        number = lax.broadcasted_iota(jnp.int32, ids[k].shape, 0)
        inside = lax.broadcasted_iota(jnp.int32, ids[k].shape, 1) < width
        for y in range(shard_rows):
            keep = inside & (number == image * shard_rows + y)
            mine = jnp.sum(jnp.where(keep, ids[k], 0.0), axis=0, keepdims=True)
            mine = jnp.broadcast_to(mine, (8, LANES))
            mine = pltpu.roll(mine, y * width, 1) if y else mine
            line = mine if y == 0 else line + mine
        flat[0:8, pl.ds(start, pixels)] = line
    total = flat.shape[1]
    whole = jnp.broadcast_to(flat[0:1, :], (8, total))
    lane = lax.broadcasted_iota(jnp.int32, (8, total), 1)
    col = lane % width
    region = lax.broadcasted_iota(jnp.int32, (REG, out_pixels), 0).astype(f32)
    start = pl.multiple_of(pixels + first_row * width, LANES)
    for dy in range(3):
        for dx in range(3):
            off = (dy - 1) * width + dx - 1
            moved = whole if off == 0 else pltpu.roll(whole, off % total, 1)
            if dx == 0:
                moved = jnp.where(col == width - 1, -1.0, moved)
            if dx == 2:
                moved = jnp.where(col == 0, -1.0, moved)
            flat[8:16, :] = moved
            line = flat[8:9, pl.ds(start, out_pixels)]
            tap = dy * 3 + dx
            hot_ref[tap * REG : (tap + 1) * REG, :] = jnp.where(region == line, 1.0, 0.0).astype(bf16)
    slot = lax.broadcasted_iota(jnp.int32, (owned, slots), 1)
    want = lax.broadcasted_iota(jnp.int32, (owned, slots), 0) + first_slot
    pick = owner_ref[...] == want
    pick_ref[...] = jnp.where(pick, 1.0, 0.0).astype(bf16)
    one_region = lax.broadcasted_iota(jnp.int32, (REG, LANES), 0).astype(f32)
    tallies = []
    for i in range(images):
        tally = jnp.zeros((REG, LANES), f32)
        for k in range(shards):
            for y in range(i * shard_rows, (i + 1) * shard_rows):
                tally = tally + jnp.where(one_region == ids[k][y : y + 1, :], 1.0, 0.0)
        tallies.append(tally)
    tally = jnp.concatenate(tallies, axis=0).astype(bf16)
    count = dot_nt(jnp.ones((8, LANES), bf16), tally)[0:1]
    mates = jnp.concatenate([partner_ref[i : i + 1, :] for i in range(images)], axis=1)
    mate = (batch * images + slot // REG) * REG + mates
    block = mate // per_key
    within = mate % per_key
    core = (within // (per_key // 2)) ^ pos_ref[3]
    place = (core * batches + ((block // shards) ^ batch)) * shards + ((block % shards) ^ row)
    place = place * (per_key // 2) + within % (per_key // 2)
    place = jnp.sum(jnp.where(pick, place, 0).astype(f32), axis=1, keepdims=True)
    number = jnp.sum(jnp.where(pick, count, 0.0), axis=1, keepdims=True)
    side = lax.broadcasted_iota(jnp.int32, (owned, LANES), 1)
    own_ref[...] = jnp.where(side == 0, place, jnp.where(side == 1, number, 0.0))


def project_kernel(z_ref, other_ref, first_ref, pe_ref, pk_ref, hot_ref, out_ref, block, hidden):
    before = first_ref.shape[0]
    pixels = z_ref.shape[0]
    taps = pk_ref.shape[0]
    block[...] = (z_ref[...] + other_ref[...].astype(f32)).astype(bf16)
    step = 256
    acc = jnp.zeros((2 * REG, out_ref.shape[1]), f32)
    for i in range(pe_ref.shape[1] // step):
        cols = slice(i * step, (i + 1) * step)
        hidden[i, 0:before, :] = first_ref[:, cols]
        h = jnp.maximum(dot(block[...], pe_ref[:, cols]), 0.0)
        hidden[i, before : before + pixels, :] = h.astype(bf16)
        sums = dot(hot_ref[...], hidden[i])
        hi = sums.astype(bf16)
        lo = (sums - hi.astype(f32)).astype(bf16)
        for t in range(taps):
            rows = slice(t * REG, (t + 1) * REG)
            both = jnp.concatenate([hi[rows], lo[rows]], axis=0)
            acc = acc + dot(both, pk_ref[t, cols, :])
    out_ref[...] = acc[0:REG] + acc[REG:]


def loss_kernel(geo, *refs):
    shards, parts = geo
    sums, row = refs[1 : shards + 1], refs[0][0]
    pick_ref, own_ref = refs[shards + 1 : shards + 3]
    embed_ref, loss_ref, table = refs[-3:]
    if parts > 1:
        table[...] = jnp.zeros(table.shape, f32)
    for k in range(shards):
        place = pl.ds(pl.multiple_of(((row ^ k) // parts) * REG, REG), REG)
        value = sums[k][...]
        table[place, :] = value if parts == 1 else table[place, :] + value
    pick = pick_ref[...]
    hi, mid, lo = split3(table[...])
    ordered = dot(pick, hi) + dot(pick, mid) + dot(pick, lo)
    unit = ordered * lax.rsqrt(jnp.sum(ordered * ordered, axis=1, keepdims=True) + norm_eps)
    embed_ref[...] = unit
    owned = unit.shape[0]
    keys = jnp.concatenate([ref[...] for ref in refs[shards + 3 : -3]], axis=0)
    wide = keys.astype(f32)
    square = wide * wide
    square_hi = square.astype(bf16)
    square_lo = (square - square_hi.astype(f32)).astype(bf16)
    ones = jnp.ones((16, keys.shape[1]), bf16)
    length = dot_nt(ones, square_hi)[0:1] + dot_nt(ones, square_lo)[0:1]
    three = dot_nt(jnp.concatenate(split3(unit), axis=0), keys)
    logits = three[0:owned] + three[owned : 2 * owned] + three[2 * owned :]
    logits = logits * (lax.rsqrt(length + norm_eps) / sharpness_divisor)
    total = jnp.log(jnp.sum(jnp.exp(logits), axis=1, keepdims=True))
    column = lax.broadcasted_iota(jnp.int32, logits.shape, 1).astype(f32)
    match = jnp.sum(jnp.where(column == own_ref[:, 0:1], logits, 0.0), axis=1, keepdims=True)
    loss = jnp.where(own_ref[:, 1:2] > 0.5, total - match, 0.0)
    line = lax.broadcasted_iota(jnp.int32, (owned, owned), 0)
    other = lax.broadcasted_iota(jnp.int32, (owned, owned), 1)
    loss_ref[...] = jnp.sum(jnp.where(line == other, loss, 0.0), axis=0, keepdims=True)


def swap(x, axis, bit):
    return lax.ppermute(x, axis, [(i, i ^ bit) for i in range(lax.axis_size(axis))])


def body(
    features,
    dw_kernel,
    ln_gain,
    widening_pointwise_matrix,
    w_reduce,
    layer_branch_scale,
    p_expand,
    p_kernel,
    region_ids,
    owner_slot,
    partner,
    key_embed,
):
    images, shard_rows, width, chans = features.shape
    shards = lax.axis_size("rows")
    batches = lax.axis_size("batch")
    row = lax.axis_index("rows")
    batch = lax.axis_index("batch")
    section = lax.axis_index("section")
    half = chans // lax.axis_size("section")
    parts = shards // images
    out_rows = shards * shard_rows // parts
    pixels = shard_rows * width
    out_pixels = out_rows * width
    slots = images * REG
    owned = slots // shards
    out_dim = p_kernel.shape[2]
    mib = 1 << 20
    span = half // CHUNKS

    w1, w2, pe, pk = widening_pointwise_matrix, w_reduce, p_expand, p_kernel
    first_row = (row % parts) * out_rows
    spot = jnp.stack(
        [row, first_row, jnp.int32(5), section, batch, row * owned]
    ).astype(jnp.int32)

    per_key, depth = key_embed.shape
    tail = max(-(-images * shard_rows // 16) * 16, per_key // 2)
    def after(here, *done):
        return lax.optimization_barrier((here, *done))[0]

    (blank,) = call(
        blank_kernel, [jax.ShapeDtypeStruct((tail, LANES), f32)], [], [], mib, 10**10, 10**4
    )()
    riders, weights = call(
        pack_kernel,
        [jax.ShapeDtypeStruct((tail, span), bf16), jax.ShapeDtypeStruct((49, half), f32)],
        [SMEM] + [VMEM] * 4,
        [pltpu.VMEM((tail, LANES), f32)],
        mib,
        0,
        10**6,
    )(spot, region_ids, key_embed, dw_kernel, blank)
    got = []
    for c in range(CHUNKS):
        blocks = []
        for k in range(shards):
            place = ((row ^ k) // parts, 0, 0, section * half + c * span)
            part = lax.dynamic_slice(features, place, (1, shard_rows, width, span)).reshape(pixels, span)
            if c == CHUNKS - 1:
                part = jnp.concatenate([part, riders], axis=0)
            blocks.append(part)
        got.append([blocks[0]] + [swap(blocks[k], "rows", k) for k in range(1, shards)])

    own, other, img = [], [], []
    for c in range(CHUNKS):
        here = after(spot, *own) if c else spot
        taps, image = call(
            functools.partial(conv_kernel, (shards, shard_rows, width, out_rows, c * span)),
            [
                jax.ShapeDtypeStruct((out_pixels, span), f32),
                jax.ShapeDtypeStruct((out_pixels, span), bf16),
            ],
            [SMEM] + [VMEM] * (shards + 1),
            [
                pltpu.VMEM((shards * shard_rows + 6, width + 16, LANES), f32),
                pltpu.VMEM((49, 8, LANES), f32),
            ],
            3 * mib,
            out_pixels * span * 98 * 100,
            out_pixels * span * 10,
        )(here, *got[c], weights)
        own.append(taps)
        img.append(image)
        other.append(swap(taps, "section", 1))

    hot, pick, facts, keys = call(
        functools.partial(
            prep_kernel,
            (shards, shard_rows, width, out_pixels, images, batches, per_key, parts),
        ),
        [
            jax.ShapeDtypeStruct((9 * REG, out_pixels), bf16),
            jax.ShapeDtypeStruct((owned, slots), bf16),
            jax.ShapeDtypeStruct((owned, LANES), f32),
            jax.ShapeDtypeStruct((shards * per_key // 2, depth), bf16),
        ],
        [SMEM] + [VMEM] * (shards + 2),
        [pltpu.VMEM((16, (shards + 2) * pixels), f32)],
        2 * mib,
        10**8,
        10**6,
    )(after(spot, *own), *got[-1], owner_slot, partner)
    pieces = [keys, swap(keys, "batch", 1)]

    hid = w1.shape[1]
    part_pixels = out_pixels // 2
    z, z_other = [], []
    for p in range(2):
        here = after(spot, pieces[-1], *z) if p else after(spot, hot)
        mine, send = call(
            functools.partial(block_kernel, (p * part_pixels, part_pixels, CHUNKS)),
            [
                jax.ShapeDtypeStruct((part_pixels, chans), f32),
                jax.ShapeDtypeStruct((part_pixels, chans), bf16),
            ],
            [SMEM] + [VMEM] * (3 * CHUNKS + 4),
            [pltpu.VMEM((2, part_pixels, half), bf16), pltpu.VMEM((part_pixels, hid), bf16)],
            8 * mib,
            4 * part_pixels * hid * chans,
            4 * hid * chans,
        )(here, *own, *other, *img, ln_gain, layer_branch_scale, w1, w2)
        z.append(mine)
        z_other.append(swap(send, "section", 1))
    bit = 2
    while bit < batches:
        pieces.append(swap(join(*pieces), "batch", bit))
        bit *= 2

    hidden = pe.shape[1]
    (hid_a,) = call(
        expand_kernel,
        [jax.ShapeDtypeStruct((part_pixels, hidden), bf16)],
        [VMEM] * 3,
        [pltpu.VMEM((part_pixels, chans), bf16)],
        6 * mib,
        2 * part_pixels * hidden * chans,
        2 * hidden * chans,
    )(z[0], z_other[0], pe)
    (pooled,) = call(
        project_kernel,
        [jax.ShapeDtypeStruct((REG, out_dim), f32)],
        [VMEM] * 6,
        [
            pltpu.VMEM((part_pixels, chans), bf16),
            pltpu.VMEM((hidden // 256, out_pixels, 256), bf16),
        ],
        8 * mib,
        2 * part_pixels * hidden * chans + 4 * 9 * REG * hidden * out_pixels,
        4 * hidden * chans,
    )(z[1], z_other[1], hid_a, pe, pk, hot)
    (pooled,) = call(
        add_kernel,
        [jax.ShapeDtypeStruct((REG, out_dim), f32)],
        [VMEM] * 2,
        [],
        mib,
        10**5,
        10**5,
    )(pooled, swap(pooled, "section", 1))
    sums = [pooled]
    for k in range(1, shards):
        top = 1 << (k.bit_length() - 1)
        sums.append(swap(sums[k ^ top], "rows", top))
    pieces[-1] = after(pieces[-1], sums[1])
    pieces.append(swap(join(*pieces), "section", 1))

    embed, loss = call(
        functools.partial(loss_kernel, (shards, parts)),
        [jax.ShapeDtypeStruct((owned, out_dim), f32), jax.ShapeDtypeStruct((1, owned), f32)],
        [SMEM] + [VMEM] * (shards + 2 + len(pieces)),
        [pltpu.VMEM((slots, out_dim), f32)],
        6 * mib,
        10**8,
        10**6,
    )(spot, *sums, pick, facts, *pieces)
    return embed, loss.reshape(owned)


def solution(mesh):
    in_specs = (
        P("batch", "rows", None, None),
        P(),
        P(),
        P(None, "section"),
        P("section", None),
        P(),
        P(None, "section"),
        P(None, "section", None),
        P("batch", "rows", None),
        P("batch", None),
        P("batch", None),
        P(("batch", "rows"), None),
    )
    out_specs = (P(("batch", "rows"), None), P(("batch", "rows")))
    return jax.shard_map(body, mesh=mesh, in_specs=in_specs, out_specs=out_specs, check_vma=False)
```

```python
import functools

import jax
import jax.numpy as jnp
from jax import lax
from jax.experimental import pallas as pl
from jax.experimental.pallas import tpu as pltpu
from jax.sharding import PartitionSpec as P

REG = 64
LANES = 128
STRIP = 4
CHUNKS = 2

sharpness_divisor = 0.1
ln_eps = 1e-06
norm_eps = 1e-06

VMEM = pl.BlockSpec(memory_space=pltpu.VMEM)
SMEM = pl.BlockSpec(memory_space=pltpu.SMEM)
f32 = jnp.float32
bf16 = jnp.bfloat16


def call(kernel, outs, in_specs, scratch, limit, flops, nbytes):
    return pl.pallas_call(
        kernel,
        out_shape=outs,
        in_specs=in_specs,
        out_specs=[VMEM] * len(outs),
        scratch_shapes=scratch,
        compiler_params=pltpu.CompilerParams(vmem_limit_bytes=limit),
        cost_estimate=pl.CostEstimate(flops=flops, bytes_accessed=nbytes, transcendentals=0),
    )


def dot(a, b):
    return jnp.dot(a, b, preferred_element_type=f32)


def dot_nt(a, b):
    return lax.dot_general(a, b, (((1,), (1,)), ((), ())), preferred_element_type=f32)


def gelu(x):
    return 0.5 * x * (1.0 + lax.erf(x * 0.7071067811865476))


def split3(x):
    hi = x.astype(bf16)
    rest = x - hi.astype(f32)
    mid = rest.astype(bf16)
    return hi, mid, (rest - mid.astype(f32)).astype(bf16)


def blank_kernel(out_ref):
    out_ref[...] = jnp.full(out_ref.shape, -1.0, f32)


def pack_kernel(pos_ref, ids_ref, key_ref, dw_ref, blank_ref, tail_ref, w_ref, line):
    section = pos_ref[3]
    keys, depth = key_ref.shape
    shard_rows, width = ids_ref.shape[1:]
    line[...] = blank_ref[...]
    for i in range(ids_ref.shape[0]):
        line[i * shard_rows : (i + 1) * shard_rows, 0:width] = ids_ref[i].astype(f32)
    tail_ref[...] = jnp.zeros(tail_ref.shape, bf16)
    tail_ref[:, depth : depth + LANES] = line[...].astype(bf16)
    tail_ref[0 : keys // 2, 0:depth] = key_ref[pl.ds(pl.multiple_of(section * (keys // 2), keys // 2), keys // 2), :]
    half = w_ref.shape[1]
    lanes = pl.ds(pl.multiple_of(section * half, LANES), half)
    for dy in range(7):
        w_ref[dy * 7 : dy * 7 + 7, :] = dw_ref[dy, :, lanes].astype(f32)


def join_kernel(*refs):
    start = 0
    for ref in refs[:-1]:
        refs[-1][start : start + ref.shape[0], :] = ref[...]
        start += ref.shape[0]


def join(*arrays):
    rows = sum(x.shape[0] for x in arrays)
    shape = jax.ShapeDtypeStruct((rows, arrays[0].shape[1]), arrays[0].dtype)
    joined = call(join_kernel, [shape], [VMEM] * len(arrays), [], 1 << 20, 0, rows * 1024)(*arrays)
    return joined[0]


def add_kernel(a_ref, b_ref, out_ref, send_ref):
    out_ref[...] = a_ref[...] + b_ref[...]
    send_ref[...] = out_ref[...].astype(bf16)


def conv_kernel(geo, pos_ref, *refs):
    shards, shard_rows, width, out_rows, first_lane = geo
    blocks = refs[:shards]
    w_ref, taps, img_ref, xpad, wide = refs[shards:]
    chunk = taps.shape[1]
    row, first_row, col0 = pos_ref[0], pos_ref[1], pos_ref[2]
    height = shards * shard_rows
    pixels = shard_rows * width
    cols = xpad.shape[1]
    out_pixels = out_rows * width
    step_rows = STRIP

    xpad[0:3] = jnp.zeros((3, cols, LANES), f32)
    xpad[height + 3 : height + 6] = jnp.zeros((3, cols, LANES), f32)
    for y in range(3, height + 3):
        xpad[y, 0:8] = jnp.zeros((8, LANES), f32)
        xpad[y, 8 + width : 16 + width] = jnp.zeros((8, LANES), f32)

    def group(g, carry):
        lanes = pl.ds(pl.multiple_of(g * LANES, LANES), LANES)
        for k in range(shards):
            value = blocks[k][0:pixels, lanes].astype(f32).reshape(shard_rows, width, LANES)
            xpad[pl.ds(3 + (row ^ k) * shard_rows, shard_rows), 8 : 8 + width, :] = value
        for t in range(49):
            w = w_ref[t : t + 1, pl.ds(pl.multiple_of(first_lane + g * LANES, LANES), LANES)]
            wide[t] = jnp.broadcast_to(w, (8, LANES))

        def strip(i, carry):
            top = first_row + i * step_rows
            acc = [jnp.zeros((width // 8, 8, LANES), f32) for _ in range(step_rows)]
            for r in range(step_rows + 6):
                for dx in range(7):
                    v = xpad[top + r, pl.ds(col0 + dx, width), :].reshape(width // 8, 8, LANES)
                    for j in range(step_rows):
                        dy = r - j
                        if 0 <= dy < 7:
                            acc[j] = acc[j] + v * wide[dy * 7 + dx][None]
            for j in range(step_rows):
                start = pl.multiple_of((i * step_rows + j) * width, width)
                taps[pl.ds(start, width), lanes] = acc[j].reshape(width, LANES)
            return carry

        return lax.fori_loop(0, out_rows // step_rows, strip, carry)

    lax.fori_loop(0, chunk // LANES, group, 0)

    for k in range(shards):
        start = (row ^ k) * pixels - first_row * width

        @pl.when((start >= 0) & (start < out_pixels))
        def _():
            img_ref[pl.ds(pl.multiple_of(start, pixels), pixels), :] = blocks[k][0:pixels, :]


def block_kernel(geo, pos_ref, *refs):
    first, pixels, chunks = geo
    own, other, img = refs[:chunks], refs[chunks : 2 * chunks], refs[2 * chunks : 3 * chunks]
    gain_ref, scale_ref, w1_ref, w2_ref, z_ref, normed, inner = refs[3 * chunks :]
    chans, hid = w1_ref.shape
    half = chans // 2
    width = half // chunks
    section = pos_ref[3]
    rows = slice(first, first + pixels)
    values = [ref[rows, :] for ref in own + other]
    mean = sum(jnp.sum(v, axis=1, keepdims=True) for v in values) * (1.0 / chans)
    values = [v - mean for v in values]
    spread = sum(jnp.sum(v * v, axis=1, keepdims=True) for v in values) * (1.0 / chans)
    inv = lax.rsqrt(spread + ln_eps)
    gains = gain_ref[...].astype(f32).reshape(1, chans)
    scales = scale_ref[...].astype(f32).reshape(1, chans)
    for c in range(chunks):
        lanes = slice(c * width, (c + 1) * width)
        for side, v in ((section, values[c]), (1 - section, values[chunks + c])):
            start = c * width
            gain = jnp.where(side == 0, gains[:, start : start + width], gains[:, half + start : half + start + width])
            normed[pl.ds(side, 1), :, lanes] = (v * inv * gain).astype(bf16)[None]
    step = 256

    def widen(i):
        cols = slice(i * step, (i + 1) * step)
        return dot(normed[0], w1_ref[0:half, cols]) + dot(normed[1], w1_ref[half:chans, cols])

    ahead = widen(0)
    for i in range(hid // step):
        h = ahead
        if i + 1 < hid // step:
            ahead = widen(i + 1)
        inner[:, i * step : (i + 1) * step] = gelu(h).astype(bf16)
    step = width if width % 256 else 256

    def narrow(i):
        return dot(inner[...], w2_ref[:, i * step : (i + 1) * step])

    ahead = narrow(0)
    for i in range(chans // step):
        z = ahead
        if i + 1 < chans // step:
            ahead = narrow(i + 1)
        cols = slice(i * step, (i + 1) * step)
        side, start = divmod(i * step, half)
        c, start = divmod(start, width)
        keep = jnp.where(section == side, 1.0, 0.0)
        z_ref[:, cols] = z * scales[:, cols] + img[c][rows, start : start + step].astype(f32) * keep


def expand_kernel(z_ref, other_ref, pe_ref, out_ref, block):
    block[...] = (z_ref[...] + other_ref[...]).astype(bf16)
    step = 256
    for i in range(pe_ref.shape[1] // step):
        cols = slice(i * step, (i + 1) * step)
        out_ref[:, cols] = jnp.maximum(dot(block[...], pe_ref[:, cols]), 0.0).astype(bf16)


def prep_kernel(geo, pos_ref, *refs):
    shards, shard_rows, width, out_pixels, per_key, parts = geo
    ids = refs[:shards]
    hot_ref, keys_ref, flat = refs[shards:]
    row, first_row = pos_ref[0], pos_ref[1]
    pixels = shard_rows * width
    depth = keys_ref.shape[1]
    for k in range(shards):
        mine = slice(k * per_key // 2, (k + 1) * per_key // 2)
        keys_ref[mine, :] = ids[k][pixels : pixels + per_key // 2, 0:depth]
    ids = [ref[pixels:, depth : depth + LANES].astype(f32) for ref in ids]
    image = row // parts
    flat[...] = jnp.full(flat.shape, -1.0, f32)
    for k in range(shards):
        start = pl.multiple_of((1 + (row ^ k)) * pixels, LANES)
        number = lax.broadcasted_iota(jnp.int32, ids[k].shape, 0)
        inside = lax.broadcasted_iota(jnp.int32, ids[k].shape, 1) < width
        for y in range(shard_rows):
            keep = inside & (number == image * shard_rows + y)
            mine = jnp.sum(jnp.where(keep, ids[k], 0.0), axis=0, keepdims=True)
            mine = jnp.broadcast_to(mine, (8, LANES))
            mine = pltpu.roll(mine, y * width, 1) if y else mine
            line = mine if y == 0 else line + mine
        flat[0:8, pl.ds(start, pixels)] = line
    total = flat.shape[1]
    whole = jnp.broadcast_to(flat[0:1, :], (8, total))
    lane = lax.broadcasted_iota(jnp.int32, (8, total), 1)
    col = lane % width
    region = lax.broadcasted_iota(jnp.int32, (REG, out_pixels), 0).astype(f32)
    start = pl.multiple_of(pixels + first_row * width, LANES)
    for dy in range(3):
        for dx in range(3):
            off = (dy - 1) * width + dx - 1
            moved = whole if off == 0 else pltpu.roll(whole, off % total, 1)
            if dx == 0:
                moved = jnp.where(col == width - 1, -1.0, moved)
            if dx == 2:
                moved = jnp.where(col == 0, -1.0, moved)
            flat[8:16, :] = moved
            line = flat[8:9, pl.ds(start, out_pixels)]
            tap = dy * 3 + dx
            hot_ref[tap * REG : (tap + 1) * REG, :] = jnp.where(region == line, 1.0, 0.0).astype(bf16)


def owner_kernel(geo, pos_ref, *refs):
    shards, shard_rows, pixels, images, batches, per_key = geo
    ids = refs[:shards]
    owner_ref, partner_ref, pick_ref, own_ref = refs[shards:]
    row, batch, first_slot = pos_ref[0], pos_ref[4], pos_ref[5]
    depth = ids[0].shape[1] - LANES
    ids = [ref[pixels:, depth : depth + LANES].astype(f32) for ref in ids]
    owned, slots = pick_ref.shape
    slot = lax.broadcasted_iota(jnp.int32, (owned, slots), 1)
    want = lax.broadcasted_iota(jnp.int32, (owned, slots), 0) + first_slot
    pick = owner_ref[...] == want
    pick_ref[...] = jnp.where(pick, 1.0, 0.0).astype(bf16)
    one_region = lax.broadcasted_iota(jnp.int32, (REG, LANES), 0).astype(f32)
    tallies = []
    for i in range(images):
        tally = jnp.zeros((REG, LANES), f32)
        for k in range(shards):
            for y in range(i * shard_rows, (i + 1) * shard_rows):
                tally = tally + jnp.where(one_region == ids[k][y : y + 1, :], 1.0, 0.0)
        tallies.append(tally)
    tally = jnp.concatenate(tallies, axis=0).astype(bf16)
    count = dot_nt(jnp.ones((8, LANES), bf16), tally)[0:1]
    mates = jnp.concatenate([partner_ref[i : i + 1, :] for i in range(images)], axis=1)
    mate = (batch * images + slot // REG) * REG + mates
    block = mate // per_key
    within = mate % per_key
    core = (within // (per_key // 2)) ^ pos_ref[3]
    apart = (block // shards) ^ batch
    turn = core
    for n in range(batches.bit_length() - 1):
        turn = turn * 2 + ((apart >> n) & 1)
    place = turn * shards + ((block % shards) ^ row)
    place = place * (per_key // 2) + within % (per_key // 2)
    place = jnp.sum(jnp.where(pick, place, 0).astype(f32), axis=1, keepdims=True)
    number = jnp.sum(jnp.where(pick, count, 0.0), axis=1, keepdims=True)
    side = lax.broadcasted_iota(jnp.int32, (owned, LANES), 1)
    own_ref[...] = jnp.where(side == 0, place, jnp.where(side == 1, number, 0.0))


def project_kernel(z_ref, other_ref, first_ref, pe_ref, pk_ref, hot_ref, out_ref, block, hidden):
    before = first_ref.shape[0]
    pixels = z_ref.shape[0]
    taps = pk_ref.shape[0]
    block[...] = (z_ref[...] + other_ref[...]).astype(bf16)
    step = 256
    acc = jnp.zeros((2 * REG, out_ref.shape[1]), f32)
    for i in range(pe_ref.shape[1] // step):
        cols = slice(i * step, (i + 1) * step)
        hidden[i, 0:before, :] = first_ref[:, cols]
        h = jnp.maximum(dot(block[...], pe_ref[:, cols]), 0.0)
        hidden[i, before : before + pixels, :] = h.astype(bf16)
        sums = dot(hot_ref[...], hidden[i])
        hi = sums.astype(bf16)
        lo = (sums - hi.astype(f32)).astype(bf16)
        for t in range(taps):
            rows = slice(t * REG, (t + 1) * REG)
            both = jnp.concatenate([hi[rows], lo[rows]], axis=0)
            acc = acc + dot(both, pk_ref[t, cols, :])
    out_ref[...] = acc[0:REG] + acc[REG:]


def keys_kernel(*refs):
    keys_ref, length_ref = refs[-2:]
    start = 0
    for ref in refs[:-2]:
        keys_ref[start : start + ref.shape[0], :] = ref[...]
        start += ref.shape[0]
    keys = keys_ref[...].astype(f32)
    square = keys * keys
    hi = square.astype(bf16)
    lo = (square - hi.astype(f32)).astype(bf16)
    ones = jnp.ones((16, keys.shape[1]), bf16)
    length_ref[...] = lax.rsqrt(dot_nt(ones, hi)[0:1] + dot_nt(ones, lo)[0:1] + norm_eps)


def loss_kernel(geo, *refs):
    shards, parts = geo
    sums, row = refs[1 : shards + 1], refs[0][0]
    pick_ref, own_ref, keys_ref, length_ref, embed_ref, loss_ref, table = refs[shards + 1 :]
    if parts > 1:
        table[...] = jnp.zeros(table.shape, f32)
    for k in range(shards):
        place = pl.ds(pl.multiple_of(((row ^ k) // parts) * REG, REG), REG)
        value = sums[k][...].astype(f32)
        table[place, :] = value if parts == 1 else table[place, :] + value
    pick = pick_ref[...]
    hi, mid, lo = split3(table[...])
    ordered = dot(pick, hi) + dot(pick, mid) + dot(pick, lo)
    unit = ordered * lax.rsqrt(jnp.sum(ordered * ordered, axis=1, keepdims=True) + norm_eps)
    embed_ref[...] = unit
    owned = unit.shape[0]
    three = dot_nt(jnp.concatenate(split3(unit), axis=0), keys_ref[...])
    logits = three[0:owned] + three[owned : 2 * owned] + three[2 * owned :]
    logits = logits * (length_ref[...] / sharpness_divisor)
    total = jnp.log(jnp.sum(jnp.exp(logits), axis=1, keepdims=True))
    column = lax.broadcasted_iota(jnp.int32, logits.shape, 1).astype(f32)
    match = jnp.sum(jnp.where(column == own_ref[:, 0:1], logits, 0.0), axis=1, keepdims=True)
    loss = jnp.where(own_ref[:, 1:2] > 0.5, total - match, 0.0)
    line = lax.broadcasted_iota(jnp.int32, (owned, owned), 0)
    other = lax.broadcasted_iota(jnp.int32, (owned, owned), 1)
    loss_ref[...] = jnp.sum(jnp.where(line == other, loss, 0.0), axis=0, keepdims=True)


def swap(x, axis, bit):
    return lax.ppermute(x, axis, [(i, i ^ bit) for i in range(lax.axis_size(axis))])


def body(
    features,
    dw_kernel,
    ln_gain,
    widening_pointwise_matrix,
    w_reduce,
    layer_branch_scale,
    p_expand,
    p_kernel,
    region_ids,
    owner_slot,
    partner,
    key_embed,
):
    images, shard_rows, width, chans = features.shape
    shards = lax.axis_size("rows")
    batches = lax.axis_size("batch")
    row = lax.axis_index("rows")
    batch = lax.axis_index("batch")
    section = lax.axis_index("section")
    half = chans // lax.axis_size("section")
    parts = shards // images
    out_rows = shards * shard_rows // parts
    pixels = shard_rows * width
    out_pixels = out_rows * width
    slots = images * REG
    owned = slots // shards
    out_dim = p_kernel.shape[2]
    mib = 1 << 20
    span = half // CHUNKS

    w1, w2, pe, pk = widening_pointwise_matrix, w_reduce, p_expand, p_kernel
    first_row = (row % parts) * out_rows
    spot = jnp.stack(
        [row, first_row, jnp.int32(5), section, batch, row * owned]
    ).astype(jnp.int32)

    per_key, depth = key_embed.shape
    tail = max(-(-images * shard_rows // 16) * 16, per_key // 2)
    def after(here, *done):
        return lax.optimization_barrier((here, *done))[0]

    (blank,) = call(
        blank_kernel, [jax.ShapeDtypeStruct((tail, LANES), f32)], [], [], mib, 10**10, 10**4
    )()
    riders, weights = call(
        pack_kernel,
        [jax.ShapeDtypeStruct((tail, span), bf16), jax.ShapeDtypeStruct((49, half), f32)],
        [SMEM] + [VMEM] * 4,
        [pltpu.VMEM((tail, LANES), f32)],
        mib,
        0,
        10**6,
    )(spot, region_ids, key_embed, dw_kernel, blank)
    got = []
    for c in range(CHUNKS):
        blocks = []
        for k in range(shards):
            place = ((row ^ k) // parts, 0, 0, section * half + c * span)
            part = lax.dynamic_slice(features, place, (1, shard_rows, width, span)).reshape(pixels, span)
            if c == CHUNKS - 1:
                part = jnp.concatenate([part, riders], axis=0)
            blocks.append(part)
        got.append([blocks[0]] + [swap(blocks[k], "rows", k) for k in range(1, shards)])

    own, other, img = [], [], []
    for c in range(CHUNKS):
        here = after(spot, *own) if c else spot
        taps, image = call(
            functools.partial(conv_kernel, (shards, shard_rows, width, out_rows, c * span)),
            [
                jax.ShapeDtypeStruct((out_pixels, span), f32),
                jax.ShapeDtypeStruct((out_pixels, span), bf16),
            ],
            [SMEM] + [VMEM] * (shards + 1),
            [
                pltpu.VMEM((shards * shard_rows + 6, width + 16, LANES), f32),
                pltpu.VMEM((49, 8, LANES), f32),
            ],
            3 * mib,
            out_pixels * span * 98 * 100,
            out_pixels * span * 10,
        )(here, *got[c], weights)
        own.append(taps)
        img.append(image)
        other.append(swap(taps, "section", 1))

    hot, keys = call(
        functools.partial(prep_kernel, (shards, shard_rows, width, out_pixels, per_key, parts)),
        [
            jax.ShapeDtypeStruct((9 * REG, out_pixels), bf16),
            jax.ShapeDtypeStruct((shards * per_key // 2, depth), bf16),
        ],
        [SMEM] + [VMEM] * shards,
        [pltpu.VMEM((16, (shards + 2) * pixels), f32)],
        2 * mib,
        10**8,
        10**6,
    )(after(spot, *own), *got[-1])
    bits = [1 << n for n in reversed(range(batches.bit_length() - 1))]
    pieces = [keys, swap(keys, "batch", bits[0])]

    hid = w1.shape[1]
    part_pixels = out_pixels // 2
    z, z_other = [], []
    for p in range(2):
        here = after(spot, pieces[-1], *z) if p else after(spot, hot)
        (mine,) = call(
            functools.partial(block_kernel, (p * part_pixels, part_pixels, CHUNKS)),
            [jax.ShapeDtypeStruct((part_pixels, chans), f32)],
            [SMEM] + [VMEM] * (3 * CHUNKS + 4),
            [pltpu.VMEM((2, part_pixels, half), bf16), pltpu.VMEM((part_pixels, hid), bf16)],
            8 * mib,
            4 * part_pixels * hid * chans,
            4 * hid * chans,
        )(here, *own, *other, *img, ln_gain, layer_branch_scale, w1, w2)
        z.append(mine)
        z_other.append(swap(mine, "section", 1))
    for bit in bits[1:]:
        pieces.append(swap(join(*pieces), "batch", bit))

    hidden = pe.shape[1]
    (hid_a,) = call(
        expand_kernel,
        [jax.ShapeDtypeStruct((part_pixels, hidden), bf16)],
        [VMEM] * 3,
        [pltpu.VMEM((part_pixels, chans), bf16)],
        6 * mib,
        2 * part_pixels * hidden * chans,
        2 * hidden * chans,
    )(z[0], z_other[0], pe)
    (pooled,) = call(
        project_kernel,
        [jax.ShapeDtypeStruct((REG, out_dim), f32)],
        [VMEM] * 6,
        [
            pltpu.VMEM((part_pixels, chans), bf16),
            pltpu.VMEM((hidden // 256, out_pixels, 256), bf16),
        ],
        8 * mib,
        2 * part_pixels * hidden * chans + 4 * 9 * REG * hidden * out_pixels,
        4 * hidden * chans,
    )(z[1], z_other[1], hid_a, pe, pk, hot)
    pick, facts = call(
        functools.partial(owner_kernel, (shards, shard_rows, pixels, images, batches, per_key)),
        [jax.ShapeDtypeStruct((owned, slots), bf16), jax.ShapeDtypeStruct((owned, LANES), f32)],
        [SMEM] + [VMEM] * (shards + 2),
        [],
        2 * mib,
        10**8,
        10**6,
    )(after(spot, pooled), *got[-1], owner_slot, partner)
    total, send = call(
        add_kernel,
        [jax.ShapeDtypeStruct((REG, out_dim), f32), jax.ShapeDtypeStruct((REG, out_dim), bf16)],
        [VMEM] * 2,
        [],
        mib,
        10**5,
        10**5,
    )(pooled, swap(pooled, "section", 1))
    sums = [total] + [swap(send, "rows", k) for k in range(1, shards)]
    pieces[-1] = after(pieces[-1], pooled)
    pieces.append(swap(join(*pieces), "section", 1))
    count = sum(x.shape[0] for x in pieces)
    keys, length = call(
        keys_kernel,
        [jax.ShapeDtypeStruct((count, depth), bf16), jax.ShapeDtypeStruct((1, count), f32)],
        [VMEM] * len(pieces),
        [],
        4 * mib,
        10**9,
        10**6,
    )(*pieces)

    embed, loss = call(
        functools.partial(loss_kernel, (shards, parts)),
        [jax.ShapeDtypeStruct((owned, out_dim), f32), jax.ShapeDtypeStruct((1, owned), f32)],
        [SMEM] + [VMEM] * (shards + 4),
        [pltpu.VMEM((slots, out_dim), f32)],
        6 * mib,
        10**8,
        10**6,
    )(spot, *sums, pick, facts, keys, length)
    return embed, loss.reshape(owned)


def solution(mesh):
    in_specs = (
        P("batch", "rows", None, None),
        P(),
        P(),
        P(None, "section"),
        P("section", None),
        P(),
        P(None, "section"),
        P(None, "section", None),
        P("batch", "rows", None),
        P("batch", None),
        P("batch", None),
        P(("batch", "rows"), None),
    )
    out_specs = (P(("batch", "rows"), None), P(("batch", "rows")))
    return jax.shard_map(body, mesh=mesh, in_specs=in_specs, out_specs=out_specs, check_vma=False)
```

```python
import functools

import jax
import jax.numpy as jnp
from jax import lax
from jax.experimental import pallas as pl
from jax.experimental.pallas import tpu as pltpu
from jax.sharding import PartitionSpec as P

REG = 64
LANES = 128
STRIP = 4
CHUNKS = 2

sharpness_divisor = 0.1
ln_eps = 1e-06
norm_eps = 1e-06

VMEM = pl.BlockSpec(memory_space=pltpu.VMEM)
SMEM = pl.BlockSpec(memory_space=pltpu.SMEM)
f32 = jnp.float32
bf16 = jnp.bfloat16


def call(kernel, outs, in_specs, scratch, limit, flops, nbytes):
    return pl.pallas_call(
        kernel,
        out_shape=outs,
        in_specs=in_specs,
        out_specs=[VMEM] * len(outs),
        scratch_shapes=scratch,
        compiler_params=pltpu.CompilerParams(vmem_limit_bytes=limit),
        cost_estimate=pl.CostEstimate(flops=flops, bytes_accessed=nbytes, transcendentals=0),
    )


def dot(a, b):
    return jnp.dot(a, b, preferred_element_type=f32)


def dot_nt(a, b):
    return lax.dot_general(a, b, (((1,), (1,)), ((), ())), preferred_element_type=f32)


def gelu(x):
    return 0.5 * x * (1.0 + lax.erf(x * 0.7071067811865476))


def split(x):
    hi = x.astype(bf16)
    return hi, (x - hi.astype(f32)).astype(bf16)


def blank_kernel(pos_ref, out_ref):
    out_ref[...] = jnp.full(out_ref.shape, -1.0, f32)


def pack_kernel(pos_ref, ids_ref, key_ref, blank_ref, tail_ref, line):
    section = pos_ref[3]
    keys, depth = key_ref.shape
    shard_rows, width = ids_ref.shape[1:]
    line[...] = blank_ref[...]
    for i in range(ids_ref.shape[0]):
        line[i * shard_rows : (i + 1) * shard_rows, 0:width] = ids_ref[i].astype(f32)
    tail_ref[...] = jnp.zeros(tail_ref.shape, bf16)
    tail_ref[:, depth : depth + LANES] = line[...].astype(bf16)
    tail_ref[0 : keys // 2, 0:depth] = key_ref[pl.ds(pl.multiple_of(section * (keys // 2), keys // 2), keys // 2), :]


def join_kernel(*refs):
    start = 0
    for ref in refs[:-1]:
        refs[-1][start : start + ref.shape[0], :] = ref[...]
        start += ref.shape[0]


def join(*arrays):
    rows = sum(x.shape[0] for x in arrays)
    shape = jax.ShapeDtypeStruct((rows, arrays[0].shape[1]), arrays[0].dtype)
    joined = call(join_kernel, [shape], [VMEM] * len(arrays), [], 1 << 20, 0, rows * 1024)(*arrays)
    return joined[0]


def add_kernel(a_ref, b_ref, out_ref, send_ref):
    out_ref[...] = a_ref[...] + b_ref[...]
    send_ref[...] = out_ref[...].astype(bf16)


def conv_kernel(geo, pos_ref, *refs):
    order, shard_rows, width, out_rows, first_lane = geo
    shards = len(order)
    blocks = dict(zip(order, refs[:shards]))
    w_ref, taps, img_ref, xpad, wide = refs[shards:]
    chunk = taps.shape[1]
    row, first_row, col0 = pos_ref[0], pos_ref[1], pos_ref[2]
    height = shards * shard_rows
    pixels = shard_rows * width
    cols = xpad.shape[1]
    out_pixels = out_rows * width
    step_rows = STRIP

    xpad[0:3] = jnp.zeros((3, cols, LANES), f32)
    xpad[height + 3 : height + 6] = jnp.zeros((3, cols, LANES), f32)
    for y in range(3, height + 3):
        xpad[y, 0:8] = jnp.zeros((8, LANES), f32)
        xpad[y, 8 + width : 16 + width] = jnp.zeros((8, LANES), f32)

    def group(g, carry):
        lanes = pl.ds(pl.multiple_of(g * LANES, LANES), LANES)
        for k in range(shards):
            value = blocks[k][0:pixels, lanes].astype(f32).reshape(shard_rows, width, LANES)
            xpad[pl.ds(3 + (row ^ k) * shard_rows, shard_rows), 8 : 8 + width, :] = value
        start = pos_ref[3] * (w_ref.shape[2] // 2) + first_lane + g * LANES
        for dy in range(7):
            w = w_ref[dy, :, pl.ds(pl.multiple_of(start, LANES), LANES)].astype(f32)
            for dx in range(7):
                wide[dy * 7 + dx] = jnp.broadcast_to(w[dx : dx + 1], (8, LANES))

        def strip(i, carry):
            top = first_row + i * step_rows
            acc = [jnp.zeros((width // 8, 8, LANES), f32) for _ in range(step_rows)]
            for r in range(step_rows + 6):
                for dx in range(7):
                    v = xpad[top + r, pl.ds(col0 + dx, width), :].reshape(width // 8, 8, LANES)
                    for j in range(step_rows):
                        dy = r - j
                        if 0 <= dy < 7:
                            acc[j] = acc[j] + v * wide[dy * 7 + dx][None]
            for j in range(step_rows):
                start = pl.multiple_of((i * step_rows + j) * width, width)
                taps[pl.ds(start, width), lanes] = acc[j].reshape(width, LANES)
            return carry

        return lax.fori_loop(0, out_rows // step_rows, strip, carry)

    lax.fori_loop(0, chunk // LANES, group, 0)

    for k in range(shards):
        start = (row ^ k) * pixels - first_row * width

        @pl.when((start >= 0) & (start < out_pixels))
        def _():
            img_ref[pl.ds(pl.multiple_of(start, pixels), pixels), :] = blocks[k][0:pixels, :]


def block_kernel(geo, pos_ref, *refs):
    first, pixels, chunks = geo
    own, other, img = refs[:chunks], refs[chunks : 2 * chunks], refs[2 * chunks : 3 * chunks]
    gain_ref, scale_ref, w1_ref, w2_ref, z_ref, normed, inner = refs[3 * chunks :]
    chans, hid = w1_ref.shape
    half = chans // 2
    width = half // chunks
    section = pos_ref[3]
    rows = slice(first, first + pixels)
    gains = gain_ref[...].astype(f32).reshape(1, chans)
    scales = scale_ref[...].astype(f32).reshape(1, chans)
    gains = [gains[:, n * width : (n + 1) * width] for n in range(2 * chunks)]
    gains_own = [jnp.where(section == 0, gains[c], gains[chunks + c]) for c in range(chunks)]
    gains_other = [jnp.where(section == 0, gains[chunks + c], gains[c]) for c in range(chunks)]
    block = 32
    for r in range(pixels // block):
        part = slice(first + r * block, first + (r + 1) * block)
        values = [ref[part, :] for ref in own + other]
        mean = sum(jnp.sum(v, axis=1, keepdims=True) for v in values) * (1.0 / chans)
        values = [v - mean for v in values]
        spread = sum(jnp.sum(v * v, axis=1, keepdims=True) for v in values) * (1.0 / chans)
        inv = lax.rsqrt(spread + ln_eps)
        values = [(v * inv * g).astype(bf16) for v, g in zip(values, gains_own + gains_other)]
        to = slice(r * block, (r + 1) * block)
        for c in range(chunks):
            lanes = slice(c * width, (c + 1) * width)
            normed[pl.ds(section, 1), to, lanes] = values[c][None]
            normed[pl.ds(1 - section, 1), to, lanes] = values[chunks + c][None]
    step = 256

    def widen(i):
        cols = slice(i * step, (i + 1) * step)
        return dot(normed[0], w1_ref[0:half, cols]) + dot(normed[1], w1_ref[half:chans, cols])

    ahead = widen(0)
    for i in range(hid // step):
        h = ahead
        if i + 1 < hid // step:
            ahead = widen(i + 1)
        inner[:, i * step : (i + 1) * step] = gelu(h).astype(bf16)
    step = width if width % 256 else 256

    def narrow(i):
        return dot(inner[...], w2_ref[:, i * step : (i + 1) * step])

    ahead = narrow(0)
    for i in range(chans // step):
        z = ahead
        if i + 1 < chans // step:
            ahead = narrow(i + 1)
        cols = slice(i * step, (i + 1) * step)
        side, start = divmod(i * step, half)
        c, start = divmod(start, width)
        keep = jnp.where(section == side, 1.0, 0.0)
        z_ref[:, cols] = z * scales[:, cols] + img[c][rows, start : start + step].astype(f32) * keep


def expand_kernel(z_ref, other_ref, pe_ref, out_ref, block):
    block[...] = (z_ref[...] + other_ref[...]).astype(bf16)
    step = 256
    for i in range(pe_ref.shape[1] // step):
        cols = slice(i * step, (i + 1) * step)
        out_ref[:, cols] = jnp.maximum(dot(block[...], pe_ref[:, cols]), 0.0).astype(bf16)


def prep_kernel(geo, pos_ref, *refs):
    order, shard_rows, width, out_pixels, parts = geo
    shards = len(order)
    ids = [refs[order.index(k)] for k in range(shards)]
    hot_ref, flat = refs[shards:]
    row, first_row = pos_ref[0], pos_ref[1]
    pixels = shard_rows * width
    depth = ids[0].shape[1] - LANES
    ids = [ref[pixels:, depth : depth + LANES].astype(f32) for ref in ids]
    image = row // parts
    flat[...] = jnp.full(flat.shape, -1.0, f32)
    for k in range(shards):
        start = pl.multiple_of((1 + (row ^ k)) * pixels, LANES)
        number = lax.broadcasted_iota(jnp.int32, ids[k].shape, 0)
        inside = lax.broadcasted_iota(jnp.int32, ids[k].shape, 1) < width
        for y in range(shard_rows):
            keep = inside & (number == image * shard_rows + y)
            mine = jnp.sum(jnp.where(keep, ids[k], 0.0), axis=0, keepdims=True)
            mine = jnp.broadcast_to(mine, (8, LANES))
            mine = pltpu.roll(mine, y * width, 1) if y else mine
            line = mine if y == 0 else line + mine
        flat[0:8, pl.ds(start, pixels)] = line
    total = flat.shape[1]
    whole = jnp.broadcast_to(flat[0:1, :], (8, total))
    lane = lax.broadcasted_iota(jnp.int32, (8, total), 1)
    col = lane % width
    region = lax.broadcasted_iota(jnp.int32, (REG, out_pixels), 0).astype(f32)
    start = pl.multiple_of(pixels + first_row * width, LANES)
    for dy in range(3):
        for dx in range(3):
            off = (dy - 1) * width + dx - 1
            moved = whole if off == 0 else pltpu.roll(whole, off % total, 1)
            if dx == 0:
                moved = jnp.where(col == width - 1, -1.0, moved)
            if dx == 2:
                moved = jnp.where(col == 0, -1.0, moved)
            flat[8:16, :] = moved
            line = flat[8:9, pl.ds(start, out_pixels)]
            tap = dy * 3 + dx
            hot_ref[tap * REG : (tap + 1) * REG, :] = jnp.where(region == line, 1.0, 0.0).astype(bf16)


def unpack_kernel(geo, *refs):
    order, pixels = geo
    keys_ref = refs[-1]
    count = keys_ref.shape[0] // len(order)
    for k, ref in zip(order, refs):
        keys_ref[k * count : (k + 1) * count, :] = ref[pixels : pixels + count, 0 : keys_ref.shape[1]]


def owner_kernel(geo, pos_ref, *refs):
    order, shard_rows, pixels, images, batches, per_key = geo
    shards = len(order)
    ids = [refs[order.index(k)] for k in range(shards)]
    owner_ref, partner_ref, pick_ref, own_ref = refs[shards:]
    row, batch, first_slot = pos_ref[0], pos_ref[4], pos_ref[5]
    depth = ids[0].shape[1] - LANES
    ids = [ref[pixels:, depth : depth + LANES].astype(f32) for ref in ids]
    owned, slots = pick_ref.shape
    slot = lax.broadcasted_iota(jnp.int32, (owned, slots), 1)
    want = lax.broadcasted_iota(jnp.int32, (owned, slots), 0) + first_slot
    pick = owner_ref[...] == want
    pick_ref[...] = jnp.where(pick, 1.0, 0.0).astype(bf16)
    one_region = lax.broadcasted_iota(jnp.int32, (REG, LANES), 0).astype(f32)
    tallies = []
    for i in range(images):
        tally = jnp.zeros((REG, LANES), f32)
        for k in range(shards):
            for y in range(i * shard_rows, (i + 1) * shard_rows):
                tally = tally + jnp.where(one_region == ids[k][y : y + 1, :], 1.0, 0.0)
        tallies.append(tally)
    tally = jnp.concatenate(tallies, axis=0).astype(bf16)
    count = dot_nt(jnp.ones((8, LANES), bf16), tally)[0:1]
    mates = jnp.concatenate([partner_ref[i : i + 1, :] for i in range(images)], axis=1)
    mate = (batch * images + slot // REG) * REG + mates
    block = mate // per_key
    within = mate % per_key
    core = (within // (per_key // 2)) ^ pos_ref[3]
    apart = (block // shards) ^ batch
    turn = core
    for n in range(batches.bit_length() - 1):
        turn = turn * 2 + ((apart >> n) & 1)
    place = turn * shards + ((block % shards) ^ row)
    place = place * (per_key // 2) + within % (per_key // 2)
    place = jnp.sum(jnp.where(pick, place, 0).astype(f32), axis=1, keepdims=True)
    number = jnp.sum(jnp.where(pick, count, 0.0), axis=1, keepdims=True)
    side = lax.broadcasted_iota(jnp.int32, (owned, LANES), 1)
    own_ref[...] = jnp.where(side == 0, place, jnp.where(side == 1, number, 0.0))


def project_kernel(z_ref, other_ref, first_ref, pe_ref, pk_ref, hot_ref, out_ref, block, hidden):
    before = first_ref.shape[0]
    pixels = z_ref.shape[0]
    taps = pk_ref.shape[0]
    block[...] = (z_ref[...] + other_ref[...]).astype(bf16)
    step = 256
    acc = jnp.zeros((2 * REG, out_ref.shape[1]), f32)
    for i in range(pe_ref.shape[1] // step):
        cols = slice(i * step, (i + 1) * step)
        hidden[i, 0:before, :] = first_ref[:, cols]
        h = jnp.maximum(dot(block[...], pe_ref[:, cols]), 0.0)
        hidden[i, before : before + pixels, :] = h.astype(bf16)
        sums = dot(hot_ref[...], hidden[i])
        hi = sums.astype(bf16)
        lo = (sums - hi.astype(f32)).astype(bf16)
        for t in range(taps):
            rows = slice(t * REG, (t + 1) * REG)
            both = jnp.concatenate([hi[rows], lo[rows]], axis=0)
            acc = acc + dot(both, pk_ref[t, cols, :])
    out_ref[...] = acc[0:REG] + acc[REG:]


def keys_kernel(*refs):
    keys_ref, length_ref = refs[-2:]
    keys = jnp.concatenate([ref[...] for ref in refs[:-2]], axis=0).astype(f32).T
    keys_ref[...] = keys.astype(bf16)
    length_ref[...] = lax.rsqrt(jnp.sum(keys * keys, axis=0, keepdims=True) + norm_eps)


def loss_kernel(geo, *refs):
    order, parts = geo
    shards = len(order)
    sums, row = dict(zip(order, refs[1 : shards + 1])), refs[0][0]
    pick_ref, own_ref, keys_ref, length_ref, embed_ref, loss_ref, table = refs[shards + 1 :]
    if parts > 1:
        table[...] = jnp.zeros(table.shape, f32)
    for k in range(shards):
        place = pl.ds(pl.multiple_of(((row ^ k) // parts) * REG, REG), REG)
        value = sums[k][...].astype(f32)
        table[place, :] = value if parts == 1 else table[place, :] + value
    pick = pick_ref[...]
    hi, lo = split(table[...])
    ordered = dot(pick, hi) + dot(pick, lo)
    unit = ordered * lax.rsqrt(jnp.sum(ordered * ordered, axis=1, keepdims=True) + norm_eps)
    embed_ref[...] = unit
    owned = unit.shape[0]
    both = dot(jnp.concatenate(split(unit), axis=0), keys_ref[...])
    logits = both[0:owned] + both[owned:]
    logits = logits * (length_ref[...] / sharpness_divisor)
    total = jnp.log(jnp.sum(jnp.exp(logits), axis=1, keepdims=True))
    column = lax.broadcasted_iota(jnp.int32, logits.shape, 1).astype(f32)
    match = jnp.sum(jnp.where(column == own_ref[:, 0:1], logits, 0.0), axis=1, keepdims=True)
    loss = jnp.where(own_ref[:, 1:2] > 0.5, total - match, 0.0)
    line = lax.broadcasted_iota(jnp.int32, (owned, owned), 0)
    other = lax.broadcasted_iota(jnp.int32, (owned, owned), 1)
    loss_ref[...] = jnp.sum(jnp.where(line == other, loss, 0.0), axis=0, keepdims=True)


def swap(x, axis, bit):
    return lax.ppermute(x, axis, [(i, i ^ bit) for i in range(lax.axis_size(axis))])


def body(
    features,
    dw_kernel,
    ln_gain,
    widening_pointwise_matrix,
    w_reduce,
    layer_branch_scale,
    p_expand,
    p_kernel,
    region_ids,
    owner_slot,
    partner,
    key_embed,
):
    images, shard_rows, width, chans = features.shape
    shards = lax.axis_size("rows")
    batches = lax.axis_size("batch")
    row = lax.axis_index("rows")
    batch = lax.axis_index("batch")
    section = lax.axis_index("section")
    half = chans // lax.axis_size("section")
    parts = shards // images
    out_rows = shards * shard_rows // parts
    pixels = shard_rows * width
    out_pixels = out_rows * width
    slots = images * REG
    owned = slots // shards
    out_dim = p_kernel.shape[2]
    mib = 1 << 20
    span = half // CHUNKS

    w1, w2, pe, pk = widening_pointwise_matrix, w_reduce, p_expand, p_kernel
    first_row = (row % parts) * out_rows
    spot = jnp.stack(
        [row, first_row, jnp.int32(5), section, batch, row * owned]
    ).astype(jnp.int32)

    per_key, depth = key_embed.shape
    tail = max(-(-images * shard_rows // 16) * 16, per_key // 2)
    def after(here, *done):
        return lax.optimization_barrier((here, *done))[0]

    parcels = []
    for c in range(CHUNKS):
        blocks = []
        for k in range(shards):
            place = ((row ^ k) // parts, 0, 0, section * half + c * span)
            part = lax.dynamic_slice(features, place, (1, shard_rows, width, span))
            blocks.append(part.reshape(pixels, span))
        parcels.append(blocks)
    (blank,) = call(
        blank_kernel, [jax.ShapeDtypeStruct((tail, LANES), f32)], [SMEM], [], mib, 10**10, 10**4
    )(after(spot, *parcels[0]))
    parcels[0] = after(parcels[0], blank)
    (riders,) = call(
        pack_kernel,
        [jax.ShapeDtypeStruct((tail, span), bf16)],
        [SMEM] + [VMEM] * 3,
        [pltpu.VMEM((tail, LANES), f32)],
        mib,
        0,
        10**6,
    )(spot, region_ids, key_embed, blank)
    parcels[-1] = [jnp.concatenate([part, riders], axis=0) for part in parcels[-1]]
    got = [
        [blocks[0]] + [swap(blocks[k], "rows", k) for k in range(1, shards)] for blocks in parcels
    ]
    order = sorted(range(shards), key=lambda k: (k > 0, -k.bit_count()))
    last = [got[-1][k] for k in order]

    own, other, img = [], [], []
    for c in range(CHUNKS):
        here = after(spot, *own) if c else spot
        taps, image = call(
            functools.partial(conv_kernel, (order, shard_rows, width, out_rows, c * span)),
            [
                jax.ShapeDtypeStruct((out_pixels, span), f32),
                jax.ShapeDtypeStruct((out_pixels, span), bf16),
            ],
            [SMEM] + [VMEM] * (shards + 1),
            [
                pltpu.VMEM((shards * shard_rows + 6, width + 16, LANES), f32),
                pltpu.VMEM((49, 8, LANES), f32),
            ],
            3 * mib,
            out_pixels * span * 98 * 100,
            out_pixels * span * 10,
        )(here, *[got[c][k] for k in order], dw_kernel)
        own.append(taps)
        img.append(image)
        other.append(swap(taps, "section", 1))

    (keys,) = call(
        functools.partial(unpack_kernel, (order, pixels)),
        [jax.ShapeDtypeStruct((shards * per_key // 2, depth), bf16)],
        [VMEM] * shards,
        [],
        mib,
        10**6,
        10**6,
    )(*after(last, *own))
    bits = [1 << n for n in reversed(range(batches.bit_length() - 1))]
    pieces = [keys, swap(keys, "batch", bits[0])]

    hid = w1.shape[1]
    part_pixels = out_pixels // 2
    z, z_other = [], []
    for p in range(2):
        here = after(spot, pieces[-1], *z) if p else after(spot, keys)
        (mine,) = call(
            functools.partial(block_kernel, (p * part_pixels, part_pixels, CHUNKS)),
            [jax.ShapeDtypeStruct((part_pixels, chans), f32)],
            [SMEM] + [VMEM] * (3 * CHUNKS + 4),
            [pltpu.VMEM((2, part_pixels, half), bf16), pltpu.VMEM((part_pixels, hid), bf16)],
            8 * mib,
            4 * part_pixels * hid * chans,
            4 * hid * chans,
        )(here, *own, *other, *img, ln_gain, layer_branch_scale, w1, w2)
        z.append(mine)
        z_other.append(swap(mine, "section", 1))
    for bit in bits[1:]:
        pieces.append(swap(join(*pieces), "batch", bit))

    hidden = pe.shape[1]
    (hid_a,) = call(
        expand_kernel,
        [jax.ShapeDtypeStruct((part_pixels, hidden), bf16)],
        [VMEM] * 3,
        [pltpu.VMEM((part_pixels, chans), bf16)],
        6 * mib,
        2 * part_pixels * hidden * chans,
        2 * hidden * chans,
    )(z[0], z_other[0], pe)
    (hot,) = call(
        functools.partial(prep_kernel, (order, shard_rows, width, out_pixels, parts)),
        [jax.ShapeDtypeStruct((9 * REG, out_pixels), bf16)],
        [SMEM] + [VMEM] * shards,
        [pltpu.VMEM((16, (shards + 2) * pixels), f32)],
        2 * mib,
        10**8,
        10**6,
    )(after(spot, hid_a), *last)
    (pooled,) = call(
        project_kernel,
        [jax.ShapeDtypeStruct((REG, out_dim), f32)],
        [VMEM] * 6,
        [
            pltpu.VMEM((part_pixels, chans), bf16),
            pltpu.VMEM((hidden // 256, out_pixels, 256), bf16),
        ],
        8 * mib,
        2 * part_pixels * hidden * chans + 4 * 9 * REG * hidden * out_pixels,
        4 * hidden * chans,
    )(z[1], z_other[1], hid_a, pe, pk, hot)
    pick, facts = call(
        functools.partial(owner_kernel, (order, shard_rows, pixels, images, batches, per_key)),
        [jax.ShapeDtypeStruct((owned, slots), bf16), jax.ShapeDtypeStruct((owned, LANES), f32)],
        [SMEM] + [VMEM] * (shards + 2),
        [],
        2 * mib,
        10**8,
        10**6,
    )(after(spot, pooled), *last, owner_slot, partner)
    total, send = call(
        add_kernel,
        [jax.ShapeDtypeStruct((REG, out_dim), f32), jax.ShapeDtypeStruct((REG, out_dim), bf16)],
        [VMEM] * 2,
        [],
        mib,
        10**5,
        10**5,
    )(pooled, swap(pooled, "section", 1))
    sums = [swap(send, "rows", k) if k else total for k in order]
    pieces[-1] = after(pieces[-1], pooled)
    pieces.append(swap(join(*pieces), "section", 1))
    count = sum(x.shape[0] for x in pieces)
    keys, length = call(
        keys_kernel,
        [jax.ShapeDtypeStruct((depth, count), bf16), jax.ShapeDtypeStruct((1, count), f32)],
        [VMEM] * len(pieces),
        [],
        4 * mib,
        10**9,
        10**6,
    )(*pieces)

    embed, loss = call(
        functools.partial(loss_kernel, (order, parts)),
        [jax.ShapeDtypeStruct((owned, out_dim), f32), jax.ShapeDtypeStruct((1, owned), f32)],
        [SMEM] + [VMEM] * (shards + 4),
        [pltpu.VMEM((slots, out_dim), f32)],
        6 * mib,
        10**8,
        10**6,
    )(spot, *sums, pick, facts, keys, length)
    return embed, loss.reshape(owned)


def solution(mesh):
    in_specs = (
        P("batch", "rows", None, None),
        P(),
        P(),
        P(None, "section"),
        P("section", None),
        P(),
        P(None, "section"),
        P(None, "section", None),
        P("batch", "rows", None),
        P("batch", None),
        P("batch", None),
        P(("batch", "rows"), None),
    )
    out_specs = (P(("batch", "rows"), None), P(("batch", "rows")))
    return jax.shard_map(body, mesh=mesh, in_specs=in_specs, out_specs=out_specs, check_vma=False)
```

```python
import functools

import jax
import jax.numpy as jnp
from jax import lax
from jax.experimental import pallas as pl
from jax.experimental.pallas import tpu as pltpu
from jax.sharding import PartitionSpec as P

REG = 64
LANES = 128
STRIP = 4
CHUNKS = 2

sharpness_divisor = 0.1
ln_eps = 1e-06
norm_eps = 1e-06

VMEM = pl.BlockSpec(memory_space=pltpu.VMEM)
SMEM = pl.BlockSpec(memory_space=pltpu.SMEM)
f32 = jnp.float32
bf16 = jnp.bfloat16


def call(kernel, outs, in_specs, scratch, limit, flops, nbytes):
    return pl.pallas_call(
        kernel,
        out_shape=outs,
        in_specs=in_specs,
        out_specs=[VMEM] * len(outs),
        scratch_shapes=scratch,
        compiler_params=pltpu.CompilerParams(vmem_limit_bytes=limit),
        cost_estimate=pl.CostEstimate(flops=flops, bytes_accessed=nbytes, transcendentals=0),
    )


def dot(a, b):
    return jnp.dot(a, b, preferred_element_type=f32)


def dot_nt(a, b):
    return lax.dot_general(a, b, (((1,), (1,)), ((), ())), preferred_element_type=f32)


def gelu(x):
    return 0.5 * x * (1.0 + lax.erf(x * 0.7071067811865476))


def split(x):
    hi = x.astype(bf16)
    return hi, (x - hi.astype(f32)).astype(bf16)


def blank_kernel(_, out_ref):
    out_ref[...] = jnp.full(out_ref.shape, -1.0, f32)


def pack_kernel(pos_ref, ids_ref, key_ref, blank_ref, tail_ref, line):
    section = pos_ref[3]
    keys, depth = key_ref.shape
    shard_rows, width = ids_ref.shape[1:]
    line[...] = blank_ref[...]
    for i in range(ids_ref.shape[0]):
        line[i * shard_rows : (i + 1) * shard_rows, 0:width] = ids_ref[i].astype(f32)
    tail_ref[...] = jnp.zeros(tail_ref.shape, bf16)
    tail_ref[:, depth : depth + LANES] = line[...].astype(bf16)
    tail_ref[0 : keys // 2, 0:depth] = key_ref[pl.ds(pl.multiple_of(section * (keys // 2), keys // 2), keys // 2), :]


def join_kernel(*refs):
    start = 0
    for ref in refs[:-1]:
        refs[-1][start : start + ref.shape[0], :] = ref[...]
        start += ref.shape[0]


def join(*arrays):
    rows = sum(x.shape[0] for x in arrays)
    shape = jax.ShapeDtypeStruct((rows, arrays[0].shape[1]), arrays[0].dtype)
    joined = call(join_kernel, [shape], [VMEM] * len(arrays), [], 1 << 20, 0, rows * 1024)(*arrays)
    return joined[0]


def add_kernel(a_ref, b_ref, out_ref, send_ref):
    out_ref[...] = a_ref[...] + b_ref[...]
    send_ref[...] = out_ref[...].astype(bf16)


def conv_kernel(geo, pos_ref, *refs):
    order, shard_rows, width, out_rows, first_lane = geo
    shards = len(order)
    blocks = dict(zip(order, refs[:shards]))
    w_ref, taps, img_ref, xpad, wide = refs[shards:]
    chunk = taps.shape[1]
    row, first_row, col0 = pos_ref[0], pos_ref[1], pos_ref[2]
    height = shards * shard_rows
    pixels = shard_rows * width
    cols = xpad.shape[1]
    out_pixels = out_rows * width
    step_rows = STRIP

    xpad[0:3] = jnp.zeros((3, cols, LANES), f32)
    xpad[height + 3 : height + 6] = jnp.zeros((3, cols, LANES), f32)
    for y in range(3, height + 3):
        xpad[y, 0:8] = jnp.zeros((8, LANES), f32)
        xpad[y, 8 + width : 16 + width] = jnp.zeros((8, LANES), f32)

    def group(g, carry):
        lanes = pl.ds(pl.multiple_of(g * LANES, LANES), LANES)
        for k in range(shards):
            value = blocks[k][0:pixels, lanes].astype(f32).reshape(shard_rows, width, LANES)
            xpad[pl.ds(3 + (row ^ k) * shard_rows, shard_rows), 8 : 8 + width, :] = value
        start = pos_ref[3] * (w_ref.shape[2] // 2) + first_lane + g * LANES
        for dy in range(7):
            w = w_ref[dy, :, pl.ds(pl.multiple_of(start, LANES), LANES)].astype(f32)
            for dx in range(7):
                wide[dy * 7 + dx] = jnp.broadcast_to(w[dx : dx + 1], (8, LANES))

        def strip(i, carry):
            top = first_row + i * step_rows
            acc = [jnp.zeros((width // 8, 8, LANES), f32) for _ in range(step_rows)]
            for r in range(step_rows + 6):
                for dx in range(7):
                    v = xpad[top + r, pl.ds(col0 + dx, width), :].reshape(width // 8, 8, LANES)
                    for j in range(step_rows):
                        dy = r - j
                        if 0 <= dy < 7:
                            acc[j] = acc[j] + v * wide[dy * 7 + dx][None]
            for j in range(step_rows):
                start = pl.multiple_of((i * step_rows + j) * width, width)
                taps[pl.ds(start, width), lanes] = acc[j].reshape(width, LANES)
            return carry

        return lax.fori_loop(0, out_rows // step_rows, strip, carry)

    lax.fori_loop(0, chunk // LANES, group, 0)

    for k in range(shards):
        start = (row ^ k) * pixels - first_row * width

        @pl.when((start >= 0) & (start < out_pixels))
        def _():
            img_ref[pl.ds(pl.multiple_of(start, pixels), pixels), :] = blocks[k][0:pixels, :]


def block_kernel(geo, pos_ref, *refs):
    first, pixels, chunks = geo
    own, other, img = refs[:chunks], refs[chunks : 2 * chunks], refs[2 * chunks : 3 * chunks]
    gain_ref, scale_ref, w1_ref, w2_ref, z_ref, normed, inner = refs[3 * chunks :]
    chans, hid = w1_ref.shape
    half = chans // 2
    width = half // chunks
    section = pos_ref[3]
    rows = slice(first, first + pixels)
    gains = gain_ref[...].astype(f32).reshape(1, chans)
    scales = scale_ref[...].astype(f32).reshape(1, chans)
    gains = [gains[:, n * width : (n + 1) * width] for n in range(2 * chunks)]
    gains_own = [jnp.where(section == 0, gains[c], gains[chunks + c]) for c in range(chunks)]
    gains_other = [jnp.where(section == 0, gains[chunks + c], gains[c]) for c in range(chunks)]
    block = 32
    for r in range(pixels // block):
        part = slice(first + r * block, first + (r + 1) * block)
        values = [ref[part, :] for ref in own + other]
        mean = sum(jnp.sum(v, axis=1, keepdims=True) for v in values) * (1.0 / chans)
        values = [v - mean for v in values]
        spread = sum(jnp.sum(v * v, axis=1, keepdims=True) for v in values) * (1.0 / chans)
        inv = lax.rsqrt(spread + ln_eps)
        values = [(v * inv * g).astype(bf16) for v, g in zip(values, gains_own + gains_other)]
        to = slice(r * block, (r + 1) * block)
        for c in range(chunks):
            for side, value in ((section, values[c]), (1 - section, values[chunks + c])):
                start = pl.multiple_of(side * half + c * width, LANES)
                normed[to, pl.ds(start, width)] = value
    step = 256

    def widen(i):
        cols = slice(i * step, (i + 1) * step)
        return dot(normed[...], w1_ref[:, cols])

    ahead = widen(0)
    for i in range(hid // step):
        h = ahead
        if i + 1 < hid // step:
            ahead = widen(i + 1)
        inner[:, i * step : (i + 1) * step] = gelu(h).astype(bf16)
    step = width if width % 256 else 256

    def narrow(i):
        return dot(inner[...], w2_ref[:, i * step : (i + 1) * step])

    ahead = narrow(0)
    for i in range(chans // step):
        z = ahead
        if i + 1 < chans // step:
            ahead = narrow(i + 1)
        cols = slice(i * step, (i + 1) * step)
        side, start = divmod(i * step, half)
        c, start = divmod(start, width)
        keep = jnp.where(section == side, 1.0, 0.0)
        z_ref[:, cols] = z * scales[:, cols] + img[c][rows, start : start + step].astype(f32) * keep


def expand_kernel(z_ref, other_ref, pe_ref, out_ref, block):
    block[...] = (z_ref[...] + other_ref[...]).astype(bf16)
    step = 256
    for i in range(pe_ref.shape[1] // step):
        cols = slice(i * step, (i + 1) * step)
        out_ref[:, cols] = jnp.maximum(dot(block[...], pe_ref[:, cols]), 0.0).astype(bf16)


def prep_kernel(geo, pos_ref, *refs):
    order, shard_rows, width, out_pixels, parts = geo
    shards = len(order)
    ids = [refs[order.index(k)] for k in range(shards)]
    hot_ref, flat = refs[shards:]
    row, first_row = pos_ref[0], pos_ref[1]
    pixels = shard_rows * width
    depth = ids[0].shape[1] - LANES
    ids = [ref[pixels:, depth : depth + LANES].astype(f32) for ref in ids]
    image = row // parts
    flat[...] = jnp.full(flat.shape, -1.0, f32)
    for k in range(shards):
        start = pl.multiple_of((1 + (row ^ k)) * pixels, LANES)
        number = lax.broadcasted_iota(jnp.int32, ids[k].shape, 0)
        inside = lax.broadcasted_iota(jnp.int32, ids[k].shape, 1) < width
        for y in range(shard_rows):
            keep = inside & (number == image * shard_rows + y)
            mine = jnp.sum(jnp.where(keep, ids[k], 0.0), axis=0, keepdims=True)
            mine = jnp.broadcast_to(mine, (8, LANES))
            mine = pltpu.roll(mine, y * width, 1) if y else mine
            line = mine if y == 0 else line + mine
        flat[0:8, pl.ds(start, pixels)] = line
    total = flat.shape[1]
    whole = jnp.broadcast_to(flat[0:1, :], (8, total))
    lane = lax.broadcasted_iota(jnp.int32, (8, total), 1)
    col = lane % width
    region = lax.broadcasted_iota(jnp.int32, (REG, out_pixels), 0).astype(f32)
    start = pl.multiple_of(pixels + first_row * width, LANES)
    for dy in range(3):
        for dx in range(3):
            off = (dy - 1) * width + dx - 1
            moved = whole if off == 0 else pltpu.roll(whole, off % total, 1)
            if dx == 0:
                moved = jnp.where(col == width - 1, -1.0, moved)
            if dx == 2:
                moved = jnp.where(col == 0, -1.0, moved)
            flat[8:16, :] = moved
            line = flat[8:9, pl.ds(start, out_pixels)]
            tap = dy * 3 + dx
            hot_ref[tap * REG : (tap + 1) * REG, :] = jnp.where(region == line, 1.0, 0.0).astype(bf16)


def unpack_kernel(geo, *refs):
    order, pixels = geo
    keys_ref = refs[-1]
    count = keys_ref.shape[0] // len(order)
    for k, ref in zip(order, refs):
        keys_ref[k * count : (k + 1) * count, :] = ref[pixels : pixels + count, 0 : keys_ref.shape[1]]


def owner_kernel(geo, pos_ref, *refs):
    order, shard_rows, pixels, images, batches, per_key = geo
    shards = len(order)
    ids = [refs[order.index(k)] for k in range(shards)]
    owner_ref, partner_ref, pick_ref, own_ref = refs[shards:]
    row, batch, first_slot = pos_ref[0], pos_ref[4], pos_ref[5]
    depth = ids[0].shape[1] - LANES
    ids = [ref[pixels:, depth : depth + LANES].astype(f32) for ref in ids]
    owned, slots = pick_ref.shape
    slot = lax.broadcasted_iota(jnp.int32, (owned, slots), 1)
    want = lax.broadcasted_iota(jnp.int32, (owned, slots), 0) + first_slot
    pick = owner_ref[...] == want
    pick_ref[...] = jnp.where(pick, 1.0, 0.0).astype(bf16)
    one_region = lax.broadcasted_iota(jnp.int32, (REG, LANES), 0).astype(f32)
    tallies = []
    for i in range(images):
        tally = jnp.zeros((REG, LANES), f32)
        for k in range(shards):
            for y in range(i * shard_rows, (i + 1) * shard_rows):
                tally = tally + jnp.where(one_region == ids[k][y : y + 1, :], 1.0, 0.0)
        tallies.append(tally)
    tally = jnp.concatenate(tallies, axis=0).astype(bf16)
    count = dot_nt(jnp.ones((8, LANES), bf16), tally)[0:1]
    mates = jnp.concatenate([partner_ref[i : i + 1, :] for i in range(images)], axis=1)
    mate = (batch * images + slot // REG) * REG + mates
    block = mate // per_key
    within = mate % per_key
    core = (within // (per_key // 2)) ^ pos_ref[3]
    apart = (block // shards) ^ batch
    turn = core
    for n in range(batches.bit_length() - 1):
        turn = turn * 2 + ((apart >> n) & 1)
    place = turn * shards + ((block % shards) ^ row)
    place = place * (per_key // 2) + within % (per_key // 2)
    place = jnp.sum(jnp.where(pick, place, 0).astype(f32), axis=1, keepdims=True)
    number = jnp.sum(jnp.where(pick, count, 0.0), axis=1, keepdims=True)
    side = lax.broadcasted_iota(jnp.int32, (owned, LANES), 1)
    own_ref[...] = jnp.where(side == 0, place, jnp.where(side == 1, number, 0.0))


def project_kernel(z_ref, other_ref, first_ref, pe_ref, pk_ref, hot_ref, out_ref, block, hidden):
    before = first_ref.shape[0]
    pixels = z_ref.shape[0]
    taps = pk_ref.shape[0]
    block[...] = (z_ref[...] + other_ref[...]).astype(bf16)
    step = 256
    acc = jnp.zeros((2 * REG, out_ref.shape[1]), f32)
    for i in range(pe_ref.shape[1] // step):
        cols = slice(i * step, (i + 1) * step)
        hidden[i, 0:before, :] = first_ref[:, cols]
        h = jnp.maximum(dot(block[...], pe_ref[:, cols]), 0.0)
        hidden[i, before : before + pixels, :] = h.astype(bf16)
        sums = dot(hot_ref[...], hidden[i])
        hi = sums.astype(bf16)
        lo = (sums - hi.astype(f32)).astype(bf16)
        for t in range(taps):
            rows = slice(t * REG, (t + 1) * REG)
            both = jnp.concatenate([hi[rows], lo[rows]], axis=0)
            acc = acc + dot(both, pk_ref[t, cols, :])
    out_ref[...] = acc[0:REG] + acc[REG:]


def keys_kernel(*refs):
    keys_ref, length_ref = refs[-2:]
    keys = jnp.concatenate([ref[...] for ref in refs[:-2]], axis=0).astype(f32).T
    keys_ref[...] = keys.astype(bf16)
    length_ref[...] = lax.rsqrt(jnp.sum(keys * keys, axis=0, keepdims=True) + norm_eps)


def loss_kernel(geo, *refs):
    shards, parts = geo
    count = shards.bit_length()
    sums, row = refs[1 : count + 1], refs[0][0]
    pick_ref, own_ref, keys_ref, length_ref, embed_ref, loss_ref, table = refs[count + 1 :]
    if parts > 1:
        table[...] = jnp.zeros(table.shape, f32)
    for k in range(shards):
        place = pl.ds(pl.multiple_of(((row ^ k) // parts) * REG, REG), REG)
        top = 1 << (k.bit_length() - 1) if k else 0
        value = sums[k.bit_length()][(k - top) * REG : (k - top + 1) * REG, :].astype(f32)
        table[place, :] = value if parts == 1 else table[place, :] + value
    pick = pick_ref[...]
    hi, lo = split(table[...])
    ordered = dot(pick, hi) + dot(pick, lo)
    unit = ordered * lax.rsqrt(jnp.sum(ordered * ordered, axis=1, keepdims=True) + norm_eps)
    embed_ref[...] = unit
    owned = unit.shape[0]
    both = dot(jnp.concatenate(split(unit), axis=0), keys_ref[...])
    logits = both[0:owned] + both[owned:]
    logits = logits * (length_ref[...] / sharpness_divisor)
    total = jnp.log(jnp.sum(jnp.exp(logits), axis=1, keepdims=True))
    column = lax.broadcasted_iota(jnp.int32, logits.shape, 1).astype(f32)
    match = jnp.sum(jnp.where(column == own_ref[:, 0:1], logits, 0.0), axis=1, keepdims=True)
    loss = jnp.where(own_ref[:, 1:2] > 0.5, total - match, 0.0)
    line = lax.broadcasted_iota(jnp.int32, (owned, owned), 0)
    other = lax.broadcasted_iota(jnp.int32, (owned, owned), 1)
    loss_ref[...] = jnp.sum(jnp.where(line == other, loss, 0.0), axis=0, keepdims=True)


def swap(x, axis, bit):
    return lax.ppermute(x, axis, [(i, i ^ bit) for i in range(lax.axis_size(axis))])


def body(
    features,
    dw_kernel,
    ln_gain,
    widening_pointwise_matrix,
    w_reduce,
    layer_branch_scale,
    p_expand,
    p_kernel,
    region_ids,
    owner_slot,
    partner,
    key_embed,
):
    images, shard_rows, width, chans = features.shape
    shards = lax.axis_size("rows")
    batches = lax.axis_size("batch")
    row = lax.axis_index("rows")
    batch = lax.axis_index("batch")
    section = lax.axis_index("section")
    half = chans // lax.axis_size("section")
    parts = shards // images
    out_rows = shards * shard_rows // parts
    pixels = shard_rows * width
    out_pixels = out_rows * width
    slots = images * REG
    owned = slots // shards
    out_dim = p_kernel.shape[2]
    mib = 1 << 20
    span = half // CHUNKS

    w1, w2, pe, pk = widening_pointwise_matrix, w_reduce, p_expand, p_kernel
    first_row = (row % parts) * out_rows
    spot = jnp.stack(
        [row, first_row, jnp.int32(5), section, batch, row * owned]
    ).astype(jnp.int32)

    per_key, depth = key_embed.shape
    tail = max(-(-images * shard_rows // 16) * 16, per_key // 2)
    def after(here, *done):
        return lax.optimization_barrier((here, *done))[0]

    parcels = []
    for c in range(CHUNKS):
        blocks = []
        for k in range(shards):
            place = ((row ^ k) // parts, 0, 0, section * half + c * span)
            part = lax.dynamic_slice(features, place, (1, shard_rows, width, span))
            blocks.append(part.reshape(pixels, span))
        parcels.append(blocks)
    (blank,) = call(
        blank_kernel, [jax.ShapeDtypeStruct((tail, LANES), f32)], [VMEM], [], mib, 10**10, 10**4
    )(parcels[0][0])
    parcels[0] = after(parcels[0], blank)
    (riders,) = call(
        pack_kernel,
        [jax.ShapeDtypeStruct((tail, span), bf16)],
        [SMEM] + [VMEM] * 3,
        [pltpu.VMEM((tail, LANES), f32)],
        mib,
        0,
        10**6,
    )(spot, region_ids, key_embed, blank)
    parcels[-1] = [jnp.concatenate([part, riders], axis=0) for part in parcels[-1]]
    got = [
        [blocks[0]] + [swap(blocks[k], "rows", k) for k in range(1, shards)] for blocks in parcels
    ]
    order = list(range(shards))
    last = [got[-1][k] for k in order]

    own, other, img = [], [], []
    for c in range(CHUNKS):
        here = after(spot, *own) if c else spot
        taps, image = call(
            functools.partial(conv_kernel, (order, shard_rows, width, out_rows, c * span)),
            [
                jax.ShapeDtypeStruct((out_pixels, span), f32),
                jax.ShapeDtypeStruct((out_pixels, span), bf16),
            ],
            [SMEM] + [VMEM] * (shards + 1),
            [
                pltpu.VMEM((shards * shard_rows + 6, width + 16, LANES), f32),
                pltpu.VMEM((49, 8, LANES), f32),
            ],
            3 * mib,
            out_pixels * span * 98 * 100,
            out_pixels * span * 10,
        )(here, *[got[c][k] for k in order], dw_kernel)
        own.append(taps)
        img.append(image)
        other.append(swap(taps, "section", 1))

    (keys,) = call(
        functools.partial(unpack_kernel, (order, pixels)),
        [jax.ShapeDtypeStruct((shards * per_key // 2, depth), bf16)],
        [VMEM] * shards,
        [],
        mib,
        10**6,
        10**6,
    )(*after(last, *own))
    bits = [1 << n for n in reversed(range(batches.bit_length() - 1))]
    pieces = [keys, swap(keys, "batch", bits[0])]

    hid = w1.shape[1]
    part_pixels = out_pixels // 2
    z, z_other = [], []
    for p in range(2):
        here = after(spot, pieces[-1], *z) if p else after(spot, keys)
        (mine,) = call(
            functools.partial(block_kernel, (p * part_pixels, part_pixels, CHUNKS)),
            [jax.ShapeDtypeStruct((part_pixels, chans), f32)],
            [SMEM] + [VMEM] * (3 * CHUNKS + 4),
            [pltpu.VMEM((part_pixels, chans), bf16), pltpu.VMEM((part_pixels, hid), bf16)],
            8 * mib,
            4 * part_pixels * hid * chans,
            4 * hid * chans,
        )(here, *own, *other, *img, ln_gain, layer_branch_scale, w1, w2)
        z.append(mine)
        z_other.append(swap(mine, "section", 1))
    for bit in bits[1:]:
        pieces.append(swap(join(*pieces), "batch", bit))

    hidden = pe.shape[1]
    (hid_a,) = call(
        expand_kernel,
        [jax.ShapeDtypeStruct((part_pixels, hidden), bf16)],
        [VMEM] * 3,
        [pltpu.VMEM((part_pixels, chans), bf16)],
        6 * mib,
        2 * part_pixels * hidden * chans,
        2 * hidden * chans,
    )(z[0], z_other[0], pe)
    (hot,) = call(
        functools.partial(prep_kernel, (order, shard_rows, width, out_pixels, parts)),
        [jax.ShapeDtypeStruct((9 * REG, out_pixels), bf16)],
        [SMEM] + [VMEM] * shards,
        [pltpu.VMEM((16, (shards + 2) * pixels), f32)],
        2 * mib,
        10**8,
        10**6,
    )(after(spot, hid_a), *last)
    (pooled,) = call(
        project_kernel,
        [jax.ShapeDtypeStruct((REG, out_dim), f32)],
        [VMEM] * 6,
        [
            pltpu.VMEM((part_pixels, chans), bf16),
            pltpu.VMEM((hidden // 256, out_pixels, 256), bf16),
        ],
        8 * mib,
        2 * part_pixels * hidden * chans + 4 * 9 * REG * hidden * out_pixels,
        4 * hidden * chans,
    )(z[1], z_other[1], hid_a, pe, pk, hot)
    pick, facts = call(
        functools.partial(owner_kernel, (order, shard_rows, pixels, images, batches, per_key)),
        [jax.ShapeDtypeStruct((owned, slots), bf16), jax.ShapeDtypeStruct((owned, LANES), f32)],
        [SMEM] + [VMEM] * (shards + 2),
        [],
        2 * mib,
        10**8,
        10**6,
    )(after(spot, pooled), *last, owner_slot, partner)
    total, send = call(
        add_kernel,
        [jax.ShapeDtypeStruct((REG, out_dim), f32), jax.ShapeDtypeStruct((REG, out_dim), bf16)],
        [VMEM] * 2,
        [],
        mib,
        10**5,
        10**5,
    )(pooled, swap(pooled, "section", 1))
    sums = [send]
    for n in range(shards.bit_length() - 1):
        sums.append(swap(join(*sums) if n else send, "rows", 1 << n))
    sums[0] = total
    pieces[-1] = after(pieces[-1], pooled)
    pieces.append(swap(join(*pieces), "section", 1))
    count = sum(x.shape[0] for x in pieces)
    keys, length = call(
        keys_kernel,
        [jax.ShapeDtypeStruct((depth, count), bf16), jax.ShapeDtypeStruct((1, count), f32)],
        [VMEM] * len(pieces),
        [],
        4 * mib,
        10**9,
        10**6,
    )(*pieces)

    embed, loss = call(
        functools.partial(loss_kernel, (shards, parts)),
        [jax.ShapeDtypeStruct((owned, out_dim), f32), jax.ShapeDtypeStruct((1, owned), f32)],
        [SMEM] + [VMEM] * (len(sums) + 4),
        [pltpu.VMEM((slots, out_dim), f32)],
        6 * mib,
        10**8,
        10**6,
    )(spot, *sums, pick, facts, keys, length)
    return embed, loss.reshape(owned)


def solution(mesh):
    in_specs = (
        P("batch", "rows", None, None),
        P(),
        P(),
        P(None, "section"),
        P("section", None),
        P(),
        P(None, "section"),
        P(None, "section", None),
        P("batch", "rows", None),
        P("batch", None),
        P("batch", None),
        P(("batch", "rows"), None),
    )
    out_specs = (P(("batch", "rows"), None), P(("batch", "rows")))
    return jax.shard_map(body, mesh=mesh, in_specs=in_specs, out_specs=out_specs, check_vma=False)
```

```python
import functools

import jax
import jax.numpy as jnp
from jax import lax
from jax.experimental import pallas as pl
from jax.experimental.pallas import tpu as pltpu
from jax.sharding import PartitionSpec as P

REG = 64
LANES = 128
STRIP = 4
CHUNKS = 2

sharpness_divisor = 0.1
ln_eps = 1e-06
norm_eps = 1e-06

VMEM = pl.BlockSpec(memory_space=pltpu.VMEM)
SMEM = pl.BlockSpec(memory_space=pltpu.SMEM)
f32 = jnp.float32
bf16 = jnp.bfloat16


def call(kernel, outs, in_specs, scratch, limit, flops, nbytes):
    return pl.pallas_call(
        kernel,
        out_shape=outs,
        in_specs=in_specs,
        out_specs=[VMEM] * len(outs),
        scratch_shapes=scratch,
        compiler_params=pltpu.CompilerParams(vmem_limit_bytes=limit),
        cost_estimate=pl.CostEstimate(flops=flops, bytes_accessed=nbytes, transcendentals=0),
    )


def dot(a, b):
    return jnp.dot(a, b, preferred_element_type=f32)


def dot_nt(a, b):
    return lax.dot_general(a, b, (((1,), (1,)), ((), ())), preferred_element_type=f32)


def gelu(x):
    return 0.5 * x * (1.0 + lax.erf(x * 0.7071067811865476))


def split(x):
    hi = x.astype(bf16)
    return hi, (x - hi.astype(f32)).astype(bf16)


def blank_kernel(_, out_ref):
    out_ref[...] = jnp.full(out_ref.shape, -1.0, f32)


def pack_kernel(pos_ref, ids_ref, key_ref, blank_ref, tail_ref, line):
    section = pos_ref[3]
    keys, depth = key_ref.shape
    shard_rows, width = ids_ref.shape[1:]
    line[...] = blank_ref[...]
    for i in range(ids_ref.shape[0]):
        line[i * shard_rows : (i + 1) * shard_rows, 0:width] = ids_ref[i].astype(f32)
    tail_ref[...] = jnp.zeros(tail_ref.shape, bf16)
    tail_ref[:, depth : depth + LANES] = line[...].astype(bf16)
    tail_ref[0 : keys // 2, 0:depth] = key_ref[pl.ds(pl.multiple_of(section * (keys // 2), keys // 2), keys // 2), :]


def join_kernel(*refs):
    start = 0
    for ref in refs[:-1]:
        refs[-1][start : start + ref.shape[0], :] = ref[...]
        start += ref.shape[0]


def join(*arrays):
    rows = sum(x.shape[0] for x in arrays)
    shape = jax.ShapeDtypeStruct((rows, arrays[0].shape[1]), arrays[0].dtype)
    joined = call(join_kernel, [shape], [VMEM] * len(arrays), [], 1 << 20, 0, rows * 1024)(*arrays)
    return joined[0]


def add_kernel(a_ref, b_ref, out_ref, send_ref):
    out_ref[...] = a_ref[...] + b_ref[...]
    send_ref[...] = out_ref[...].astype(bf16)


def conv_kernel(geo, pos_ref, *refs):
    order, shard_rows, width, out_rows, first_lane = geo
    shards = len(order)
    blocks = dict(zip(order, refs[:shards]))
    w_ref, taps, img_ref, xpad, wide = refs[shards:]
    chunk = taps.shape[1]
    row, first_row, col0 = pos_ref[0], pos_ref[1], pos_ref[2]
    height = shards * shard_rows
    pixels = shard_rows * width
    cols = xpad.shape[1]
    out_pixels = out_rows * width
    step_rows = STRIP

    xpad[0:3] = jnp.zeros((3, cols, LANES), f32)
    xpad[height + 3 : height + 6] = jnp.zeros((3, cols, LANES), f32)
    for y in range(3, height + 3):
        xpad[y, 0:8] = jnp.zeros((8, LANES), f32)
        xpad[y, 8 + width : 16 + width] = jnp.zeros((8, LANES), f32)

    def group(g, carry):
        lanes = pl.ds(pl.multiple_of(g * LANES, LANES), LANES)
        for k in range(shards):
            value = blocks[k][0:pixels, lanes].astype(f32).reshape(shard_rows, width, LANES)
            xpad[pl.ds(3 + (row ^ k) * shard_rows, shard_rows), 8 : 8 + width, :] = value
        start = pos_ref[3] * (w_ref.shape[2] // 2) + first_lane + g * LANES
        for dy in range(7):
            w = w_ref[dy, :, pl.ds(pl.multiple_of(start, LANES), LANES)].astype(f32)
            for dx in range(7):
                wide[dy * 7 + dx] = jnp.broadcast_to(w[dx : dx + 1], (8, LANES))

        def strip(i, carry):
            top = first_row + i * step_rows
            acc = [jnp.zeros((width // 8, 8, LANES), f32) for _ in range(step_rows)]
            for r in range(step_rows + 6):
                for dx in range(7):
                    v = xpad[top + r, pl.ds(col0 + dx, width), :].reshape(width // 8, 8, LANES)
                    for j in range(step_rows):
                        dy = r - j
                        if 0 <= dy < 7:
                            acc[j] = acc[j] + v * wide[dy * 7 + dx][None]
            for j in range(step_rows):
                start = pl.multiple_of((i * step_rows + j) * width, width)
                taps[pl.ds(start, width), lanes] = acc[j].reshape(width, LANES)
            return carry

        return lax.fori_loop(0, out_rows // step_rows, strip, carry)

    lax.fori_loop(0, chunk // LANES, group, 0)

    for k in range(shards):
        start = (row ^ k) * pixels - first_row * width

        @pl.when((start >= 0) & (start < out_pixels))
        def _():
            img_ref[pl.ds(pl.multiple_of(start, pixels), pixels), :] = blocks[k][0:pixels, :]


def block_kernel(geo, pos_ref, *refs):
    first, pixels, chunks = geo
    own, other, img = refs[:chunks], refs[chunks : 2 * chunks], refs[2 * chunks : 3 * chunks]
    gain_ref, scale_ref, w1_ref, w2_ref, z_ref, normed, inner, wide = refs[3 * chunks :]
    chans, hid = w1_ref.shape
    half = chans // 2
    width = half // chunks
    section = pos_ref[3]
    rows = slice(first, first + pixels)
    gains = gain_ref[...].astype(f32).reshape(1, chans)
    scales = scale_ref[...].astype(f32).reshape(1, chans)
    gains = [gains[:, n * width : (n + 1) * width] for n in range(2 * chunks)]
    gains_own = [jnp.where(section == 0, gains[c], gains[chunks + c]) for c in range(chunks)]
    gains_other = [jnp.where(section == 0, gains[chunks + c], gains[c]) for c in range(chunks)]
    block = 32
    for r in range(pixels // block):
        part = slice(first + r * block, first + (r + 1) * block)
        values = [ref[part, :] for ref in own + other]
        mean = sum(jnp.sum(v, axis=1, keepdims=True) for v in values) * (1.0 / chans)
        values = [v - mean for v in values]
        spread = sum(jnp.sum(v * v, axis=1, keepdims=True) for v in values) * (1.0 / chans)
        inv = lax.rsqrt(spread + ln_eps)
        values = [(v * inv * g).astype(bf16) for v, g in zip(values, gains_own + gains_other)]
        to = slice(r * block, (r + 1) * block)
        for c in range(chunks):
            for side, value in ((section, values[c]), (1 - section, values[chunks + c])):
                start = pl.multiple_of(side * half + c * width, LANES)
                normed[to, pl.ds(start, width)] = value
    step = 256

    def widen(i):
        cols = slice(i * step, (i + 1) * step)
        return dot(normed[...], w1_ref[:, cols])

    wide[0] = widen(0)
    for i in range(hid // step):
        if i + 1 < hid // step:
            wide[(i + 1) % 2] = widen(i + 1)
        inner[:, i * step : (i + 1) * step] = gelu(wide[i % 2]).astype(bf16)
    step = width if width % 256 else 256

    def narrow(i):
        return dot(inner[...], w2_ref[:, i * step : (i + 1) * step])

    ahead = narrow(0)
    for i in range(chans // step):
        z = ahead
        if i + 1 < chans // step:
            ahead = narrow(i + 1)
        cols = slice(i * step, (i + 1) * step)
        side, start = divmod(i * step, half)
        c, start = divmod(start, width)
        keep = jnp.where(section == side, 1.0, 0.0)
        z_ref[:, cols] = z * scales[:, cols] + img[c][rows, start : start + step].astype(f32) * keep


def expand_kernel(z_ref, other_ref, pe_ref, out_ref, block):
    block[...] = (z_ref[...] + other_ref[...]).astype(bf16)
    step = 256
    for i in range(pe_ref.shape[1] // step):
        cols = slice(i * step, (i + 1) * step)
        out_ref[:, cols] = jnp.maximum(dot(block[...], pe_ref[:, cols]), 0.0).astype(bf16)


def prep_kernel(geo, pos_ref, *refs):
    order, shard_rows, width, out_pixels, parts = geo
    shards = len(order)
    ids = [refs[order.index(k)] for k in range(shards)]
    hot_ref, flat = refs[shards:]
    row, first_row = pos_ref[0], pos_ref[1]
    pixels = shard_rows * width
    depth = ids[0].shape[1] - LANES
    ids = [ref[pixels:, depth : depth + LANES].astype(f32) for ref in ids]
    image = row // parts
    flat[...] = jnp.full(flat.shape, -1.0, f32)
    for k in range(shards):
        start = pl.multiple_of((1 + (row ^ k)) * pixels, LANES)
        number = lax.broadcasted_iota(jnp.int32, ids[k].shape, 0)
        inside = lax.broadcasted_iota(jnp.int32, ids[k].shape, 1) < width
        for y in range(shard_rows):
            keep = inside & (number == image * shard_rows + y)
            mine = jnp.sum(jnp.where(keep, ids[k], 0.0), axis=0, keepdims=True)
            mine = jnp.broadcast_to(mine, (8, LANES))
            mine = pltpu.roll(mine, y * width, 1) if y else mine
            line = mine if y == 0 else line + mine
        flat[0:8, pl.ds(start, pixels)] = line
    total = flat.shape[1]
    whole = jnp.broadcast_to(flat[0:1, :], (8, total))
    lane = lax.broadcasted_iota(jnp.int32, (8, total), 1)
    col = lane % width
    region = lax.broadcasted_iota(jnp.int32, (REG, out_pixels), 0).astype(f32)
    start = pl.multiple_of(pixels + first_row * width, LANES)
    for dy in range(3):
        for dx in range(3):
            off = (dy - 1) * width + dx - 1
            moved = whole if off == 0 else pltpu.roll(whole, off % total, 1)
            if dx == 0:
                moved = jnp.where(col == width - 1, -1.0, moved)
            if dx == 2:
                moved = jnp.where(col == 0, -1.0, moved)
            flat[8:16, :] = moved
            line = flat[8:9, pl.ds(start, out_pixels)]
            tap = dy * 3 + dx
            hot_ref[tap * REG : (tap + 1) * REG, :] = jnp.where(region == line, 1.0, 0.0).astype(bf16)


def unpack_kernel(geo, *refs):
    order, pixels = geo
    keys_ref = refs[-1]
    count = keys_ref.shape[0] // len(order)
    for k, ref in zip(order, refs):
        keys_ref[k * count : (k + 1) * count, :] = ref[pixels : pixels + count, 0 : keys_ref.shape[1]]


def owner_kernel(geo, pos_ref, *refs):
    order, shard_rows, pixels, images, batches, per_key = geo
    shards = len(order)
    ids = [refs[order.index(k)] for k in range(shards)]
    owner_ref, partner_ref, pick_ref, own_ref = refs[shards:]
    row, batch, first_slot = pos_ref[0], pos_ref[4], pos_ref[5]
    depth = ids[0].shape[1] - LANES
    ids = [ref[pixels:, depth : depth + LANES].astype(f32) for ref in ids]
    owned, slots = pick_ref.shape
    slot = lax.broadcasted_iota(jnp.int32, (owned, slots), 1)
    want = lax.broadcasted_iota(jnp.int32, (owned, slots), 0) + first_slot
    pick = owner_ref[...] == want
    pick_ref[...] = jnp.where(pick, 1.0, 0.0).astype(bf16)
    one_region = lax.broadcasted_iota(jnp.int32, (REG, LANES), 0).astype(f32)
    tallies = []
    for i in range(images):
        tally = jnp.zeros((REG, LANES), f32)
        for k in range(shards):
            for y in range(i * shard_rows, (i + 1) * shard_rows):
                tally = tally + jnp.where(one_region == ids[k][y : y + 1, :], 1.0, 0.0)
        tallies.append(tally)
    tally = jnp.concatenate(tallies, axis=0).astype(bf16)
    count = dot_nt(jnp.ones((8, LANES), bf16), tally)[0:1]
    mates = jnp.concatenate([partner_ref[i : i + 1, :] for i in range(images)], axis=1)
    mate = (batch * images + slot // REG) * REG + mates
    block = mate // per_key
    within = mate % per_key
    core = (within // (per_key // 2)) ^ pos_ref[3]
    apart = (block // shards) ^ batch
    turn = core
    for n in range(batches.bit_length() - 1):
        turn = turn * 2 + ((apart >> n) & 1)
    place = turn * shards + ((block % shards) ^ row)
    place = place * (per_key // 2) + within % (per_key // 2)
    place = jnp.sum(jnp.where(pick, place, 0).astype(f32), axis=1, keepdims=True)
    number = jnp.sum(jnp.where(pick, count, 0.0), axis=1, keepdims=True)
    side = lax.broadcasted_iota(jnp.int32, (owned, LANES), 1)
    own_ref[...] = jnp.where(side == 0, place, jnp.where(side == 1, number, 0.0))


def project_kernel(z_ref, other_ref, first_ref, pe_ref, pk_ref, hot_ref, out_ref, block, hidden, sums):
    before = first_ref.shape[0]
    pixels = z_ref.shape[0]
    taps = pk_ref.shape[0]
    block[...] = (z_ref[...] + other_ref[...]).astype(bf16)
    step = 256
    acc = jnp.zeros((2 * REG, out_ref.shape[1]), f32)
    tiles = pe_ref.shape[1] // step

    def collect(i):
        cols = slice(i * step, (i + 1) * step)
        hidden[i, 0:before, :] = first_ref[:, cols]
        h = jnp.maximum(dot(block[...], pe_ref[:, cols]), 0.0)
        hidden[i, before : before + pixels, :] = h.astype(bf16)
        sums[i % 2] = dot(hot_ref[...], hidden[i])

    collect(0)
    for i in range(tiles):
        if i + 1 < tiles:
            collect(i + 1)
        cols = slice(i * step, (i + 1) * step)
        for t in range(taps):
            both = jnp.concatenate(split(sums[i % 2, t * REG : (t + 1) * REG, :]), axis=0)
            acc = acc + dot(both, pk_ref[t, cols, :])
    out_ref[...] = acc[0:REG] + acc[REG:]


def keys_kernel(*refs):
    keys_ref, length_ref = refs[-2:]
    keys = jnp.concatenate([ref[...] for ref in refs[:-2]], axis=0).astype(f32).T
    keys_ref[...] = keys.astype(bf16)
    length_ref[...] = lax.rsqrt(jnp.sum(keys * keys, axis=0, keepdims=True) + norm_eps)


def loss_kernel(geo, *refs):
    shards, parts = geo
    sums, row = refs[1 : shards + 1], refs[0][0]
    pick_ref, own_ref, keys_ref, length_ref, embed_ref, loss_ref, table = refs[shards + 1 :]
    if parts > 1:
        table[...] = jnp.zeros(table.shape, f32)
    for k in range(shards):
        place = pl.ds(pl.multiple_of(((row ^ k) // parts) * REG, REG), REG)
        value = sums[k][...].astype(f32)
        table[place, :] = value if parts == 1 else table[place, :] + value
    pick = pick_ref[...]
    hi, lo = split(table[...])
    ordered = dot(pick, hi) + dot(pick, lo)
    unit = ordered * lax.rsqrt(jnp.sum(ordered * ordered, axis=1, keepdims=True) + norm_eps)
    embed_ref[...] = unit
    owned = unit.shape[0]
    both = dot(jnp.concatenate(split(unit), axis=0), keys_ref[...])
    logits = both[0:owned] + both[owned:]
    logits = logits * (length_ref[...] / sharpness_divisor)
    total = jnp.log(jnp.sum(jnp.exp(logits), axis=1, keepdims=True))
    column = lax.broadcasted_iota(jnp.int32, logits.shape, 1).astype(f32)
    match = jnp.sum(jnp.where(column == own_ref[:, 0:1], logits, 0.0), axis=1, keepdims=True)
    loss = jnp.where(own_ref[:, 1:2] > 0.5, total - match, 0.0)
    line = lax.broadcasted_iota(jnp.int32, (owned, owned), 0)
    other = lax.broadcasted_iota(jnp.int32, (owned, owned), 1)
    loss_ref[...] = jnp.sum(jnp.where(line == other, loss, 0.0), axis=0, keepdims=True)


def swap(x, axis, bit):
    return lax.ppermute(x, axis, [(i, i ^ bit) for i in range(lax.axis_size(axis))])


def body(
    features,
    dw_kernel,
    ln_gain,
    widening_pointwise_matrix,
    w_reduce,
    layer_branch_scale,
    p_expand,
    p_kernel,
    region_ids,
    owner_slot,
    partner,
    key_embed,
):
    images, shard_rows, width, chans = features.shape
    shards = lax.axis_size("rows")
    batches = lax.axis_size("batch")
    row = lax.axis_index("rows")
    batch = lax.axis_index("batch")
    section = lax.axis_index("section")
    half = chans // lax.axis_size("section")
    parts = shards // images
    out_rows = shards * shard_rows // parts
    pixels = shard_rows * width
    out_pixels = out_rows * width
    slots = images * REG
    owned = slots // shards
    out_dim = p_kernel.shape[2]
    mib = 1 << 20
    span = half // CHUNKS

    w1, w2, pe, pk = widening_pointwise_matrix, w_reduce, p_expand, p_kernel
    first_row = (row % parts) * out_rows
    spot = jnp.stack(
        [row, first_row, jnp.int32(5), section, batch, row * owned]
    ).astype(jnp.int32)

    per_key, depth = key_embed.shape
    tail = max(-(-images * shard_rows // 16) * 16, per_key // 2)
    def after(here, *done):
        return lax.optimization_barrier((here, *done))[0]

    parcels = []
    for c in range(CHUNKS):
        blocks = []
        for k in range(shards):
            place = ((row ^ k) // parts, 0, 0, section * half + c * span)
            part = lax.dynamic_slice(features, place, (1, shard_rows, width, span))
            blocks.append(part.reshape(pixels, span))
        parcels.append(blocks)
    (blank,) = call(
        blank_kernel, [jax.ShapeDtypeStruct((tail, LANES), f32)], [VMEM], [], mib, 10**10, 10**4
    )(parcels[0][0])
    parcels[0] = after(parcels[0], blank)
    (riders,) = call(
        pack_kernel,
        [jax.ShapeDtypeStruct((tail, span), bf16)],
        [SMEM] + [VMEM] * 3,
        [pltpu.VMEM((tail, LANES), f32)],
        mib,
        0,
        10**6,
    )(spot, region_ids, key_embed, blank)
    parcels[-1] = [jnp.concatenate([part, riders], axis=0) for part in parcels[-1]]
    got = [
        [blocks[0]] + [swap(blocks[k], "rows", k) for k in range(1, shards)] for blocks in parcels
    ]
    order = list(range(shards))
    last = [got[-1][k] for k in order]

    own, other, img = [], [], []
    for c in range(CHUNKS):
        here = after(spot, *own) if c else spot
        taps, image = call(
            functools.partial(conv_kernel, (order, shard_rows, width, out_rows, c * span)),
            [
                jax.ShapeDtypeStruct((out_pixels, span), f32),
                jax.ShapeDtypeStruct((out_pixels, span), bf16),
            ],
            [SMEM] + [VMEM] * (shards + 1),
            [
                pltpu.VMEM((shards * shard_rows + 6, width + 16, LANES), f32),
                pltpu.VMEM((49, 8, LANES), f32),
            ],
            3 * mib,
            out_pixels * span * 98 * 100,
            out_pixels * span * 10,
        )(here, *[got[c][k] for k in order], dw_kernel)
        own.append(taps)
        img.append(image)
        other.append(swap(taps, "section", 1))

    (keys,) = call(
        functools.partial(unpack_kernel, (order, pixels)),
        [jax.ShapeDtypeStruct((shards * per_key // 2, depth), bf16)],
        [VMEM] * shards,
        [],
        mib,
        10**6,
        10**6,
    )(*after(last, *own))
    bits = [1 << n for n in reversed(range(batches.bit_length() - 1))]
    pieces = [keys, swap(keys, "batch", bits[0])]

    hid = w1.shape[1]
    part_pixels = out_pixels // 2
    z, z_other = [], []
    for p in range(2):
        here = after(spot, pieces[-1], *z) if p else after(spot, keys)
        (mine,) = call(
            functools.partial(block_kernel, (p * part_pixels, part_pixels, CHUNKS)),
            [jax.ShapeDtypeStruct((part_pixels, chans), f32)],
            [SMEM] + [VMEM] * (3 * CHUNKS + 4),
            [
                pltpu.VMEM((part_pixels, chans), bf16),
                pltpu.VMEM((part_pixels, hid), bf16),
                pltpu.VMEM((2, part_pixels, 256), f32),
            ],
            8 * mib,
            4 * part_pixels * hid * chans,
            4 * hid * chans,
        )(here, *own, *other, *img, ln_gain, layer_branch_scale, w1, w2)
        z.append(mine)
        z_other.append(swap(mine, "section", 1))
    for bit in bits[1:]:
        pieces.append(swap(join(*pieces), "batch", bit))

    hidden = pe.shape[1]
    (hid_a,) = call(
        expand_kernel,
        [jax.ShapeDtypeStruct((part_pixels, hidden), bf16)],
        [VMEM] * 3,
        [pltpu.VMEM((part_pixels, chans), bf16)],
        6 * mib,
        2 * part_pixels * hidden * chans,
        2 * hidden * chans,
    )(z[0], z_other[0], pe)
    (hot,) = call(
        functools.partial(prep_kernel, (order, shard_rows, width, out_pixels, parts)),
        [jax.ShapeDtypeStruct((9 * REG, out_pixels), bf16)],
        [SMEM] + [VMEM] * shards,
        [pltpu.VMEM((16, (shards + 2) * pixels), f32)],
        2 * mib,
        10**8,
        10**6,
    )(after(spot, hid_a), *last)
    (pooled,) = call(
        project_kernel,
        [jax.ShapeDtypeStruct((REG, out_dim), f32)],
        [VMEM] * 6,
        [
            pltpu.VMEM((part_pixels, chans), bf16),
            pltpu.VMEM((hidden // 256, out_pixels, 256), bf16),
            pltpu.VMEM((2, 9 * REG, 256), f32),
        ],
        8 * mib,
        2 * part_pixels * hidden * chans + 4 * 9 * REG * hidden * out_pixels,
        4 * hidden * chans,
    )(z[1], z_other[1], hid_a, pe, pk, hot)
    pick, facts = call(
        functools.partial(owner_kernel, (order, shard_rows, pixels, images, batches, per_key)),
        [jax.ShapeDtypeStruct((owned, slots), bf16), jax.ShapeDtypeStruct((owned, LANES), f32)],
        [SMEM] + [VMEM] * (shards + 2),
        [],
        2 * mib,
        10**8,
        10**6,
    )(after(spot, pooled), *last, owner_slot, partner)
    total, send = call(
        add_kernel,
        [jax.ShapeDtypeStruct((REG, out_dim), f32), jax.ShapeDtypeStruct((REG, out_dim), bf16)],
        [VMEM] * 2,
        [],
        mib,
        10**5,
        10**5,
    )(pooled, swap(pooled, "section", 1))
    sums = [swap(send, "rows", k) if k else total for k in range(shards)]
    pieces[-1] = after(pieces[-1], pooled)
    pieces.append(swap(join(*pieces), "section", 1))
    count = sum(x.shape[0] for x in pieces)
    keys, length = call(
        keys_kernel,
        [jax.ShapeDtypeStruct((depth, count), bf16), jax.ShapeDtypeStruct((1, count), f32)],
        [VMEM] * len(pieces),
        [],
        4 * mib,
        10**9,
        10**6,
    )(*pieces)

    embed, loss = call(
        functools.partial(loss_kernel, (shards, parts)),
        [jax.ShapeDtypeStruct((owned, out_dim), f32), jax.ShapeDtypeStruct((1, owned), f32)],
        [SMEM] + [VMEM] * (len(sums) + 4),
        [pltpu.VMEM((slots, out_dim), f32)],
        6 * mib,
        10**8,
        10**6,
    )(spot, *sums, pick, facts, keys, length)
    return embed, loss.reshape(owned)


def solution(mesh):
    in_specs = (
        P("batch", "rows", None, None),
        P(),
        P(),
        P(None, "section"),
        P("section", None),
        P(),
        P(None, "section"),
        P(None, "section", None),
        P("batch", "rows", None),
        P("batch", None),
        P("batch", None),
        P(("batch", "rows"), None),
    )
    out_specs = (P(("batch", "rows"), None), P(("batch", "rows")))
    return jax.shard_map(body, mesh=mesh, in_specs=in_specs, out_specs=out_specs, check_vma=False)
```

```python
import functools

import jax
import jax.numpy as jnp
from jax import lax
from jax.experimental import pallas as pl
from jax.experimental.pallas import tpu as pltpu
from jax.sharding import PartitionSpec as P

REG = 64
LANES = 128
STRIP = 4
CHUNKS = 2

sharpness_divisor = 0.1
ln_eps = 1e-06
norm_eps = 1e-06

VMEM = pl.BlockSpec(memory_space=pltpu.VMEM)
SMEM = pl.BlockSpec(memory_space=pltpu.SMEM)
f32 = jnp.float32
bf16 = jnp.bfloat16


def call(kernel, outs, in_specs, scratch, limit, flops, nbytes):
    return pl.pallas_call(
        kernel,
        out_shape=outs,
        in_specs=in_specs,
        out_specs=[VMEM] * len(outs),
        scratch_shapes=scratch,
        compiler_params=pltpu.CompilerParams(vmem_limit_bytes=limit),
        cost_estimate=pl.CostEstimate(flops=flops, bytes_accessed=nbytes, transcendentals=0),
    )


def dot(a, b):
    return jnp.dot(a, b, preferred_element_type=f32)


def dot_nt(a, b):
    return lax.dot_general(a, b, (((1,), (1,)), ((), ())), preferred_element_type=f32)


def gelu(x):
    return 0.5 * x * (1.0 + lax.erf(x * 0.7071067811865476))


def split(x):
    hi = x.astype(bf16)
    return hi, (x - hi.astype(f32)).astype(bf16)


def blank_kernel(_, out_ref):
    out_ref[...] = jnp.full(out_ref.shape, -1.0, f32)


def pack_kernel(pos_ref, ids_ref, key_ref, blank_ref, tail_ref, line):
    section = pos_ref[3]
    keys, depth = key_ref.shape
    shard_rows, width = ids_ref.shape[1:]
    line[...] = blank_ref[...]
    for i in range(ids_ref.shape[0]):
        line[i * shard_rows : (i + 1) * shard_rows, 0:width] = ids_ref[i].astype(f32)
    tail_ref[...] = jnp.zeros(tail_ref.shape, bf16)
    tail_ref[:, depth : depth + LANES] = line[...].astype(bf16)
    tail_ref[0 : keys // 2, 0:depth] = key_ref[pl.ds(pl.multiple_of(section * (keys // 2), keys // 2), keys // 2), :]


def join_kernel(*refs):
    start = 0
    for ref in refs[:-1]:
        refs[-1][start : start + ref.shape[0], :] = ref[...]
        start += ref.shape[0]


def join(*arrays):
    rows = sum(x.shape[0] for x in arrays)
    shape = jax.ShapeDtypeStruct((rows, arrays[0].shape[1]), arrays[0].dtype)
    joined = call(join_kernel, [shape], [VMEM] * len(arrays), [], 1 << 20, 0, rows * 1024)(*arrays)
    return joined[0]


def add_kernel(a_ref, b_ref, out_ref, send_ref):
    out_ref[...] = a_ref[...] + b_ref[...]
    send_ref[...] = out_ref[...].astype(bf16)


def conv_kernel(geo, pos_ref, *refs):
    order, shard_rows, width, out_rows, first_lane, lane0 = geo
    shards = len(order)
    blocks = dict(zip(order, refs[:shards]))
    w_ref, taps, img_ref, xpad, wide = refs[shards:]
    chunk = taps.shape[1]
    row, first_row, col0 = pos_ref[0], pos_ref[1], pos_ref[2]
    height = shards * shard_rows
    pixels = shard_rows * width
    cols = xpad.shape[1]
    out_pixels = out_rows * width
    step_rows = STRIP

    xpad[0:3] = jnp.zeros((3, cols, LANES), f32)
    xpad[height + 3 : height + 6] = jnp.zeros((3, cols, LANES), f32)
    for y in range(3, height + 3):
        xpad[y, 0:8] = jnp.zeros((8, LANES), f32)
        xpad[y, 8 + width : 16 + width] = jnp.zeros((8, LANES), f32)

    def group(g, carry):
        lanes = pl.ds(pl.multiple_of(g * LANES, LANES), LANES)
        for k in range(shards):
            value = blocks[k][0:pixels, pl.ds(pl.multiple_of(lane0 + g * LANES, LANES), LANES)].astype(f32).reshape(shard_rows, width, LANES)
            xpad[pl.ds(3 + (row ^ k) * shard_rows, shard_rows), 8 : 8 + width, :] = value
        start = pos_ref[3] * (w_ref.shape[2] // 2) + first_lane + g * LANES
        for dy in range(7):
            w = w_ref[dy, :, pl.ds(pl.multiple_of(start, LANES), LANES)].astype(f32)
            for dx in range(7):
                wide[dy * 7 + dx] = jnp.broadcast_to(w[dx : dx + 1], (8, LANES))

        def strip(i, carry):
            top = first_row + i * step_rows
            acc = [jnp.zeros((width // 8, 8, LANES), f32) for _ in range(step_rows)]
            for r in range(step_rows + 6):
                for dx in range(7):
                    v = xpad[top + r, pl.ds(col0 + dx, width), :].reshape(width // 8, 8, LANES)
                    for j in range(step_rows):
                        dy = r - j
                        if 0 <= dy < 7:
                            acc[j] = acc[j] + v * wide[dy * 7 + dx][None]
            for j in range(step_rows):
                start = pl.multiple_of((i * step_rows + j) * width, width)
                taps[pl.ds(start, width), lanes] = acc[j].reshape(width, LANES)
            return carry

        return lax.fori_loop(0, out_rows // step_rows, strip, carry)

    lax.fori_loop(0, chunk // LANES, group, 0)

    for k in range(shards):
        start = (row ^ k) * pixels - first_row * width

        @pl.when((start >= 0) & (start < out_pixels))
        def _():
            img_ref[pl.ds(pl.multiple_of(start, pixels), pixels), :] = blocks[k][0:pixels, lane0 : lane0 + chunk]


def block_kernel(geo, pos_ref, *refs):
    first, pixels, widths = geo
    chunks = len(widths)
    own, other, img = refs[:chunks], refs[chunks : 2 * chunks], refs[2 * chunks : 3 * chunks]
    gain_ref, scale_ref, w1_ref, w2_ref, z_ref, normed, inner, wide = refs[3 * chunks :]
    chans, hid = w1_ref.shape
    half = chans // 2
    starts = [sum(widths[:c]) for c in range(chunks)]
    section = pos_ref[3]
    rows = slice(first, first + pixels)
    gains = gain_ref[...].astype(f32).reshape(1, chans)
    scales = scale_ref[...].astype(f32).reshape(1, chans)
    low = [gains[:, n : n + w] for n, w in zip(starts, widths)]
    high = [gains[:, half + n : half + n + w] for n, w in zip(starts, widths)]
    gains_own = [jnp.where(section == 0, x, y) for x, y in zip(low, high)]
    gains_other = [jnp.where(section == 0, y, x) for x, y in zip(low, high)]
    block = 32
    for r in range(pixels // block):
        part = slice(first + r * block, first + (r + 1) * block)
        values = [ref[part, :] for ref in own + other]
        mean = sum(jnp.sum(v, axis=1, keepdims=True) for v in values) * (1.0 / chans)
        values = [v - mean for v in values]
        spread = sum(jnp.sum(v * v, axis=1, keepdims=True) for v in values) * (1.0 / chans)
        inv = lax.rsqrt(spread + ln_eps)
        values = [(v * inv * g).astype(bf16) for v, g in zip(values, gains_own + gains_other)]
        to = slice(r * block, (r + 1) * block)
        for c in range(chunks):
            for side, value in ((section, values[c]), (1 - section, values[chunks + c])):
                start = pl.multiple_of(side * half + starts[c], LANES)
                normed[to, pl.ds(start, widths[c])] = value
    step = 256

    def widen(i):
        cols = slice(i * step, (i + 1) * step)
        return dot(normed[...], w1_ref[:, cols])

    wide[0] = widen(0)
    for i in range(hid // step):
        if i + 1 < hid // step:
            wide[(i + 1) % 2] = widen(i + 1)
        inner[:, i * step : (i + 1) * step] = gelu(wide[i % 2]).astype(bf16)

    def image(start):
        found = []
        for c in range(chunks):
            low, high = max(start, starts[c]), min(start + step, starts[c] + widths[c])
            if low < high:
                found.append(img[c][rows, low - starts[c] : high - starts[c]])
        return found[0] if len(found) == 1 else jnp.concatenate(found, axis=1)

    for i in range(chans // step):
        cols = slice(i * step, (i + 1) * step)
        side, start = divmod(i * step, half)
        keep = jnp.where(section == side, 1.0, 0.0)
        z = dot(inner[...], w2_ref[:, cols]) * scales[:, cols]
        z_ref[:, cols] = z + image(start).astype(f32) * keep


def expand_kernel(z_ref, other_ref, pe_ref, out_ref, block):
    block[...] = (z_ref[...] + other_ref[...]).astype(bf16)
    step = 256
    for i in range(pe_ref.shape[1] // step):
        cols = slice(i * step, (i + 1) * step)
        out_ref[:, cols] = jnp.maximum(dot(block[...], pe_ref[:, cols]), 0.0).astype(bf16)


def prep_kernel(geo, pos_ref, *refs):
    order, shard_rows, width, out_pixels, parts = geo
    shards = len(order)
    ids = [refs[order.index(k)] for k in range(shards)]
    hot_ref, flat = refs[shards:]
    row, first_row = pos_ref[0], pos_ref[1]
    pixels = shard_rows * width
    depth = ids[0].shape[1] - LANES
    ids = [ref[pixels:, depth : depth + LANES].astype(f32) for ref in ids]
    image = row // parts
    flat[...] = jnp.full(flat.shape, -1.0, f32)
    for k in range(shards):
        start = pl.multiple_of((1 + (row ^ k)) * pixels, LANES)
        number = lax.broadcasted_iota(jnp.int32, ids[k].shape, 0)
        inside = lax.broadcasted_iota(jnp.int32, ids[k].shape, 1) < width
        for y in range(shard_rows):
            keep = inside & (number == image * shard_rows + y)
            mine = jnp.sum(jnp.where(keep, ids[k], 0.0), axis=0, keepdims=True)
            mine = jnp.broadcast_to(mine, (8, LANES))
            mine = pltpu.roll(mine, y * width, 1) if y else mine
            line = mine if y == 0 else line + mine
        flat[0:8, pl.ds(start, pixels)] = line
    total = flat.shape[1]
    whole = jnp.broadcast_to(flat[0:1, :], (8, total))
    lane = lax.broadcasted_iota(jnp.int32, (8, total), 1)
    col = lane % width
    region = lax.broadcasted_iota(jnp.int32, (REG, out_pixels), 0).astype(f32)
    start = pl.multiple_of(pixels + first_row * width, LANES)
    for dy in range(3):
        for dx in range(3):
            off = (dy - 1) * width + dx - 1
            moved = whole if off == 0 else pltpu.roll(whole, off % total, 1)
            if dx == 0:
                moved = jnp.where(col == width - 1, -1.0, moved)
            if dx == 2:
                moved = jnp.where(col == 0, -1.0, moved)
            flat[8:16, :] = moved
            line = flat[8:9, pl.ds(start, out_pixels)]
            tap = dy * 3 + dx
            hot_ref[tap * REG : (tap + 1) * REG, :] = jnp.where(region == line, 1.0, 0.0).astype(bf16)


def unpack_kernel(geo, *refs):
    order, pixels = geo
    keys_ref = refs[-1]
    count = keys_ref.shape[0] // len(order)
    for k, ref in zip(order, refs):
        keys_ref[k * count : (k + 1) * count, :] = ref[pixels : pixels + count, 0 : keys_ref.shape[1]]


def owner_kernel(geo, pos_ref, *refs):
    order, shard_rows, pixels, images, batches, per_key = geo
    shards = len(order)
    ids = [refs[order.index(k)] for k in range(shards)]
    owner_ref, partner_ref, pick_ref, own_ref = refs[shards:]
    row, batch, first_slot = pos_ref[0], pos_ref[4], pos_ref[5]
    depth = ids[0].shape[1] - LANES
    ids = [ref[pixels:, depth : depth + LANES].astype(f32) for ref in ids]
    owned, slots = pick_ref.shape
    slot = lax.broadcasted_iota(jnp.int32, (owned, slots), 1)
    want = lax.broadcasted_iota(jnp.int32, (owned, slots), 0) + first_slot
    pick = owner_ref[...] == want
    pick_ref[...] = jnp.where(pick, 1.0, 0.0).astype(bf16)
    one_region = lax.broadcasted_iota(jnp.int32, (REG, LANES), 0).astype(f32)
    tallies = []
    for i in range(images):
        tally = jnp.zeros((REG, LANES), f32)
        for k in range(shards):
            for y in range(i * shard_rows, (i + 1) * shard_rows):
                tally = tally + jnp.where(one_region == ids[k][y : y + 1, :], 1.0, 0.0)
        tallies.append(tally)
    tally = jnp.concatenate(tallies, axis=0).astype(bf16)
    count = dot_nt(jnp.ones((8, LANES), bf16), tally)[0:1]
    mates = jnp.concatenate([partner_ref[i : i + 1, :] for i in range(images)], axis=1)
    mate = (batch * images + slot // REG) * REG + mates
    block = mate // per_key
    within = mate % per_key
    core = (within // (per_key // 2)) ^ pos_ref[3]
    apart = (block // shards) ^ batch
    turn = core
    for n in range(batches.bit_length() - 1):
        turn = turn * 2 + ((apart >> n) & 1)
    place = turn * shards + ((block % shards) ^ row)
    place = place * (per_key // 2) + within % (per_key // 2)
    place = jnp.sum(jnp.where(pick, place, 0).astype(f32), axis=1, keepdims=True)
    number = jnp.sum(jnp.where(pick, count, 0.0), axis=1, keepdims=True)
    side = lax.broadcasted_iota(jnp.int32, (owned, LANES), 1)
    own_ref[...] = jnp.where(side == 0, place, jnp.where(side == 1, number, 0.0))


def project_kernel(z_ref, other_ref, first_ref, pe_ref, pk_ref, hot_ref, out_ref, block, hidden):
    before = first_ref.shape[0]
    pixels = z_ref.shape[0]
    taps = pk_ref.shape[0]
    block[...] = (z_ref[...] + other_ref[...]).astype(bf16)
    step = 256
    acc = jnp.zeros((2 * REG, out_ref.shape[1]), f32)
    for i in range(pe_ref.shape[1] // step):
        cols = slice(i * step, (i + 1) * step)
        hidden[i, 0:before, :] = first_ref[:, cols]
        h = jnp.maximum(dot(block[...], pe_ref[:, cols]), 0.0)
        hidden[i, before : before + pixels, :] = h.astype(bf16)
        sums = dot(hot_ref[...], hidden[i])
        hi = sums.astype(bf16)
        lo = (sums - hi.astype(f32)).astype(bf16)
        for t in range(taps):
            rows = slice(t * REG, (t + 1) * REG)
            both = jnp.concatenate([hi[rows], lo[rows]], axis=0)
            acc = acc + dot(both, pk_ref[t, cols, :])
    out_ref[...] = acc[0:REG] + acc[REG:]


def keys_kernel(*refs):
    keys_ref, length_ref = refs[-2:]
    keys = jnp.concatenate([ref[...] for ref in refs[:-2]], axis=0).astype(f32).T
    keys_ref[...] = keys.astype(bf16)
    length_ref[...] = lax.rsqrt(jnp.sum(keys * keys, axis=0, keepdims=True) + norm_eps)


def loss_kernel(geo, *refs):
    shards, parts = geo
    sums, row = refs[1 : shards + 1], refs[0][0]
    pick_ref, own_ref, keys_ref, length_ref, embed_ref, loss_ref, table = refs[shards + 1 :]
    if parts > 1:
        table[...] = jnp.zeros(table.shape, f32)
    for k in range(shards):
        place = pl.ds(pl.multiple_of(((row ^ k) // parts) * REG, REG), REG)
        value = sums[k][...].astype(f32)
        table[place, :] = value if parts == 1 else table[place, :] + value
    pick = pick_ref[...]
    hi, lo = split(table[...])
    ordered = dot(pick, hi) + dot(pick, lo)
    unit = ordered * lax.rsqrt(jnp.sum(ordered * ordered, axis=1, keepdims=True) + norm_eps)
    embed_ref[...] = unit
    owned = unit.shape[0]
    both = dot(jnp.concatenate(split(unit), axis=0), keys_ref[...])
    logits = both[0:owned] + both[owned:]
    logits = logits * (length_ref[...] / sharpness_divisor)
    total = jnp.log(jnp.sum(jnp.exp(logits), axis=1, keepdims=True))
    column = lax.broadcasted_iota(jnp.int32, logits.shape, 1).astype(f32)
    match = jnp.sum(jnp.where(column == own_ref[:, 0:1], logits, 0.0), axis=1, keepdims=True)
    loss = jnp.where(own_ref[:, 1:2] > 0.5, total - match, 0.0)
    line = lax.broadcasted_iota(jnp.int32, (owned, owned), 0)
    other = lax.broadcasted_iota(jnp.int32, (owned, owned), 1)
    loss_ref[...] = jnp.sum(jnp.where(line == other, loss, 0.0), axis=0, keepdims=True)


def swap(x, axis, bit):
    return lax.ppermute(x, axis, [(i, i ^ bit) for i in range(lax.axis_size(axis))])


def body(
    features,
    dw_kernel,
    ln_gain,
    widening_pointwise_matrix,
    w_reduce,
    layer_branch_scale,
    p_expand,
    p_kernel,
    region_ids,
    owner_slot,
    partner,
    key_embed,
):
    images, shard_rows, width, chans = features.shape
    shards = lax.axis_size("rows")
    batches = lax.axis_size("batch")
    row = lax.axis_index("rows")
    batch = lax.axis_index("batch")
    section = lax.axis_index("section")
    half = chans // lax.axis_size("section")
    parts = shards // images
    out_rows = shards * shard_rows // parts
    pixels = shard_rows * width
    out_pixels = out_rows * width
    slots = images * REG
    owned = slots // shards
    out_dim = p_kernel.shape[2]
    mib = 1 << 20
    span = half // CHUNKS

    w1, w2, pe, pk = widening_pointwise_matrix, w_reduce, p_expand, p_kernel
    first_row = (row % parts) * out_rows
    spot = jnp.stack(
        [row, first_row, jnp.int32(5), section, batch, row * owned]
    ).astype(jnp.int32)

    per_key, depth = key_embed.shape
    tail = max(-(-images * shard_rows // 16) * 16, per_key // 2)
    def after(here, *done):
        return lax.optimization_barrier((here, *done))[0]

    parcels = []
    for c in range(CHUNKS):
        blocks = []
        for k in range(shards):
            place = ((row ^ k) // parts, 0, 0, section * half + c * span)
            part = lax.dynamic_slice(features, place, (1, shard_rows, width, span))
            blocks.append(part.reshape(pixels, span))
        parcels.append(blocks)
    (blank,) = call(
        blank_kernel, [jax.ShapeDtypeStruct((tail, LANES), f32)], [VMEM], [], mib, 10**10, 10**4
    )(parcels[0][0])
    parcels[0] = after(parcels[0], blank)
    (riders,) = call(
        pack_kernel,
        [jax.ShapeDtypeStruct((tail, span), bf16)],
        [SMEM] + [VMEM] * 3,
        [pltpu.VMEM((tail, LANES), f32)],
        mib,
        0,
        10**6,
    )(spot, region_ids, key_embed, blank)
    parcels[-1] = [jnp.concatenate([part, riders], axis=0) for part in parcels[-1]]
    got = [
        [blocks[0]] + [swap(blocks[k], "rows", k) for k in range(1, shards)] for blocks in parcels
    ]
    order = list(range(shards))
    last = [got[-1][k] for k in order]

    cuts = [(c, 0, span) for c in range(CHUNKS)]
    own, other, img = [], [], []
    for c, lane0, wide in cuts:
        here = after(spot, *own) if own else spot
        taps, image = call(
            functools.partial(conv_kernel, (order, shard_rows, width, out_rows, c * span + lane0, lane0)),
            [
                jax.ShapeDtypeStruct((out_pixels, wide), f32),
                jax.ShapeDtypeStruct((out_pixels, wide), bf16),
            ],
            [SMEM] + [VMEM] * (shards + 1),
            [
                pltpu.VMEM((shards * shard_rows + 6, width + 16, LANES), f32),
                pltpu.VMEM((49, 8, LANES), f32),
            ],
            3 * mib,
            out_pixels * wide * 98 * 100,
            out_pixels * wide * 10,
        )(here, *[got[c][k] for k in order], dw_kernel)
        own.append(taps)
        img.append(image)
        other.append(swap(taps, "section", 1))

    (keys,) = call(
        functools.partial(unpack_kernel, (order, pixels)),
        [jax.ShapeDtypeStruct((shards * per_key // 2, depth), bf16)],
        [VMEM] * shards,
        [],
        mib,
        10**6,
        10**6,
    )(*after(last, *own))
    bits = [1 << n for n in reversed(range(batches.bit_length() - 1))]
    pieces = [keys, swap(keys, "batch", bits[0])]

    hid = w1.shape[1]
    part_pixels = out_pixels // 2
    z, z_other = [], []
    for p in range(2):
        here = after(spot, pieces[-1], *z) if p else after(spot, keys)
        (mine,) = call(
            functools.partial(block_kernel, (p * part_pixels, part_pixels, [w for _, _, w in cuts])),
            [jax.ShapeDtypeStruct((part_pixels, chans), f32)],
            [SMEM] + [VMEM] * (3 * len(cuts) + 4),
            [
                pltpu.VMEM((part_pixels, chans), bf16),
                pltpu.VMEM((part_pixels, hid), bf16),
                pltpu.VMEM((2, part_pixels, 256), f32),
            ],
            8 * mib,
            4 * part_pixels * hid * chans,
            4 * hid * chans,
        )(here, *own, *other, *img, ln_gain, layer_branch_scale, w1, w2)
        z.append(mine)
        z_other.append(swap(mine, "section", 1))
    for bit in bits[1:]:
        pieces.append(swap(join(*pieces), "batch", bit))

    hidden = pe.shape[1]
    (hid_a,) = call(
        expand_kernel,
        [jax.ShapeDtypeStruct((part_pixels, hidden), bf16)],
        [VMEM] * 3,
        [pltpu.VMEM((part_pixels, chans), bf16)],
        6 * mib,
        2 * part_pixels * hidden * chans,
        2 * hidden * chans,
    )(z[0], z_other[0], pe)
    (hot,) = call(
        functools.partial(prep_kernel, (order, shard_rows, width, out_pixels, parts)),
        [jax.ShapeDtypeStruct((9 * REG, out_pixels), bf16)],
        [SMEM] + [VMEM] * shards,
        [pltpu.VMEM((16, (shards + 2) * pixels), f32)],
        2 * mib,
        10**8,
        10**6,
    )(after(spot, hid_a), *last)
    (pooled,) = call(
        project_kernel,
        [jax.ShapeDtypeStruct((REG, out_dim), f32)],
        [VMEM] * 6,
        [
            pltpu.VMEM((part_pixels, chans), bf16),
            pltpu.VMEM((hidden // 256, out_pixels, 256), bf16),
        ],
        8 * mib,
        2 * part_pixels * hidden * chans + 4 * 9 * REG * hidden * out_pixels,
        4 * hidden * chans,
    )(z[1], z_other[1], hid_a, pe, pk, hot)
    pick, facts = call(
        functools.partial(owner_kernel, (order, shard_rows, pixels, images, batches, per_key)),
        [jax.ShapeDtypeStruct((owned, slots), bf16), jax.ShapeDtypeStruct((owned, LANES), f32)],
        [SMEM] + [VMEM] * (shards + 2),
        [],
        2 * mib,
        10**8,
        10**6,
    )(after(spot, pooled), *last, owner_slot, partner)
    total, send = call(
        add_kernel,
        [jax.ShapeDtypeStruct((REG, out_dim), f32), jax.ShapeDtypeStruct((REG, out_dim), bf16)],
        [VMEM] * 2,
        [],
        mib,
        10**5,
        10**5,
    )(pooled, swap(pooled, "section", 1))
    sums = [swap(send, "rows", k) if k else total for k in range(shards)]
    pieces[-1] = after(pieces[-1], pooled)
    pieces.append(swap(join(*pieces), "section", 1))
    count = sum(x.shape[0] for x in pieces)
    keys, length = call(
        keys_kernel,
        [jax.ShapeDtypeStruct((depth, count), bf16), jax.ShapeDtypeStruct((1, count), f32)],
        [VMEM] * len(pieces),
        [],
        4 * mib,
        10**9,
        10**6,
    )(*pieces)

    embed, loss = call(
        functools.partial(loss_kernel, (shards, parts)),
        [jax.ShapeDtypeStruct((owned, out_dim), f32), jax.ShapeDtypeStruct((1, owned), f32)],
        [SMEM] + [VMEM] * (len(sums) + 4),
        [pltpu.VMEM((slots, out_dim), f32)],
        6 * mib,
        10**8,
        10**6,
    )(spot, *sums, pick, facts, keys, length)
    return embed, loss.reshape(owned)


def solution(mesh):
    in_specs = (
        P("batch", "rows", None, None),
        P(),
        P(),
        P(None, "section"),
        P("section", None),
        P(),
        P(None, "section"),
        P(None, "section", None),
        P("batch", "rows", None),
        P("batch", None),
        P("batch", None),
        P(("batch", "rows"), None),
    )
    out_specs = (P(("batch", "rows"), None), P(("batch", "rows")))
    return jax.shard_map(body, mesh=mesh, in_specs=in_specs, out_specs=out_specs, check_vma=False)
```

```python
import functools

import jax
import jax.numpy as jnp
from jax import lax
from jax.experimental import pallas as pl
from jax.experimental.pallas import tpu as pltpu
from jax.sharding import PartitionSpec as P

REG = 64
LANES = 128
STRIP = 4
CHUNKS = 2

sharpness_divisor = 0.1
ln_eps = 1e-06
norm_eps = 1e-06

VMEM = pl.BlockSpec(memory_space=pltpu.VMEM)
SMEM = pl.BlockSpec(memory_space=pltpu.SMEM)
f32 = jnp.float32
bf16 = jnp.bfloat16


def call(kernel, outs, in_specs, scratch, limit, flops, nbytes):
    return pl.pallas_call(
        kernel,
        out_shape=outs,
        in_specs=in_specs,
        out_specs=[VMEM] * len(outs),
        scratch_shapes=scratch,
        compiler_params=pltpu.CompilerParams(vmem_limit_bytes=limit),
        cost_estimate=pl.CostEstimate(flops=flops, bytes_accessed=nbytes, transcendentals=0),
    )


def dot(a, b):
    return jnp.dot(a, b, preferred_element_type=f32)


def dot_nt(a, b):
    return lax.dot_general(a, b, (((1,), (1,)), ((), ())), preferred_element_type=f32)


def gelu(x):
    return 0.5 * x * (1.0 + lax.erf(x * 0.7071067811865476))


def split(x):
    hi = x.astype(bf16)
    return hi, (x - hi.astype(f32)).astype(bf16)


def blank_kernel(_, out_ref):
    out_ref[...] = jnp.full(out_ref.shape, -1.0, f32)


def pack_kernel(pos_ref, ids_ref, key_ref, blank_ref, tail_ref, line):
    section = pos_ref[3]
    keys, depth = key_ref.shape
    shard_rows, width = ids_ref.shape[1:]
    line[...] = blank_ref[...]
    for i in range(ids_ref.shape[0]):
        line[i * shard_rows : (i + 1) * shard_rows, 0:width] = ids_ref[i].astype(f32)
    tail_ref[...] = jnp.zeros(tail_ref.shape, bf16)
    tail_ref[:, depth : depth + LANES] = line[...].astype(bf16)
    tail_ref[0 : keys // 2, 0:depth] = key_ref[pl.ds(pl.multiple_of(section * (keys // 2), keys // 2), keys // 2), :]


def join_kernel(*refs):
    start = 0
    for ref in refs[:-1]:
        refs[-1][start : start + ref.shape[0], :] = ref[...]
        start += ref.shape[0]


def join(*arrays):
    rows = sum(x.shape[0] for x in arrays)
    shape = jax.ShapeDtypeStruct((rows, arrays[0].shape[1]), arrays[0].dtype)
    joined = call(join_kernel, [shape], [VMEM] * len(arrays), [], 1 << 20, 0, rows * 1024)(*arrays)
    return joined[0]


def add_kernel(a_ref, b_ref, out_ref, send_ref):
    out_ref[...] = a_ref[...] + b_ref[...]
    send_ref[...] = out_ref[...].astype(bf16)


def conv_kernel(geo, pos_ref, *refs):
    order, shard_rows, width, out_rows, first_lane, lane0 = geo
    shards = len(order)
    blocks = dict(zip(order, refs[:shards]))
    w_ref, taps, img_ref, xpad, wide = refs[shards:]
    chunk = taps.shape[1]
    row, first_row, col0 = pos_ref[0], pos_ref[1], pos_ref[2]
    height = shards * shard_rows
    pixels = shard_rows * width
    cols = xpad.shape[1]
    out_pixels = out_rows * width
    step_rows = STRIP

    xpad[0:3] = jnp.zeros((3, cols, LANES), f32)
    xpad[height + 3 : height + 6] = jnp.zeros((3, cols, LANES), f32)
    for y in range(3, height + 3):
        xpad[y, 0:8] = jnp.zeros((8, LANES), f32)
        xpad[y, 8 + width : 16 + width] = jnp.zeros((8, LANES), f32)

    def group(g, carry):
        lanes = pl.ds(pl.multiple_of(g * LANES, LANES), LANES)
        for k in range(shards):
            value = blocks[k][0:pixels, pl.ds(pl.multiple_of(lane0 + g * LANES, LANES), LANES)].astype(f32).reshape(shard_rows, width, LANES)
            xpad[pl.ds(3 + (row ^ k) * shard_rows, shard_rows), 8 : 8 + width, :] = value
        start = pos_ref[3] * (w_ref.shape[2] // 2) + first_lane + g * LANES
        for dy in range(7):
            w = w_ref[dy, :, pl.ds(pl.multiple_of(start, LANES), LANES)].astype(f32)
            for dx in range(7):
                wide[dy * 7 + dx] = jnp.broadcast_to(w[dx : dx + 1], (8, LANES))

        def strip(i, carry):
            top = first_row + i * step_rows
            acc = [jnp.zeros((width // 8, 8, LANES), f32) for _ in range(step_rows)]
            for r in range(step_rows + 6):
                for dx in range(7):
                    v = xpad[top + r, pl.ds(col0 + dx, width), :].reshape(width // 8, 8, LANES)
                    for j in range(step_rows):
                        dy = r - j
                        if 0 <= dy < 7:
                            acc[j] = acc[j] + v * wide[dy * 7 + dx][None]
            for j in range(step_rows):
                start = pl.multiple_of((i * step_rows + j) * width, width)
                taps[pl.ds(start, width), lanes] = acc[j].reshape(width, LANES)
            return carry

        return lax.fori_loop(0, out_rows // step_rows, strip, carry)

    lax.fori_loop(0, chunk // LANES, group, 0)

    for k in range(shards):
        start = (row ^ k) * pixels - first_row * width

        @pl.when((start >= 0) & (start < out_pixels))
        def _():
            img_ref[pl.ds(pl.multiple_of(start, pixels), pixels), :] = blocks[k][0:pixels, lane0 : lane0 + chunk]


def block_kernel(geo, pos_ref, *refs):
    first, pixels, widths = geo
    chunks = len(widths)
    own, other, img = refs[:chunks], refs[chunks : 2 * chunks], refs[2 * chunks : 3 * chunks]
    gain_ref, scale_ref, w1_ref, w2_ref, z_ref, normed, inner, wide = refs[3 * chunks :]
    chans, hid = w1_ref.shape
    half = chans // 2
    starts = [sum(widths[:c]) for c in range(chunks)]
    section = pos_ref[3]
    rows = slice(first, first + pixels)
    gains = gain_ref[...].astype(f32).reshape(1, chans)
    scales = scale_ref[...].astype(f32).reshape(1, chans)
    low = [gains[:, n : n + w] for n, w in zip(starts, widths)]
    high = [gains[:, half + n : half + n + w] for n, w in zip(starts, widths)]
    gains_own = [jnp.where(section == 0, x, y) for x, y in zip(low, high)]
    gains_other = [jnp.where(section == 0, y, x) for x, y in zip(low, high)]
    block = 32
    for r in range(pixels // block):
        part = slice(first + r * block, first + (r + 1) * block)
        values = [ref[part, :] for ref in own + other]
        mean = sum(jnp.sum(v, axis=1, keepdims=True) for v in values) * (1.0 / chans)
        values = [v - mean for v in values]
        spread = sum(jnp.sum(v * v, axis=1, keepdims=True) for v in values) * (1.0 / chans)
        inv = lax.rsqrt(spread + ln_eps)
        values = [(v * inv * g).astype(bf16) for v, g in zip(values, gains_own + gains_other)]
        to = slice(r * block, (r + 1) * block)
        for c in range(chunks):
            for side, value in ((section, values[c]), (1 - section, values[chunks + c])):
                start = pl.multiple_of(side * half + starts[c], LANES)
                normed[to, pl.ds(start, widths[c])] = value
    step = 512

    def widen(i):
        cols = slice(i * step, (i + 1) * step)
        return dot(normed[...], w1_ref[:, cols])

    wide[0] = widen(0)
    for i in range(hid // step):
        if i + 1 < hid // step:
            wide[(i + 1) % 2] = widen(i + 1)
        inner[:, i * step : (i + 1) * step] = gelu(wide[i % 2]).astype(bf16)
    step = half

    def image(start):
        found = []
        for c in range(chunks):
            low, high = max(start, starts[c]), min(start + step, starts[c] + widths[c])
            if low < high:
                found.append(img[c][rows, low - starts[c] : high - starts[c]])
        return found[0] if len(found) == 1 else jnp.concatenate(found, axis=1)

    for i in range(chans // step):
        cols = slice(i * step, (i + 1) * step)
        side, start = divmod(i * step, half)
        keep = jnp.where(section == side, 1.0, 0.0)
        z = dot(inner[...], w2_ref[:, cols]) * scales[:, cols]
        z_ref[:, cols] = z + image(start).astype(f32) * keep


def expand_kernel(z_ref, other_ref, pe_ref, out_ref, block):
    block[...] = (z_ref[...] + other_ref[...]).astype(bf16)
    step = 512
    for i in range(pe_ref.shape[1] // step):
        cols = slice(i * step, (i + 1) * step)
        out_ref[:, cols] = jnp.maximum(dot(block[...], pe_ref[:, cols]), 0.0).astype(bf16)


def prep_kernel(geo, pos_ref, *refs):
    order, shard_rows, width, out_pixels, parts = geo
    shards = len(order)
    ids = [refs[order.index(k)] for k in range(shards)]
    hot_ref, flat = refs[shards:]
    row, first_row = pos_ref[0], pos_ref[1]
    pixels = shard_rows * width
    depth = ids[0].shape[1] - LANES
    ids = [ref[pixels:, depth : depth + LANES].astype(f32) for ref in ids]
    image = row // parts
    flat[...] = jnp.full(flat.shape, -1.0, f32)
    for k in range(shards):
        start = pl.multiple_of((1 + (row ^ k)) * pixels, LANES)
        number = lax.broadcasted_iota(jnp.int32, ids[k].shape, 0)
        inside = lax.broadcasted_iota(jnp.int32, ids[k].shape, 1) < width
        for y in range(shard_rows):
            keep = inside & (number == image * shard_rows + y)
            mine = jnp.sum(jnp.where(keep, ids[k], 0.0), axis=0, keepdims=True)
            mine = jnp.broadcast_to(mine, (8, LANES))
            mine = pltpu.roll(mine, y * width, 1) if y else mine
            line = mine if y == 0 else line + mine
        flat[0:8, pl.ds(start, pixels)] = line
    total = flat.shape[1]
    whole = jnp.broadcast_to(flat[0:1, :], (8, total))
    lane = lax.broadcasted_iota(jnp.int32, (8, total), 1)
    col = lane % width
    region = lax.broadcasted_iota(jnp.int32, (REG, out_pixels), 0).astype(f32)
    start = pl.multiple_of(pixels + first_row * width, LANES)
    for dy in range(3):
        for dx in range(3):
            off = (dy - 1) * width + dx - 1
            moved = whole if off == 0 else pltpu.roll(whole, off % total, 1)
            if dx == 0:
                moved = jnp.where(col == width - 1, -1.0, moved)
            if dx == 2:
                moved = jnp.where(col == 0, -1.0, moved)
            flat[8:16, :] = moved
            line = flat[8:9, pl.ds(start, out_pixels)]
            tap = dy * 3 + dx
            hot_ref[tap * REG : (tap + 1) * REG, :] = jnp.where(region == line, 1.0, 0.0).astype(bf16)


def unpack_kernel(geo, *refs):
    order, pixels = geo
    keys_ref = refs[-1]
    count = keys_ref.shape[0] // len(order)
    for k, ref in zip(order, refs):
        keys_ref[k * count : (k + 1) * count, :] = ref[pixels : pixels + count, 0 : keys_ref.shape[1]]


def owner_kernel(geo, pos_ref, *refs):
    order, shard_rows, pixels, images, batches, per_key = geo
    shards = len(order)
    ids = [refs[order.index(k)] for k in range(shards)]
    owner_ref, partner_ref, pick_ref, own_ref = refs[shards:]
    row, batch, first_slot = pos_ref[0], pos_ref[4], pos_ref[5]
    depth = ids[0].shape[1] - LANES
    ids = [ref[pixels:, depth : depth + LANES].astype(f32) for ref in ids]
    owned, slots = pick_ref.shape
    slot = lax.broadcasted_iota(jnp.int32, (owned, slots), 1)
    want = lax.broadcasted_iota(jnp.int32, (owned, slots), 0) + first_slot
    pick = owner_ref[...] == want
    pick_ref[...] = jnp.where(pick, 1.0, 0.0).astype(bf16)
    one_region = lax.broadcasted_iota(jnp.int32, (REG, LANES), 0).astype(f32)
    tallies = []
    for i in range(images):
        tally = jnp.zeros((REG, LANES), f32)
        for k in range(shards):
            for y in range(i * shard_rows, (i + 1) * shard_rows):
                tally = tally + jnp.where(one_region == ids[k][y : y + 1, :], 1.0, 0.0)
        tallies.append(tally)
    tally = jnp.concatenate(tallies, axis=0).astype(bf16)
    count = dot_nt(jnp.ones((8, LANES), bf16), tally)[0:1]
    mates = jnp.concatenate([partner_ref[i : i + 1, :] for i in range(images)], axis=1)
    mate = (batch * images + slot // REG) * REG + mates
    block = mate // per_key
    within = mate % per_key
    core = (within // (per_key // 2)) ^ pos_ref[3]
    apart = (block // shards) ^ batch
    turn = core
    for n in range(batches.bit_length() - 1):
        turn = turn * 2 + ((apart >> n) & 1)
    place = turn * shards + ((block % shards) ^ row)
    place = place * (per_key // 2) + within % (per_key // 2)
    place = jnp.sum(jnp.where(pick, place, 0).astype(f32), axis=1, keepdims=True)
    number = jnp.sum(jnp.where(pick, count, 0.0), axis=1, keepdims=True)
    side = lax.broadcasted_iota(jnp.int32, (owned, LANES), 1)
    own_ref[...] = jnp.where(side == 0, place, jnp.where(side == 1, number, 0.0))


def project_kernel(z_ref, other_ref, first_ref, pe_ref, pk_ref, hot_ref, out_ref, block, hidden):
    before = first_ref.shape[0]
    pixels = z_ref.shape[0]
    taps = pk_ref.shape[0]
    block[...] = (z_ref[...] + other_ref[...]).astype(bf16)
    step = 256
    acc = jnp.zeros((2 * REG, out_ref.shape[1]), f32)
    for i in range(pe_ref.shape[1] // step):
        cols = slice(i * step, (i + 1) * step)
        hidden[i, 0:before, :] = first_ref[:, cols]
        h = jnp.maximum(dot(block[...], pe_ref[:, cols]), 0.0)
        hidden[i, before : before + pixels, :] = h.astype(bf16)
        sums = dot(hot_ref[...], hidden[i])
        hi = sums.astype(bf16)
        lo = (sums - hi.astype(f32)).astype(bf16)
        for t in range(taps):
            rows = slice(t * REG, (t + 1) * REG)
            both = jnp.concatenate([hi[rows], lo[rows]], axis=0)
            acc = acc + dot(both, pk_ref[t, cols, :])
    out_ref[...] = acc[0:REG] + acc[REG:]


def keys_kernel(*refs):
    keys_ref, length_ref = refs[-2:]
    keys = jnp.concatenate([ref[...] for ref in refs[:-2]], axis=0).astype(f32).T
    keys_ref[...] = keys.astype(bf16)
    length_ref[...] = lax.rsqrt(jnp.sum(keys * keys, axis=0, keepdims=True) + norm_eps)


def loss_kernel(geo, *refs):
    shards, parts = geo
    sums, row = refs[1 : shards + 1], refs[0][0]
    pick_ref, own_ref, keys_ref, length_ref, embed_ref, loss_ref, table = refs[shards + 1 :]
    if parts > 1:
        table[...] = jnp.zeros(table.shape, f32)
    for k in range(shards):
        place = pl.ds(pl.multiple_of(((row ^ k) // parts) * REG, REG), REG)
        value = sums[k][...].astype(f32)
        table[place, :] = value if parts == 1 else table[place, :] + value
    pick = pick_ref[...]
    hi, lo = split(table[...])
    ordered = dot(pick, hi) + dot(pick, lo)
    unit = ordered * lax.rsqrt(jnp.sum(ordered * ordered, axis=1, keepdims=True) + norm_eps)
    embed_ref[...] = unit
    owned = unit.shape[0]
    both = dot(jnp.concatenate(split(unit), axis=0), keys_ref[...])
    logits = both[0:owned] + both[owned:]
    logits = logits * (length_ref[...] / sharpness_divisor)
    total = jnp.log(jnp.sum(jnp.exp(logits), axis=1, keepdims=True))
    column = lax.broadcasted_iota(jnp.int32, logits.shape, 1).astype(f32)
    match = jnp.sum(jnp.where(column == own_ref[:, 0:1], logits, 0.0), axis=1, keepdims=True)
    loss = jnp.where(own_ref[:, 1:2] > 0.5, total - match, 0.0)
    line = lax.broadcasted_iota(jnp.int32, (owned, owned), 0)
    other = lax.broadcasted_iota(jnp.int32, (owned, owned), 1)
    loss_ref[...] = jnp.sum(jnp.where(line == other, loss, 0.0), axis=0, keepdims=True)


def swap(x, axis, bit):
    return lax.ppermute(x, axis, [(i, i ^ bit) for i in range(lax.axis_size(axis))])


def body(
    features,
    dw_kernel,
    ln_gain,
    widening_pointwise_matrix,
    w_reduce,
    layer_branch_scale,
    p_expand,
    p_kernel,
    region_ids,
    owner_slot,
    partner,
    key_embed,
):
    images, shard_rows, width, chans = features.shape
    shards = lax.axis_size("rows")
    batches = lax.axis_size("batch")
    row = lax.axis_index("rows")
    batch = lax.axis_index("batch")
    section = lax.axis_index("section")
    half = chans // lax.axis_size("section")
    parts = shards // images
    out_rows = shards * shard_rows // parts
    pixels = shard_rows * width
    out_pixels = out_rows * width
    slots = images * REG
    owned = slots // shards
    out_dim = p_kernel.shape[2]
    mib = 1 << 20
    span = half // CHUNKS

    w1, w2, pe, pk = widening_pointwise_matrix, w_reduce, p_expand, p_kernel
    first_row = (row % parts) * out_rows
    spot = jnp.stack(
        [row, first_row, jnp.int32(5), section, batch, row * owned]
    ).astype(jnp.int32)

    per_key, depth = key_embed.shape
    tail = max(-(-images * shard_rows // 16) * 16, per_key // 2)
    def after(here, *done):
        return lax.optimization_barrier((here, *done))[0]

    parcels = []
    for c in range(CHUNKS):
        blocks = []
        for k in range(shards):
            place = ((row ^ k) // parts, 0, 0, section * half + c * span)
            part = lax.dynamic_slice(features, place, (1, shard_rows, width, span))
            blocks.append(part.reshape(pixels, span))
        parcels.append(blocks)
    (blank,) = call(
        blank_kernel, [jax.ShapeDtypeStruct((tail, LANES), f32)], [VMEM], [], mib, 10**10, 10**4
    )(parcels[0][0])
    parcels[0] = after(parcels[0], blank)
    (riders,) = call(
        pack_kernel,
        [jax.ShapeDtypeStruct((tail, span), bf16)],
        [SMEM] + [VMEM] * 3,
        [pltpu.VMEM((tail, LANES), f32)],
        mib,
        0,
        10**6,
    )(spot, region_ids, key_embed, blank)
    parcels[-1] = [jnp.concatenate([part, riders], axis=0) for part in parcels[-1]]
    got = [
        [blocks[0]] + [swap(blocks[k], "rows", k) for k in range(1, shards)] for blocks in parcels
    ]
    order = list(range(shards))
    last = [got[-1][k] for k in order]

    cuts = [(c, 0, span) for c in range(CHUNKS)]
    own, other, img = [], [], []
    for c, lane0, wide in cuts:
        here = after(spot, *own) if own else spot
        taps, image = call(
            functools.partial(conv_kernel, (order, shard_rows, width, out_rows, c * span + lane0, lane0)),
            [
                jax.ShapeDtypeStruct((out_pixels, wide), f32),
                jax.ShapeDtypeStruct((out_pixels, wide), bf16),
            ],
            [SMEM] + [VMEM] * (shards + 1),
            [
                pltpu.VMEM((shards * shard_rows + 6, width + 16, LANES), f32),
                pltpu.VMEM((49, 8, LANES), f32),
            ],
            3 * mib,
            out_pixels * wide * 98 * 100,
            out_pixels * wide * 10,
        )(here, *[got[c][k] for k in order], dw_kernel)
        own.append(taps)
        img.append(image)
        other.append(swap(taps, "section", 1))

    (keys,) = call(
        functools.partial(unpack_kernel, (order, pixels)),
        [jax.ShapeDtypeStruct((shards * per_key // 2, depth), bf16)],
        [VMEM] * shards,
        [],
        mib,
        10**6,
        10**6,
    )(*after(last, *own))
    bits = [1 << n for n in reversed(range(batches.bit_length() - 1))]
    pieces = [keys, swap(keys, "batch", bits[0])]

    hid = w1.shape[1]
    part_pixels = out_pixels // 2
    z, z_other = [], []
    for p in range(2):
        here = after(spot, pieces[-1], *z) if p else after(spot, keys)
        (mine,) = call(
            functools.partial(block_kernel, (p * part_pixels, part_pixels, [w for _, _, w in cuts])),
            [jax.ShapeDtypeStruct((part_pixels, chans), f32)],
            [SMEM] + [VMEM] * (3 * len(cuts) + 4),
            [
                pltpu.VMEM((part_pixels, chans), bf16),
                pltpu.VMEM((part_pixels, hid), bf16),
                pltpu.VMEM((2, part_pixels, 512), f32),
            ],
            8 * mib,
            4 * part_pixels * hid * chans,
            4 * hid * chans,
        )(here, *own, *other, *img, ln_gain, layer_branch_scale, w1, w2)
        z.append(mine)
        z_other.append(swap(mine, "section", 1))
    for bit in bits[1:]:
        pieces.append(swap(join(*pieces), "batch", bit))

    hidden = pe.shape[1]
    (hid_a,) = call(
        expand_kernel,
        [jax.ShapeDtypeStruct((part_pixels, hidden), bf16)],
        [VMEM] * 3,
        [pltpu.VMEM((part_pixels, chans), bf16)],
        6 * mib,
        2 * part_pixels * hidden * chans,
        2 * hidden * chans,
    )(z[0], z_other[0], pe)
    (hot,) = call(
        functools.partial(prep_kernel, (order, shard_rows, width, out_pixels, parts)),
        [jax.ShapeDtypeStruct((9 * REG, out_pixels), bf16)],
        [SMEM] + [VMEM] * shards,
        [pltpu.VMEM((16, (shards + 2) * pixels), f32)],
        2 * mib,
        10**8,
        10**6,
    )(after(spot, hid_a), *last)
    (pooled,) = call(
        project_kernel,
        [jax.ShapeDtypeStruct((REG, out_dim), f32)],
        [VMEM] * 6,
        [
            pltpu.VMEM((part_pixels, chans), bf16),
            pltpu.VMEM((hidden // 256, out_pixels, 256), bf16),
        ],
        8 * mib,
        2 * part_pixels * hidden * chans + 4 * 9 * REG * hidden * out_pixels,
        4 * hidden * chans,
    )(z[1], z_other[1], hid_a, pe, pk, hot)
    pick, facts = call(
        functools.partial(owner_kernel, (order, shard_rows, pixels, images, batches, per_key)),
        [jax.ShapeDtypeStruct((owned, slots), bf16), jax.ShapeDtypeStruct((owned, LANES), f32)],
        [SMEM] + [VMEM] * (shards + 2),
        [],
        2 * mib,
        10**8,
        10**6,
    )(after(spot, pooled), *last, owner_slot, partner)
    total, send = call(
        add_kernel,
        [jax.ShapeDtypeStruct((REG, out_dim), f32), jax.ShapeDtypeStruct((REG, out_dim), bf16)],
        [VMEM] * 2,
        [],
        mib,
        10**5,
        10**5,
    )(pooled, swap(pooled, "section", 1))
    sums = [swap(send, "rows", k) if k else total for k in range(shards)]
    pieces[-1] = after(pieces[-1], pooled)
    pieces.append(swap(join(*pieces), "section", 1))
    count = sum(x.shape[0] for x in pieces)
    keys, length = call(
        keys_kernel,
        [jax.ShapeDtypeStruct((depth, count), bf16), jax.ShapeDtypeStruct((1, count), f32)],
        [VMEM] * len(pieces),
        [],
        4 * mib,
        10**9,
        10**6,
    )(*pieces)

    embed, loss = call(
        functools.partial(loss_kernel, (shards, parts)),
        [jax.ShapeDtypeStruct((owned, out_dim), f32), jax.ShapeDtypeStruct((1, owned), f32)],
        [SMEM] + [VMEM] * (len(sums) + 4),
        [pltpu.VMEM((slots, out_dim), f32)],
        6 * mib,
        10**8,
        10**6,
    )(spot, *sums, pick, facts, keys, length)
    return embed, loss.reshape(owned)


def solution(mesh):
    in_specs = (
        P("batch", "rows", None, None),
        P(),
        P(),
        P(None, "section"),
        P("section", None),
        P(),
        P(None, "section"),
        P(None, "section", None),
        P("batch", "rows", None),
        P("batch", None),
        P("batch", None),
        P(("batch", "rows"), None),
    )
    out_specs = (P(("batch", "rows"), None), P(("batch", "rows")))
    return jax.shard_map(body, mesh=mesh, in_specs=in_specs, out_specs=out_specs, check_vma=False)
```

```python
import functools

import jax
import jax.numpy as jnp
from jax import lax
from jax.experimental import pallas as pl
from jax.experimental.pallas import tpu as pltpu
from jax.sharding import PartitionSpec as P

REG = 64
LANES = 128
STRIP = 4
CHUNKS = 2

sharpness_divisor = 0.1
ln_eps = 1e-06
norm_eps = 1e-06

VMEM = pl.BlockSpec(memory_space=pltpu.VMEM)
SMEM = pl.BlockSpec(memory_space=pltpu.SMEM)
f32 = jnp.float32
bf16 = jnp.bfloat16


def call(kernel, outs, in_specs, scratch, limit, flops, nbytes):
    return pl.pallas_call(
        kernel,
        out_shape=outs,
        in_specs=in_specs,
        out_specs=[VMEM] * len(outs),
        scratch_shapes=scratch,
        compiler_params=pltpu.CompilerParams(vmem_limit_bytes=limit),
        cost_estimate=pl.CostEstimate(flops=flops, bytes_accessed=nbytes, transcendentals=0),
    )


def dot(a, b):
    return jnp.dot(a, b, preferred_element_type=f32)


def dot_nt(a, b):
    return lax.dot_general(a, b, (((1,), (1,)), ((), ())), preferred_element_type=f32)


def gelu(x):
    return 0.5 * x * (1.0 + lax.erf(x * 0.7071067811865476))


def split(x):
    hi = x.astype(bf16)
    return hi, (x - hi.astype(f32)).astype(bf16)


def blank_kernel(_, out_ref):
    out_ref[...] = jnp.full(out_ref.shape, -1.0, f32)


def pack_kernel(pos_ref, ids_ref, key_ref, blank_ref, tail_ref, line):
    section = pos_ref[3]
    keys, depth = key_ref.shape
    shard_rows, width = ids_ref.shape[1:]
    line[...] = blank_ref[...]
    for i in range(ids_ref.shape[0]):
        line[i * shard_rows : (i + 1) * shard_rows, 0:width] = ids_ref[i].astype(f32)
    tail_ref[...] = jnp.zeros(tail_ref.shape, bf16)
    tail_ref[:, depth : depth + LANES] = line[...].astype(bf16)
    tail_ref[0 : keys // 2, 0:depth] = key_ref[pl.ds(pl.multiple_of(section * (keys // 2), keys // 2), keys // 2), :]


def join_kernel(*refs):
    start = 0
    for ref in refs[:-1]:
        refs[-1][start : start + ref.shape[0], :] = ref[...]
        start += ref.shape[0]


def join(*arrays):
    rows = sum(x.shape[0] for x in arrays)
    shape = jax.ShapeDtypeStruct((rows, arrays[0].shape[1]), arrays[0].dtype)
    joined = call(join_kernel, [shape], [VMEM] * len(arrays), [], 1 << 20, 0, rows * 1024)(*arrays)
    return joined[0]


def add_kernel(a_ref, b_ref, out_ref, send_ref):
    out_ref[...] = a_ref[...] + b_ref[...]
    send_ref[...] = out_ref[...].astype(bf16)


def conv_kernel(geo, pos_ref, *refs):
    order, shard_rows, width, out_rows, first_lane, lane0 = geo
    shards = len(order)
    blocks = dict(zip(order, refs[:shards]))
    w_ref, taps, img_ref, xpad, wide = refs[shards:]
    chunk = taps.shape[1]
    row, first_row, col0 = pos_ref[0], pos_ref[1], pos_ref[2]
    height = shards * shard_rows
    pixels = shard_rows * width
    cols = xpad.shape[1]
    out_pixels = out_rows * width
    step_rows = STRIP

    xpad[0:3] = jnp.zeros((3, cols, LANES), f32)
    xpad[height + 3 : height + 6] = jnp.zeros((3, cols, LANES), f32)
    for y in range(3, height + 3):
        xpad[y, 0:8] = jnp.zeros((8, LANES), f32)
        xpad[y, 8 + width : 16 + width] = jnp.zeros((8, LANES), f32)

    def group(g, carry):
        lanes = pl.ds(pl.multiple_of(g * LANES, LANES), LANES)
        for k in range(shards):
            value = blocks[k][0:pixels, pl.ds(pl.multiple_of(lane0 + g * LANES, LANES), LANES)].astype(f32).reshape(shard_rows, width, LANES)
            xpad[pl.ds(3 + (row ^ k) * shard_rows, shard_rows), 8 : 8 + width, :] = value
        start = pos_ref[3] * (w_ref.shape[2] // 2) + first_lane + g * LANES
        for dy in range(7):
            w = w_ref[dy, :, pl.ds(pl.multiple_of(start, LANES), LANES)].astype(f32)
            for dx in range(7):
                wide[dy * 7 + dx] = jnp.broadcast_to(w[dx : dx + 1], (8, LANES))

        def strip(i, carry):
            top = first_row + i * step_rows
            acc = [jnp.zeros((width // 8, 8, LANES), f32) for _ in range(step_rows)]
            for r in range(step_rows + 6):
                for dx in range(7):
                    v = xpad[top + r, pl.ds(col0 + dx, width), :].reshape(width // 8, 8, LANES)
                    for j in range(step_rows):
                        dy = r - j
                        if 0 <= dy < 7:
                            acc[j] = acc[j] + v * wide[dy * 7 + dx][None]
            for j in range(step_rows):
                start = pl.multiple_of((i * step_rows + j) * width, width)
                taps[pl.ds(start, width), lanes] = acc[j].reshape(width, LANES)
            return carry

        return lax.fori_loop(0, out_rows // step_rows, strip, carry)

    lax.fori_loop(0, chunk // LANES, group, 0)

    for k in range(shards):
        start = (row ^ k) * pixels - first_row * width

        @pl.when((start >= 0) & (start < out_pixels))
        def _():
            img_ref[pl.ds(pl.multiple_of(start, pixels), pixels), :] = blocks[k][0:pixels, lane0 : lane0 + chunk]


def block_kernel(geo, pos_ref, *refs):
    first, pixels, widths = geo
    chunks = len(widths)
    own, other, img = refs[:chunks], refs[chunks : 2 * chunks], refs[2 * chunks : 3 * chunks]
    gain_ref, scale_ref, w1_ref, w2_ref, z_ref, normed, inner, wide = refs[3 * chunks :]
    chans, hid = w1_ref.shape
    half = chans // 2
    starts = [sum(widths[:c]) for c in range(chunks)]
    section = pos_ref[3]
    rows = slice(first, first + pixels)
    gains = gain_ref[...].astype(f32).reshape(1, chans)
    scales = scale_ref[...].astype(f32).reshape(1, chans)
    low = [gains[:, n : n + w] for n, w in zip(starts, widths)]
    high = [gains[:, half + n : half + n + w] for n, w in zip(starts, widths)]
    gains_own = [jnp.where(section == 0, x, y) for x, y in zip(low, high)]
    gains_other = [jnp.where(section == 0, y, x) for x, y in zip(low, high)]
    block = 32
    for r in range(pixels // block):
        part = slice(first + r * block, first + (r + 1) * block)
        values = [ref[part, :] for ref in own + other]
        mean = sum(jnp.sum(v, axis=1, keepdims=True) for v in values) * (1.0 / chans)
        values = [v - mean for v in values]
        spread = sum(jnp.sum(v * v, axis=1, keepdims=True) for v in values) * (1.0 / chans)
        inv = lax.rsqrt(spread + ln_eps)
        values = [(v * inv * g).astype(bf16) for v, g in zip(values, gains_own + gains_other)]
        to = slice(r * block, (r + 1) * block)
        for c in range(chunks):
            for side, value in ((section, values[c]), (1 - section, values[chunks + c])):
                start = pl.multiple_of(side * half + starts[c], LANES)
                normed[to, pl.ds(start, widths[c])] = value
    step = 512

    def widen(i):
        cols = slice(i * step, (i + 1) * step)
        return dot(normed[...], w1_ref[:, cols])

    wide[0] = widen(0)
    for i in range(hid // step):
        if i + 1 < hid // step:
            wide[(i + 1) % 2] = widen(i + 1)
        inner[:, i * step : (i + 1) * step] = gelu(wide[i % 2]).astype(bf16)
    step = half

    def image(start):
        found = []
        for c in range(chunks):
            low, high = max(start, starts[c]), min(start + step, starts[c] + widths[c])
            if low < high:
                found.append(img[c][rows, low - starts[c] : high - starts[c]])
        return found[0] if len(found) == 1 else jnp.concatenate(found, axis=1)

    for i in range(chans // step):
        cols = slice(i * step, (i + 1) * step)
        side, start = divmod(i * step, half)
        keep = jnp.where(section == side, 1.0, 0.0)
        z = dot(inner[...], w2_ref[:, cols]) * scales[:, cols]
        z_ref[:, cols] = z + image(start).astype(f32) * keep


def expand_kernel(z_ref, other_ref, pe_ref, out_ref, block):
    block[...] = (z_ref[...] + other_ref[...]).astype(bf16)
    step = 512
    for i in range(pe_ref.shape[1] // step):
        cols = slice(i * step, (i + 1) * step)
        out_ref[:, cols] = jnp.maximum(dot(block[...], pe_ref[:, cols]), 0.0).astype(bf16)


def prep_kernel(geo, pos_ref, *refs):
    order, shard_rows, width, out_pixels, parts = geo
    shards = len(order)
    ids = [refs[order.index(k)] for k in range(shards)]
    hot_ref, flat = refs[shards:]
    row, first_row = pos_ref[0], pos_ref[1]
    pixels = shard_rows * width
    depth = ids[0].shape[1] - LANES
    ids = [ref[pixels:, depth : depth + LANES].astype(f32) for ref in ids]
    image = row // parts
    flat[...] = jnp.full(flat.shape, -1.0, f32)
    for k in range(shards):
        start = pl.multiple_of((1 + (row ^ k)) * pixels, LANES)
        number = lax.broadcasted_iota(jnp.int32, ids[k].shape, 0)
        inside = lax.broadcasted_iota(jnp.int32, ids[k].shape, 1) < width
        for y in range(shard_rows):
            keep = inside & (number == image * shard_rows + y)
            mine = jnp.sum(jnp.where(keep, ids[k], 0.0), axis=0, keepdims=True)
            mine = jnp.broadcast_to(mine, (8, LANES))
            mine = pltpu.roll(mine, y * width, 1) if y else mine
            line = mine if y == 0 else line + mine
        flat[0:8, pl.ds(start, pixels)] = line
    total = flat.shape[1]
    whole = jnp.broadcast_to(flat[0:1, :], (8, total))
    lane = lax.broadcasted_iota(jnp.int32, (8, total), 1)
    col = lane % width
    region = lax.broadcasted_iota(jnp.int32, (REG, out_pixels), 0).astype(f32)
    start = pl.multiple_of(pixels + first_row * width, LANES)
    for dy in range(3):
        for dx in range(3):
            off = (dy - 1) * width + dx - 1
            moved = whole if off == 0 else pltpu.roll(whole, off % total, 1)
            if dx == 0:
                moved = jnp.where(col == width - 1, -1.0, moved)
            if dx == 2:
                moved = jnp.where(col == 0, -1.0, moved)
            flat[8:16, :] = moved
            line = flat[8:9, pl.ds(start, out_pixels)]
            tap = dy * 3 + dx
            hot_ref[tap * REG : (tap + 1) * REG, :] = jnp.where(region == line, 1.0, 0.0).astype(bf16)


def unpack_kernel(geo, *refs):
    order, pixels = geo
    keys_ref = refs[-1]
    count = keys_ref.shape[0] // len(order)
    for k, ref in zip(order, refs):
        keys_ref[k * count : (k + 1) * count, :] = ref[pixels : pixels + count, 0 : keys_ref.shape[1]]


def owner_kernel(geo, pos_ref, *refs):
    order, shard_rows, pixels, images, batches, per_key = geo
    shards = len(order)
    ids = [refs[order.index(k)] for k in range(shards)]
    owner_ref, partner_ref, pick_ref, own_ref = refs[shards:]
    row, batch, first_slot = pos_ref[0], pos_ref[4], pos_ref[5]
    depth = ids[0].shape[1] - LANES
    ids = [ref[pixels:, depth : depth + LANES].astype(f32) for ref in ids]
    owned, slots = pick_ref.shape
    slot = lax.broadcasted_iota(jnp.int32, (owned, slots), 1)
    want = lax.broadcasted_iota(jnp.int32, (owned, slots), 0) + first_slot
    pick = owner_ref[...] == want
    pick_ref[...] = jnp.where(pick, 1.0, 0.0).astype(bf16)
    one_region = lax.broadcasted_iota(jnp.int32, (REG, LANES), 0).astype(f32)
    tallies = []
    for i in range(images):
        tally = jnp.zeros((REG, LANES), f32)
        for k in range(shards):
            for y in range(i * shard_rows, (i + 1) * shard_rows):
                tally = tally + jnp.where(one_region == ids[k][y : y + 1, :], 1.0, 0.0)
        tallies.append(tally)
    tally = jnp.concatenate(tallies, axis=0).astype(bf16)
    count = dot_nt(jnp.ones((8, LANES), bf16), tally)[0:1]
    mates = jnp.concatenate([partner_ref[i : i + 1, :] for i in range(images)], axis=1)
    mate = (batch * images + slot // REG) * REG + mates
    block = mate // per_key
    within = mate % per_key
    core = (within // (per_key // 2)) ^ pos_ref[3]
    apart = (block // shards) ^ batch
    turn = core
    for n in range(batches.bit_length() - 1):
        turn = turn * 2 + ((apart >> n) & 1)
    place = turn * shards + ((block % shards) ^ row)
    place = place * (per_key // 2) + within % (per_key // 2)
    place = jnp.sum(jnp.where(pick, place, 0).astype(f32), axis=1, keepdims=True)
    number = jnp.sum(jnp.where(pick, count, 0.0), axis=1, keepdims=True)
    side = lax.broadcasted_iota(jnp.int32, (owned, LANES), 1)
    own_ref[...] = jnp.where(side == 0, place, jnp.where(side == 1, number, 0.0))


def project_kernel(z_ref, other_ref, first_ref, pe_ref, pk_ref, hot_ref, out_ref, block, hidden):
    before = first_ref.shape[0]
    pixels = z_ref.shape[0]
    taps = pk_ref.shape[0]
    block[...] = (z_ref[...] + other_ref[...]).astype(bf16)
    step = 256
    acc = jnp.zeros((2 * REG, out_ref.shape[1]), f32)
    for i in range(pe_ref.shape[1] // step):
        cols = slice(i * step, (i + 1) * step)
        hidden[i, 0:before, :] = first_ref[:, cols]
        h = jnp.maximum(dot(block[...], pe_ref[:, cols]), 0.0)
        hidden[i, before : before + pixels, :] = h.astype(bf16)
        sums = dot(hot_ref[...], hidden[i])
        hi = sums.astype(bf16)
        lo = (sums - hi.astype(f32)).astype(bf16)
        for t in range(taps):
            rows = slice(t * REG, (t + 1) * REG)
            both = jnp.concatenate([hi[rows], lo[rows]], axis=0)
            acc = acc + dot(both, pk_ref[t, cols, :])
    out_ref[...] = acc[0:REG] + acc[REG:]


def keys_kernel(*refs):
    keys_ref, length_ref = refs[-2:]
    keys = jnp.concatenate([ref[...] for ref in refs[:-2]], axis=0).astype(f32).T
    keys_ref[...] = keys.astype(bf16)
    length_ref[...] = lax.rsqrt(jnp.sum(keys * keys, axis=0, keepdims=True) + norm_eps)


def loss_kernel(geo, *refs):
    shards, parts = geo
    sums, row = refs[1 : shards + 1], refs[0][0]
    pick_ref, own_ref, keys_ref, length_ref, embed_ref, loss_ref, table = refs[shards + 1 :]
    if parts > 1:
        table[...] = jnp.zeros(table.shape, f32)
    for k in range(shards):
        place = pl.ds(pl.multiple_of(((row ^ k) // parts) * REG, REG), REG)
        value = sums[k][...].astype(f32)
        table[place, :] = value if parts == 1 else table[place, :] + value
    pick = pick_ref[...]
    hi, lo = split(table[...])
    ordered = dot(pick, hi) + dot(pick, lo)
    unit = ordered * lax.rsqrt(jnp.sum(ordered * ordered, axis=1, keepdims=True) + norm_eps)
    embed_ref[...] = unit
    owned = unit.shape[0]
    both = dot(jnp.concatenate(split(unit), axis=0), keys_ref[...])
    logits = both[0:owned] + both[owned:]
    logits = logits * (length_ref[...] / sharpness_divisor)
    total = jnp.log(jnp.sum(jnp.exp(logits), axis=1, keepdims=True))
    column = lax.broadcasted_iota(jnp.int32, logits.shape, 1).astype(f32)
    match = jnp.sum(jnp.where(column == own_ref[:, 0:1], logits, 0.0), axis=1, keepdims=True)
    loss = jnp.where(own_ref[:, 1:2] > 0.5, total - match, 0.0)
    line = lax.broadcasted_iota(jnp.int32, (owned, owned), 0)
    other = lax.broadcasted_iota(jnp.int32, (owned, owned), 1)
    loss_ref[...] = jnp.sum(jnp.where(line == other, loss, 0.0), axis=0, keepdims=True)


def swap(x, axis, bit):
    return lax.ppermute(x, axis, [(i, i ^ bit) for i in range(lax.axis_size(axis))])


def body(
    features,
    dw_kernel,
    ln_gain,
    widening_pointwise_matrix,
    w_reduce,
    layer_branch_scale,
    p_expand,
    p_kernel,
    region_ids,
    owner_slot,
    partner,
    key_embed,
):
    images, shard_rows, width, chans = features.shape
    shards = lax.axis_size("rows")
    batches = lax.axis_size("batch")
    row = lax.axis_index("rows")
    batch = lax.axis_index("batch")
    section = lax.axis_index("section")
    half = chans // lax.axis_size("section")
    parts = shards // images
    out_rows = shards * shard_rows // parts
    pixels = shard_rows * width
    out_pixels = out_rows * width
    slots = images * REG
    owned = slots // shards
    out_dim = p_kernel.shape[2]
    mib = 1 << 20
    span = half // CHUNKS

    w1, w2, pe, pk = widening_pointwise_matrix, w_reduce, p_expand, p_kernel
    first_row = (row % parts) * out_rows
    spot = jnp.stack(
        [row, first_row, jnp.int32(5), section, batch, row * owned]
    ).astype(jnp.int32)

    per_key, depth = key_embed.shape
    tail = max(-(-images * shard_rows // 16) * 16, per_key // 2)
    def after(here, *done):
        return lax.optimization_barrier((here, *done))[0]

    parcels = []
    for c in range(CHUNKS):
        blocks = []
        for k in range(shards):
            place = ((row ^ k) // parts, 0, 0, section * half + c * span)
            part = lax.dynamic_slice(features, place, (1, shard_rows, width, span))
            blocks.append(part.reshape(pixels, span))
        parcels.append(blocks)
    (blank,) = call(
        blank_kernel, [jax.ShapeDtypeStruct((tail, LANES), f32)], [VMEM], [], mib, 10**10, 10**4
    )(parcels[0][0])
    parcels[0] = after(parcels[0], blank)
    (riders,) = call(
        pack_kernel,
        [jax.ShapeDtypeStruct((tail, span), bf16)],
        [SMEM] + [VMEM] * 3,
        [pltpu.VMEM((tail, LANES), f32)],
        mib,
        0,
        10**6,
    )(spot, region_ids, key_embed, blank)
    parcels[-1] = [jnp.concatenate([part, riders], axis=0) for part in parcels[-1]]
    got = [
        [blocks[0]] + [swap(blocks[k], "rows", k) for k in range(1, shards)] for blocks in parcels
    ]
    order = list(range(shards))
    last = [got[-1][k] for k in order]

    late = span - LANES
    cuts = [(c, 0, span) for c in range(CHUNKS - 1)]
    cuts += [(CHUNKS - 1, 0, late), (CHUNKS - 1, late, span - late)]
    own, other, img = [], [], []
    for c, lane0, wide in cuts:
        here = after(spot, *own) if own else after(spot, *parcels[-1])
        taps, image = call(
            functools.partial(conv_kernel, (order, shard_rows, width, out_rows, c * span + lane0, lane0)),
            [
                jax.ShapeDtypeStruct((out_pixels, wide), f32),
                jax.ShapeDtypeStruct((out_pixels, wide), bf16),
            ],
            [SMEM] + [VMEM] * (shards + 1),
            [
                pltpu.VMEM((shards * shard_rows + 6, width + 16, LANES), f32),
                pltpu.VMEM((49, 8, LANES), f32),
            ],
            3 * mib,
            out_pixels * span * 98 * 100,
            out_pixels * wide * 10,
        )(here, *[got[c][k] for k in order], dw_kernel)
        own.append(taps)
        img.append(image)
        other.append(swap(taps, "section", 1))

    (keys,) = call(
        functools.partial(unpack_kernel, (order, pixels)),
        [jax.ShapeDtypeStruct((shards * per_key // 2, depth), bf16)],
        [VMEM] * shards,
        [],
        mib,
        10**6,
        10**6,
    )(*after(last, *own))
    bits = [1 << n for n in reversed(range(batches.bit_length() - 1))]
    pieces = [keys, swap(keys, "batch", bits[0])]

    hid = w1.shape[1]
    part_pixels = out_pixels // 2
    z, z_other = [], []
    for p in range(2):
        here = after(spot, pieces[-1], *z) if p else after(spot, keys)
        (mine,) = call(
            functools.partial(block_kernel, (p * part_pixels, part_pixels, [w for _, _, w in cuts])),
            [jax.ShapeDtypeStruct((part_pixels, chans), f32)],
            [SMEM] + [VMEM] * (3 * len(cuts) + 4),
            [
                pltpu.VMEM((part_pixels, chans), bf16),
                pltpu.VMEM((part_pixels, hid), bf16),
                pltpu.VMEM((2, part_pixels, 512), f32),
            ],
            8 * mib,
            4 * part_pixels * hid * chans,
            4 * hid * chans,
        )(here, *own, *other, *img, ln_gain, layer_branch_scale, w1, w2)
        z.append(mine)
        z_other.append(swap(mine, "section", 1))
    for bit in bits[1:]:
        pieces.append(swap(join(*pieces), "batch", bit))

    hidden = pe.shape[1]
    (hid_a,) = call(
        expand_kernel,
        [jax.ShapeDtypeStruct((part_pixels, hidden), bf16)],
        [VMEM] * 3,
        [pltpu.VMEM((part_pixels, chans), bf16)],
        6 * mib,
        2 * part_pixels * hidden * chans,
        2 * hidden * chans,
    )(z[0], z_other[0], pe)
    (hot,) = call(
        functools.partial(prep_kernel, (order, shard_rows, width, out_pixels, parts)),
        [jax.ShapeDtypeStruct((9 * REG, out_pixels), bf16)],
        [SMEM] + [VMEM] * shards,
        [pltpu.VMEM((16, (shards + 2) * pixels), f32)],
        2 * mib,
        10**8,
        10**6,
    )(after(spot, hid_a), *last)
    (pooled,) = call(
        project_kernel,
        [jax.ShapeDtypeStruct((REG, out_dim), f32)],
        [VMEM] * 6,
        [
            pltpu.VMEM((part_pixels, chans), bf16),
            pltpu.VMEM((hidden // 256, out_pixels, 256), bf16),
        ],
        8 * mib,
        2 * part_pixels * hidden * chans + 4 * 9 * REG * hidden * out_pixels,
        4 * hidden * chans,
    )(z[1], z_other[1], hid_a, pe, pk, hot)
    pick, facts = call(
        functools.partial(owner_kernel, (order, shard_rows, pixels, images, batches, per_key)),
        [jax.ShapeDtypeStruct((owned, slots), bf16), jax.ShapeDtypeStruct((owned, LANES), f32)],
        [SMEM] + [VMEM] * (shards + 2),
        [],
        2 * mib,
        10**8,
        10**6,
    )(after(spot, pooled), *last, owner_slot, partner)
    total, send = call(
        add_kernel,
        [jax.ShapeDtypeStruct((REG, out_dim), f32), jax.ShapeDtypeStruct((REG, out_dim), bf16)],
        [VMEM] * 2,
        [],
        mib,
        10**5,
        10**5,
    )(pooled, swap(pooled, "section", 1))
    sums = [swap(send, "rows", k) if k else total for k in range(shards)]
    pieces[-1] = after(pieces[-1], pooled)
    pieces.append(swap(join(*pieces), "section", 1))
    count = sum(x.shape[0] for x in pieces)
    keys, length = call(
        keys_kernel,
        [jax.ShapeDtypeStruct((depth, count), bf16), jax.ShapeDtypeStruct((1, count), f32)],
        [VMEM] * len(pieces),
        [],
        4 * mib,
        10**9,
        10**6,
    )(*pieces)

    embed, loss = call(
        functools.partial(loss_kernel, (shards, parts)),
        [jax.ShapeDtypeStruct((owned, out_dim), f32), jax.ShapeDtypeStruct((1, owned), f32)],
        [SMEM] + [VMEM] * (len(sums) + 4),
        [pltpu.VMEM((slots, out_dim), f32)],
        6 * mib,
        10**8,
        10**6,
    )(spot, *sums, pick, facts, keys, length)
    return embed, loss.reshape(owned)


def solution(mesh):
    in_specs = (
        P("batch", "rows", None, None),
        P(),
        P(),
        P(None, "section"),
        P("section", None),
        P(),
        P(None, "section"),
        P(None, "section", None),
        P("batch", "rows", None),
        P("batch", None),
        P("batch", None),
        P(("batch", "rows"), None),
    )
    out_specs = (P(("batch", "rows"), None), P(("batch", "rows")))
    return jax.shard_map(body, mesh=mesh, in_specs=in_specs, out_specs=out_specs, check_vma=False)
```

```python
import functools

import jax
import jax.numpy as jnp
from jax import lax
from jax.experimental import pallas as pl
from jax.experimental.pallas import tpu as pltpu
from jax.sharding import PartitionSpec as P

REG = 64
LANES = 128
STRIP = 4
CHUNKS = 2

sharpness_divisor = 0.1
ln_eps = 1e-06
norm_eps = 1e-06

VMEM = pl.BlockSpec(memory_space=pltpu.VMEM)
SMEM = pl.BlockSpec(memory_space=pltpu.SMEM)
f32 = jnp.float32
bf16 = jnp.bfloat16


def call(kernel, outs, in_specs, scratch, limit, flops, nbytes):
    return pl.pallas_call(
        kernel,
        out_shape=outs,
        in_specs=in_specs,
        out_specs=[VMEM] * len(outs),
        scratch_shapes=scratch,
        compiler_params=pltpu.CompilerParams(vmem_limit_bytes=limit),
        cost_estimate=pl.CostEstimate(flops=flops, bytes_accessed=nbytes, transcendentals=0),
    )


def dot(a, b):
    return jnp.dot(a, b, preferred_element_type=f32)


def dot_nt(a, b):
    return lax.dot_general(a, b, (((1,), (1,)), ((), ())), preferred_element_type=f32)


def gelu(x):
    return 0.5 * x * (1.0 + lax.erf(x * 0.7071067811865476))


def split(x):
    hi = x.astype(bf16)
    return hi, (x - hi.astype(f32)).astype(bf16)


def blank_kernel(_, out_ref):
    out_ref[...] = jnp.full(out_ref.shape, -1.0, f32)


def pack_kernel(pos_ref, ids_ref, key_ref, blank_ref, tail_ref, line):
    section = pos_ref[3]
    keys, depth = key_ref.shape
    shard_rows, width = ids_ref.shape[1:]
    line[...] = blank_ref[...]
    for i in range(ids_ref.shape[0]):
        line[i * shard_rows : (i + 1) * shard_rows, 0:width] = ids_ref[i].astype(f32)
    tail_ref[...] = jnp.zeros(tail_ref.shape, bf16)
    tail_ref[:, depth : depth + LANES] = line[...].astype(bf16)
    tail_ref[0 : keys // 2, 0:depth] = key_ref[pl.ds(pl.multiple_of(section * (keys // 2), keys // 2), keys // 2), :]


def join_kernel(*refs):
    start = 0
    for ref in refs[:-1]:
        refs[-1][start : start + ref.shape[0], :] = ref[...]
        start += ref.shape[0]


def join(*arrays):
    rows = sum(x.shape[0] for x in arrays)
    shape = jax.ShapeDtypeStruct((rows, arrays[0].shape[1]), arrays[0].dtype)
    joined = call(join_kernel, [shape], [VMEM] * len(arrays), [], 1 << 20, 0, rows * 1024)(*arrays)
    return joined[0]


def add_kernel(a_ref, b_ref, out_ref, send_ref):
    out_ref[...] = a_ref[...] + b_ref[...]
    send_ref[...] = out_ref[...].astype(bf16)


def conv_kernel(geo, pos_ref, *refs):
    order, shard_rows, width, out_rows, first_lane, lane0 = geo
    shards = len(order)
    blocks = dict(zip(order, refs[:shards]))
    w_ref, taps, img_ref, xpad, wide = refs[shards:]
    chunk = taps.shape[1]
    row, first_row, col0 = pos_ref[0], pos_ref[1], pos_ref[2]
    height = shards * shard_rows
    pixels = shard_rows * width
    cols = xpad.shape[1]
    out_pixels = out_rows * width
    step_rows = STRIP

    xpad[0:3] = jnp.zeros((3, cols, LANES), f32)
    xpad[height + 3 : height + 6] = jnp.zeros((3, cols, LANES), f32)
    for y in range(3, height + 3):
        xpad[y, 0:8] = jnp.zeros((8, LANES), f32)
        xpad[y, 8 + width : 16 + width] = jnp.zeros((8, LANES), f32)

    def group(g, carry):
        lanes = pl.ds(pl.multiple_of(g * LANES, LANES), LANES)
        for k in range(shards):
            value = blocks[k][0:pixels, pl.ds(pl.multiple_of(lane0 + g * LANES, LANES), LANES)].astype(f32).reshape(shard_rows, width, LANES)
            xpad[pl.ds(3 + (row ^ k) * shard_rows, shard_rows), 8 : 8 + width, :] = value
        start = pos_ref[3] * (w_ref.shape[2] // 2) + first_lane + g * LANES
        for dy in range(7):
            w = w_ref[dy, :, pl.ds(pl.multiple_of(start, LANES), LANES)].astype(f32)
            for dx in range(7):
                wide[dy * 7 + dx] = jnp.broadcast_to(w[dx : dx + 1], (8, LANES))

        def strip(i, carry):
            top = first_row + i * step_rows
            acc = [jnp.zeros((width // 8, 8, LANES), f32) for _ in range(step_rows)]
            for r in range(step_rows + 6):
                for dx in range(7):
                    v = xpad[top + r, pl.ds(col0 + dx, width), :].reshape(width // 8, 8, LANES)
                    for j in range(step_rows):
                        dy = r - j
                        if 0 <= dy < 7:
                            acc[j] = acc[j] + v * wide[dy * 7 + dx][None]
            for j in range(step_rows):
                start = pl.multiple_of((i * step_rows + j) * width, width)
                taps[pl.ds(start, width), lanes] = acc[j].reshape(width, LANES)
            return carry

        return lax.fori_loop(0, out_rows // step_rows, strip, carry)

    lax.fori_loop(0, chunk // LANES, group, 0)

    for k in range(shards):
        start = (row ^ k) * pixels - first_row * width

        @pl.when((start >= 0) & (start < out_pixels))
        def _():
            img_ref[pl.ds(pl.multiple_of(start, pixels), pixels), :] = blocks[k][0:pixels, lane0 : lane0 + chunk]


def block_kernel(geo, pos_ref, *refs):
    first, pixels, widths = geo
    chunks = len(widths)
    own, other, img = refs[:chunks], refs[chunks : 2 * chunks], refs[2 * chunks : 3 * chunks]
    gain_ref, scale_ref, w1_ref, w2_ref, z_ref, normed, inner, wide = refs[3 * chunks :]
    chans, hid = w1_ref.shape
    half = chans // 2
    starts = [sum(widths[:c]) for c in range(chunks)]
    section = pos_ref[3]
    rows = slice(first, first + pixels)
    gains = gain_ref[...].astype(f32).reshape(1, chans)
    scales = scale_ref[...].astype(f32).reshape(1, chans)
    low = [gains[:, n : n + w] for n, w in zip(starts, widths)]
    high = [gains[:, half + n : half + n + w] for n, w in zip(starts, widths)]
    gains_own = [jnp.where(section == 0, x, y) for x, y in zip(low, high)]
    gains_other = [jnp.where(section == 0, y, x) for x, y in zip(low, high)]
    block = 32
    for r in range(pixels // block):
        part = slice(first + r * block, first + (r + 1) * block)
        values = [ref[part, :] for ref in own + other]
        mean = sum(jnp.sum(v, axis=1, keepdims=True) for v in values) * (1.0 / chans)
        values = [v - mean for v in values]
        spread = sum(jnp.sum(v * v, axis=1, keepdims=True) for v in values) * (1.0 / chans)
        inv = lax.rsqrt(spread + ln_eps)
        values = [(v * inv * g).astype(bf16) for v, g in zip(values, gains_own + gains_other)]
        to = slice(r * block, (r + 1) * block)
        for c in range(chunks):
            for side, value in ((section, values[c]), (1 - section, values[chunks + c])):
                start = pl.multiple_of(side * half + starts[c], LANES)
                normed[to, pl.ds(start, widths[c])] = value
    step = 512

    def widen(i):
        cols = slice(i * step, (i + 1) * step)
        return dot(normed[...], w1_ref[:, cols])

    wide[0] = widen(0)
    for i in range(hid // step):
        if i + 1 < hid // step:
            wide[(i + 1) % 2] = widen(i + 1)
        inner[:, i * step : (i + 1) * step] = gelu(wide[i % 2]).astype(bf16)
    step = half

    def image(start):
        found = []
        for c in range(chunks):
            low, high = max(start, starts[c]), min(start + step, starts[c] + widths[c])
            if low < high:
                found.append(img[c][rows, low - starts[c] : high - starts[c]])
        return found[0] if len(found) == 1 else jnp.concatenate(found, axis=1)

    for i in range(chans // step):
        cols = slice(i * step, (i + 1) * step)
        side, start = divmod(i * step, half)
        keep = jnp.where(section == side, 1.0, 0.0)
        z = dot(inner[...], w2_ref[:, cols]) * scales[:, cols]
        z_ref[:, cols] = z + image(start).astype(f32) * keep


def expand_kernel(z_ref, other_ref, pe_ref, out_ref, block):
    block[...] = (z_ref[...] + other_ref[...]).astype(bf16)
    step = 512
    for i in range(pe_ref.shape[1] // step):
        cols = slice(i * step, (i + 1) * step)
        out_ref[:, cols] = jnp.maximum(dot(block[...], pe_ref[:, cols]), 0.0).astype(bf16)


def prep_kernel(geo, pos_ref, *refs):
    order, shard_rows, width, out_pixels, parts = geo
    shards = len(order)
    ids = [refs[order.index(k)] for k in range(shards)]
    hot_ref, flat = refs[shards:]
    row, first_row = pos_ref[0], pos_ref[1]
    pixels = shard_rows * width
    depth = ids[0].shape[1] - LANES
    ids = [ref[pixels:, depth : depth + LANES].astype(f32) for ref in ids]
    image = row // parts
    flat[...] = jnp.full(flat.shape, -1.0, f32)
    for k in range(shards):
        start = pl.multiple_of((1 + (row ^ k)) * pixels, LANES)
        number = lax.broadcasted_iota(jnp.int32, ids[k].shape, 0)
        inside = lax.broadcasted_iota(jnp.int32, ids[k].shape, 1) < width
        for y in range(shard_rows):
            keep = inside & (number == image * shard_rows + y)
            mine = jnp.sum(jnp.where(keep, ids[k], 0.0), axis=0, keepdims=True)
            mine = jnp.broadcast_to(mine, (8, LANES))
            mine = pltpu.roll(mine, y * width, 1) if y else mine
            line = mine if y == 0 else line + mine
        flat[0:8, pl.ds(start, pixels)] = line
    total = flat.shape[1]
    whole = jnp.broadcast_to(flat[0:1, :], (8, total))
    lane = lax.broadcasted_iota(jnp.int32, (8, total), 1)
    col = lane % width
    region = lax.broadcasted_iota(jnp.int32, (REG, out_pixels), 0).astype(f32)
    start = pl.multiple_of(pixels + first_row * width, LANES)
    for dy in range(3):
        for dx in range(3):
            off = (dy - 1) * width + dx - 1
            moved = whole if off == 0 else pltpu.roll(whole, off % total, 1)
            if dx == 0:
                moved = jnp.where(col == width - 1, -1.0, moved)
            if dx == 2:
                moved = jnp.where(col == 0, -1.0, moved)
            flat[8:16, :] = moved
            line = flat[8:9, pl.ds(start, out_pixels)]
            tap = dy * 3 + dx
            hot_ref[tap * REG : (tap + 1) * REG, :] = jnp.where(region == line, 1.0, 0.0).astype(bf16)


def unpack_kernel(geo, *refs):
    order, pixels = geo
    keys_ref = refs[-1]
    count = keys_ref.shape[0] // len(order)
    for k, ref in zip(order, refs):
        keys_ref[k * count : (k + 1) * count, :] = ref[pixels : pixels + count, 0 : keys_ref.shape[1]]


def owner_kernel(geo, pos_ref, *refs):
    order, shard_rows, pixels, images, batches, per_key = geo
    shards = len(order)
    ids = [refs[order.index(k)] for k in range(shards)]
    owner_ref, partner_ref, pick_ref, own_ref = refs[shards:]
    row, batch, first_slot = pos_ref[0], pos_ref[4], pos_ref[5]
    depth = ids[0].shape[1] - LANES
    ids = [ref[pixels:, depth : depth + LANES].astype(f32) for ref in ids]
    owned, slots = pick_ref.shape
    slot = lax.broadcasted_iota(jnp.int32, (owned, slots), 1)
    want = lax.broadcasted_iota(jnp.int32, (owned, slots), 0) + first_slot
    pick = owner_ref[...] == want
    pick_ref[...] = jnp.where(pick, 1.0, 0.0).astype(bf16)
    one_region = lax.broadcasted_iota(jnp.int32, (REG, LANES), 0).astype(f32)
    tallies = []
    for i in range(images):
        tally = jnp.zeros((REG, LANES), f32)
        for k in range(shards):
            for y in range(i * shard_rows, (i + 1) * shard_rows):
                tally = tally + jnp.where(one_region == ids[k][y : y + 1, :], 1.0, 0.0)
        tallies.append(tally)
    tally = jnp.concatenate(tallies, axis=0).astype(bf16)
    count = dot_nt(jnp.ones((8, LANES), bf16), tally)[0:1]
    mates = jnp.concatenate([partner_ref[i : i + 1, :] for i in range(images)], axis=1)
    mate = (batch * images + slot // REG) * REG + mates
    block = mate // per_key
    within = mate % per_key
    core = (within // (per_key // 2)) ^ pos_ref[3]
    apart = (block // shards) ^ batch
    turn = core
    for n in range(batches.bit_length() - 1):
        turn = turn * 2 + ((apart >> n) & 1)
    place = turn * shards + ((block % shards) ^ row)
    place = place * (per_key // 2) + within % (per_key // 2)
    place = jnp.sum(jnp.where(pick, place, 0).astype(f32), axis=1, keepdims=True)
    number = jnp.sum(jnp.where(pick, count, 0.0), axis=1, keepdims=True)
    side = lax.broadcasted_iota(jnp.int32, (owned, LANES), 1)
    own_ref[...] = jnp.where(side == 0, place, jnp.where(side == 1, number, 0.0))


def project_kernel(z_ref, other_ref, first_ref, pe_ref, pk_ref, hot_ref, out_ref, block, hidden):
    before = first_ref.shape[0]
    pixels = z_ref.shape[0]
    taps = pk_ref.shape[0]
    block[...] = (z_ref[...] + other_ref[...]).astype(bf16)
    step = 512
    acc = jnp.zeros((2 * REG, out_ref.shape[1]), f32)
    for i in range(pe_ref.shape[1] // step):
        cols = slice(i * step, (i + 1) * step)
        hidden[i, 0:before, :] = first_ref[:, cols]
        h = jnp.maximum(dot(block[...], pe_ref[:, cols]), 0.0)
        hidden[i, before : before + pixels, :] = h.astype(bf16)
        sums = dot(hot_ref[...], hidden[i])
        hi = sums.astype(bf16)
        lo = (sums - hi.astype(f32)).astype(bf16)
        for t in range(taps):
            rows = slice(t * REG, (t + 1) * REG)
            both = jnp.concatenate([hi[rows], lo[rows]], axis=0)
            acc = acc + dot(both, pk_ref[t, cols, :])
    out_ref[...] = acc[0:REG] + acc[REG:]


def keys_kernel(*refs):
    keys_ref, length_ref = refs[-2:]
    keys = jnp.concatenate([ref[...] for ref in refs[:-2]], axis=0).astype(f32).T
    keys_ref[...] = keys.astype(bf16)
    length_ref[...] = lax.rsqrt(jnp.sum(keys * keys, axis=0, keepdims=True) + norm_eps)


def loss_kernel(geo, *refs):
    shards, parts = geo
    sums, row = refs[1 : shards + 1], refs[0][0]
    pick_ref, own_ref, keys_ref, length_ref, embed_ref, loss_ref, table = refs[shards + 1 :]
    if parts > 1:
        table[...] = jnp.zeros(table.shape, f32)
    for k in range(shards):
        place = pl.ds(pl.multiple_of(((row ^ k) // parts) * REG, REG), REG)
        value = sums[k][...].astype(f32)
        table[place, :] = value if parts == 1 else table[place, :] + value
    pick = pick_ref[...]
    hi, lo = split(table[...])
    ordered = dot(pick, hi) + dot(pick, lo)
    unit = ordered * lax.rsqrt(jnp.sum(ordered * ordered, axis=1, keepdims=True) + norm_eps)
    embed_ref[...] = unit
    owned = unit.shape[0]
    both = dot(jnp.concatenate(split(unit), axis=0), keys_ref[...])
    logits = both[0:owned] + both[owned:]
    logits = logits * (length_ref[...] / sharpness_divisor)
    total = jnp.log(jnp.sum(jnp.exp(logits), axis=1, keepdims=True))
    column = lax.broadcasted_iota(jnp.int32, logits.shape, 1).astype(f32)
    match = jnp.sum(jnp.where(column == own_ref[:, 0:1], logits, 0.0), axis=1, keepdims=True)
    loss = jnp.where(own_ref[:, 1:2] > 0.5, total - match, 0.0)
    line = lax.broadcasted_iota(jnp.int32, (owned, owned), 0)
    other = lax.broadcasted_iota(jnp.int32, (owned, owned), 1)
    loss_ref[...] = jnp.sum(jnp.where(line == other, loss, 0.0), axis=0, keepdims=True)


def swap(x, axis, bit):
    return lax.ppermute(x, axis, [(i, i ^ bit) for i in range(lax.axis_size(axis))])


def body(
    features,
    dw_kernel,
    ln_gain,
    widening_pointwise_matrix,
    w_reduce,
    layer_branch_scale,
    p_expand,
    p_kernel,
    region_ids,
    owner_slot,
    partner,
    key_embed,
):
    images, shard_rows, width, chans = features.shape
    shards = lax.axis_size("rows")
    batches = lax.axis_size("batch")
    row = lax.axis_index("rows")
    batch = lax.axis_index("batch")
    section = lax.axis_index("section")
    half = chans // lax.axis_size("section")
    parts = shards // images
    out_rows = shards * shard_rows // parts
    pixels = shard_rows * width
    out_pixels = out_rows * width
    slots = images * REG
    owned = slots // shards
    out_dim = p_kernel.shape[2]
    mib = 1 << 20
    span = half // CHUNKS

    w1, w2, pe, pk = widening_pointwise_matrix, w_reduce, p_expand, p_kernel
    first_row = (row % parts) * out_rows
    spot = jnp.stack(
        [row, first_row, jnp.int32(5), section, batch, row * owned]
    ).astype(jnp.int32)

    per_key, depth = key_embed.shape
    tail = max(-(-images * shard_rows // 16) * 16, per_key // 2)
    def after(here, *done):
        return lax.optimization_barrier((here, *done))[0]

    parcels = []
    for c in range(CHUNKS):
        blocks = []
        for k in range(shards):
            place = ((row ^ k) // parts, 0, 0, section * half + c * span)
            part = lax.dynamic_slice(features, place, (1, shard_rows, width, span))
            blocks.append(part.reshape(pixels, span))
        parcels.append(blocks)
    (blank,) = call(
        blank_kernel, [jax.ShapeDtypeStruct((tail, LANES), f32)], [VMEM], [], mib, 10**10, 10**4
    )(parcels[0][0])
    parcels[0] = after(parcels[0], blank)
    (riders,) = call(
        pack_kernel,
        [jax.ShapeDtypeStruct((tail, span), bf16)],
        [SMEM] + [VMEM] * 3,
        [pltpu.VMEM((tail, LANES), f32)],
        mib,
        0,
        10**6,
    )(spot, region_ids, key_embed, blank)
    parcels[-1] = [jnp.concatenate([part, riders], axis=0) for part in parcels[-1]]
    got = [
        [blocks[0]] + [swap(blocks[k], "rows", k) for k in range(1, shards)] for blocks in parcels
    ]
    order = list(range(shards))
    last = [got[-1][k] for k in order]

    cuts = [(c, 0, span) for c in range(CHUNKS)]
    own, other, img = [], [], []
    for c, lane0, wide in cuts:
        here = after(spot, *own) if own else spot
        taps, image = call(
            functools.partial(conv_kernel, (order, shard_rows, width, out_rows, c * span + lane0, lane0)),
            [
                jax.ShapeDtypeStruct((out_pixels, wide), f32),
                jax.ShapeDtypeStruct((out_pixels, wide), bf16),
            ],
            [SMEM] + [VMEM] * (shards + 1),
            [
                pltpu.VMEM((shards * shard_rows + 6, width + 16, LANES), f32),
                pltpu.VMEM((49, 8, LANES), f32),
            ],
            3 * mib,
            out_pixels * wide * 98 * 100,
            out_pixels * wide * 10,
        )(here, *[got[c][k] for k in order], dw_kernel)
        own.append(taps)
        img.append(image)
        other.append(swap(taps, "section", 1))

    (keys,) = call(
        functools.partial(unpack_kernel, (order, pixels)),
        [jax.ShapeDtypeStruct((shards * per_key // 2, depth), bf16)],
        [VMEM] * shards,
        [],
        mib,
        10**6,
        10**6,
    )(*after(last, *own))
    bits = [1 << n for n in reversed(range(batches.bit_length() - 1))]
    pieces = [keys, swap(keys, "batch", bits[0])]

    hid = w1.shape[1]
    part_pixels = out_pixels // 2
    z, z_other = [], []
    for p in range(2):
        here = after(spot, pieces[-1], *z) if p else after(spot, keys)
        (mine,) = call(
            functools.partial(block_kernel, (p * part_pixels, part_pixels, [w for _, _, w in cuts])),
            [jax.ShapeDtypeStruct((part_pixels, chans), f32)],
            [SMEM] + [VMEM] * (3 * len(cuts) + 4),
            [
                pltpu.VMEM((part_pixels, chans), bf16),
                pltpu.VMEM((part_pixels, hid), bf16),
                pltpu.VMEM((2, part_pixels, 512), f32),
            ],
            8 * mib,
            4 * part_pixels * hid * chans,
            4 * hid * chans,
        )(here, *own, *other, *img, ln_gain, layer_branch_scale, w1, w2)
        z.append(mine)
        z_other.append(swap(mine, "section", 1))
    for bit in bits[1:]:
        pieces.append(swap(join(*pieces), "batch", bit))

    hidden = pe.shape[1]
    (hid_a,) = call(
        expand_kernel,
        [jax.ShapeDtypeStruct((part_pixels, hidden), bf16)],
        [VMEM] * 3,
        [pltpu.VMEM((part_pixels, chans), bf16)],
        6 * mib,
        2 * part_pixels * hidden * chans,
        2 * hidden * chans,
    )(z[0], z_other[0], pe)
    (hot,) = call(
        functools.partial(prep_kernel, (order, shard_rows, width, out_pixels, parts)),
        [jax.ShapeDtypeStruct((9 * REG, out_pixels), bf16)],
        [SMEM] + [VMEM] * shards,
        [pltpu.VMEM((16, (shards + 2) * pixels), f32)],
        2 * mib,
        10**8,
        10**6,
    )(after(spot, hid_a), *last)
    (pooled,) = call(
        project_kernel,
        [jax.ShapeDtypeStruct((REG, out_dim), f32)],
        [VMEM] * 6,
        [
            pltpu.VMEM((part_pixels, chans), bf16),
            pltpu.VMEM((hidden // 512, out_pixels, 512), bf16),
        ],
        8 * mib,
        2 * part_pixels * hidden * chans + 4 * 9 * REG * hidden * out_pixels,
        4 * hidden * chans,
    )(z[1], z_other[1], hid_a, pe, pk, hot)
    pick, facts = call(
        functools.partial(owner_kernel, (order, shard_rows, pixels, images, batches, per_key)),
        [jax.ShapeDtypeStruct((owned, slots), bf16), jax.ShapeDtypeStruct((owned, LANES), f32)],
        [SMEM] + [VMEM] * (shards + 2),
        [],
        2 * mib,
        10**8,
        10**6,
    )(after(spot, pooled), *last, owner_slot, partner)
    total, send = call(
        add_kernel,
        [jax.ShapeDtypeStruct((REG, out_dim), f32), jax.ShapeDtypeStruct((REG, out_dim), bf16)],
        [VMEM] * 2,
        [],
        mib,
        10**5,
        10**5,
    )(pooled, swap(pooled, "section", 1))
    sums = [swap(send, "rows", k) if k else total for k in range(shards)]
    pieces[-1] = after(pieces[-1], pooled)
    pieces.append(swap(join(*pieces), "section", 1))
    count = sum(x.shape[0] for x in pieces)
    keys, length = call(
        keys_kernel,
        [jax.ShapeDtypeStruct((depth, count), bf16), jax.ShapeDtypeStruct((1, count), f32)],
        [VMEM] * len(pieces),
        [],
        4 * mib,
        10**9,
        10**6,
    )(*pieces)

    embed, loss = call(
        functools.partial(loss_kernel, (shards, parts)),
        [jax.ShapeDtypeStruct((owned, out_dim), f32), jax.ShapeDtypeStruct((1, owned), f32)],
        [SMEM] + [VMEM] * (len(sums) + 4),
        [pltpu.VMEM((slots, out_dim), f32)],
        6 * mib,
        10**8,
        10**6,
    )(spot, *sums, pick, facts, keys, length)
    return embed, loss.reshape(owned)


def solution(mesh):
    in_specs = (
        P("batch", "rows", None, None),
        P(),
        P(),
        P(None, "section"),
        P("section", None),
        P(),
        P(None, "section"),
        P(None, "section", None),
        P("batch", "rows", None),
        P("batch", None),
        P("batch", None),
        P(("batch", "rows"), None),
    )
    out_specs = (P(("batch", "rows"), None), P(("batch", "rows")))
    return jax.shard_map(body, mesh=mesh, in_specs=in_specs, out_specs=out_specs, check_vma=False)
```
